1024 devices in a mesh: row: 16 (over x, y_lo), blk: 64 (over z, y_hi, core).
Axes of the slice: x: 4, y: 8 (y_hi: 2, y_lo: 4; y = y_hi * 4 + y_lo), z: 16, core: 2. Of those that a mesh axis runs over, the one named last changes fastest.
Arguments:
- state: float32 [16, 5, 16, 512, 128], P('row', None, None, 'blk'), may hold values from -6 to 6
- viscosity: float32 [16, 16, 512, 128], P('row', None, 'blk'), may hold values from 0.02 to 0.2
- coupling: float32 [16, 5, 5], P('row'), may hold values from -1.5 to 1.5
- offsets: int32 [4, 8], replicated, may hold values from 0 to 511
- live_span: int32 [16], P('row'), may hold values from 64 to 128, as said below
Outputs:
- updated: float32 [16, 5, 16, 512, 128], P('row', None, None, 'blk')
The draws below stay inside these ranges and needn't reach their ends.
Inputs may be any that keep to these rules, and one draw needn't show every extreme that they name: `live_span`: every row has at least half of its 128 span cells fluid, and in every draw some row has all 128.
All inputs are finite; a program needn't handle non-finite values.
Results may differ from the reference program's by a relative error of at most 0.0001.
Values sent between devices are 32-bit elements; how exact they have to be, the bound alone decides.
A program may use at most 32 MiB of HBM per device.

```python
import math
import jax
import jax.numpy as jnp
from jax import lax

A = 16
P_SIZE = 8
S = 128
NVAR = 5
MODES = 5
SECTIONS = 4
NROW = 16
HALF = 8
NP = 512


def draw_live_span(key, part):
    values = jax.random.randint(key, (NROW,), S // 2, S + 1)
    chosen = jax.random.randint(jax.random.fold_in(key, 7), (), 0, NROW)
    return values.at[chosen].set(S).astype(jnp.int32)


def draw_offsets(key, part):
    values = jax.random.randint(key, (SECTIONS, HALF), 0, NP)
    chosen = jax.random.randint(jax.random.fold_in(key, 11), (SECTIONS,), 0, HALF)
    extra = jax.random.randint(jax.random.fold_in(key, 13), (SECTIONS,), 0, P_SIZE)
    values = values.at[0, (chosen[0] + 1) % HALF].set(NP - 1)
    values = values.at[1, (chosen[1] + 1) % HALF].set(0)
    section_ids = jnp.arange(SECTIONS)
    values = values.at[section_ids, chosen].set(NP // 2 + extra)
    return values.astype(jnp.int32)


def shard_levels(stream_key, shape, pieces, low, largest):
    def one(dim, blocks):
        steps = jax.random.uniform(jax.random.fold_in(jax.random.fold_in(stream_key, 6), dim), (blocks,), jnp.float32, low / len(pieces), largest / len(pieces))
        return jnp.repeat(jnp.exp(steps), shape[dim] // blocks).reshape((-1,) + (1,) * (len(shape) - dim - 1))

    factor_of = one(*pieces[0])
    for cut in pieces[1:]:
        factor_of = factor_of * one(*cut)
    return factor_of


def scatter_about(stream_key, shape, spread, most, shards=(), kind=jnp.bfloat16):
    values = jax.random.normal(stream_key, shape, jnp.float32) * spread
    if len(shards) > 0:
        values = shard_levels(stream_key, shape, shards, -0.22, 0.18) * values
    return jnp.clip(values, min=-most, max=most).astype(kind)


def setup_inputs(seed: int = 0) -> dict:
    streams_of = jax.random.split(jax.random.key(seed), 6)
    return {
        "state": scatter_about(streams_of[0], (NROW, NVAR, A, NP, S), 1.0, 6.0, ((0, 16), (3, 64)), jnp.float32),
        "viscosity": jnp.clip(jnp.exp(math.log(0.2) - 2.3025851 * jax.random.uniform(streams_of[1], (NROW, A, NP, S), jnp.float32) ** shard_levels(streams_of[1], (NROW, A, NP, S), ((0, 16), (2, 64)), -0.2, 0.2)), 0.02, 0.2),
        "coupling": scatter_about(streams_of[2], (NROW, NVAR, NVAR), 0.3, 1.5, ((0, 16),), jnp.float32),
        "offsets": draw_offsets(jax.random.fold_in(streams_of[5], 71), 0),
        "live_span": draw_live_span(jax.random.fold_in(streams_of[5], 71), 0),
    }


section_alphas = (0.25, 1.0 / 3.0, 0.5, 1.0)
time_step = 0.25
speed_axial = 1.0
speed_pitch = 0.6
speed_span = 0.3


def basis_table(position, count, harmonics):
    rows = [jnp.ones_like(position)]
    for order in range(1, harmonics + 1):
        rows.append(jnp.cos(order * position))
    for order in range(1, harmonics + 1):
        rows.append(jnp.sin(order * position))
    return jnp.stack(rows)


def mode_weights(count, harmonics):
    return jnp.array([1.0 / count] + [2.0 / count] * (2 * harmonics), jnp.float32)


def rates(field, ghost, viscosity, coupling, mask):
    up_axial = jnp.concatenate([field[:, :, 1:], ghost[:, :, None]], 2)
    down_axial = jnp.concatenate([field[:, :, :1], field[:, :, :-1]], 2)
    up_pitch = jnp.roll(field, -1, 3)
    down_pitch = jnp.roll(field, 1, 3)
    up_span = jnp.concatenate([field[..., 1:], field[..., -1:]], 4)
    down_span = jnp.concatenate([field[..., :1], field[..., :-1]], 4)
    advect = speed_axial * (up_axial - field) - speed_pitch * (field - down_pitch) - speed_span * (field - down_span)
    beside_all = up_axial + down_axial + up_pitch + down_pitch + up_span + down_span - 6.0 * field
    source = jnp.einsum("rvw,rwaps->rvaps", coupling, field, precision=lax.Precision.HIGHEST)
    return (advect + viscosity[:, None] * beside_all + source) * mask


def reference(state, viscosity, coupling, offsets, live_span):
    position = jnp.arange(NP).astype(jnp.float32) * jnp.float32(2.0 * math.pi / NP)
    basis = basis_table(position, NP, MODES)
    weights = mode_weights(NP, MODES)
    mask = (jnp.arange(S)[None, :] < live_span[:, None]).astype(jnp.float32)[:, None, None, None, :]
    field = state
    for section in range(SECTIONS):
        turn = offsets[section]
        shifts = jnp.stack([turn, (NP - turn) % NP], 1).reshape(-1).astype(jnp.int32)
        strips = field[:, :, A - 1]
        partner = strips.reshape(HALF, 2, NVAR, NP, S)[:, ::-1].reshape(NROW, NVAR, NP, S)
        index = (jnp.arange(NP)[None, :].astype(jnp.int32) + shifts[:, None]) % NP
        window = jax.vmap(lambda strip, where: jnp.take(strip, where, axis=1))(partner, index)
        coef = jnp.einsum("mi,rvis->rmvs", basis, window, precision=lax.Precision.HIGHEST) * weights[None, :, None, None]
        recon = jnp.einsum("mi,rmvs->rvis", basis, coef, precision=lax.Precision.HIGHEST)
        ghost = 0.5 * (window + recon)
        field = state + section_alphas[section] * time_step * rates(field, ghost, viscosity, coupling, mask)
    return field
```

```python
import functools
import math

import jax
import jax.numpy as jnp
import numpy as np
from jax import lax
from jax.experimental import pallas as pl
from jax.experimental.pallas import tpu as pltpu
from jax.sharding import PartitionSpec as P

MESH = pl.DeviceIdType.MESH
MODES = 5
SECTIONS = 4
NVAR = 5
AXIAL = 16
PITCH = 8
SPAN = 128
BLOCKS = 64
NP = BLOCKS * PITCH
SLICES = 16
CHUNK = 64
PAD = 8

section_alphas = (0.25, 1.0 / 3.0, 0.5, 1.0)
time_step = 0.25
speed_axial = 1.0
speed_pitch = 0.6
speed_span = 0.3
HIGHEST = lax.Precision.HIGHEST


def basis_tables():
    theta = np.arange(NP) * (2.0 * math.pi / NP)
    rows = [np.ones(NP)]
    rows += [np.cos(j * theta) for j in range(1, MODES + 1)]
    rows += [np.sin(j * theta) for j in range(1, MODES + 1)]
    table = np.zeros((16, NP))
    table[: 2 * MODES + 1] = np.stack(rows)
    weights = np.full((16, 1), 2.0 / NP)
    weights[0] = 1.0 / NP
    return (table * weights).astype(np.float32), table.T.astype(np.float32).copy()


def worker_of(pair, s):
    return 2 * pair + (s // 2) % 2, 4 * s + 2 * (s % 2)


def kernel(
    state, visc, coup, offs, live, basis, basis_t, out,
    msg, recv, cst, hs, hr, vb, xa, xb, xc, hb, st, gbuf, fld, vext, gx,
    main_s, main_r, cst_s, cst_r, halo_s, halo_r, ret_s, ret_r,
):
    row = lax.axis_index("row")
    blk = lax.axis_index("blk")
    pair, parity = row // 2, row % 2
    z = blk // 4
    own_row, own_blk = worker_of(pair, z)
    is_worker = jnp.logical_and(own_row == row, own_blk == blk)
    after, before = (blk + 1) % BLOCKS, (blk + BLOCKS - 1) % BLOCKS

    bar = pltpu.get_barrier_semaphore()

    def greet(r, b):
        pl.semaphore_signal(bar, inc=1, device_id=(r, b), device_id_type=MESH)

    @pl.when(is_worker)
    def _():
        def greet_source(i, c):
            at = (blk + BLOCKS // 2 + i) % BLOCKS
            greet(row ^ 1, at)

            @pl.when(at != blk)
            def _():
                greet(row, at)

            return c

        lax.fori_loop(0, BLOCKS, greet_source, 0)

    for i in range(SLICES):
        s = (z + SLICES // 2 + i) % SLICES
        wr, wb = worker_of(pair, s)

        @pl.when(jnp.logical_not(jnp.logical_and(wr == row, wb == blk)))
        def _():
            greet(wr, wb)

    greet(row, after)
    greet(row, before)
    greet(row ^ 1, blk)

    lane8 = lax.broadcasted_iota(jnp.int32, (8, 128), 1)
    slot8 = lane8 // 16
    top = AXIAL - 1
    tiles = (
        [(v, top) for v in range(NVAR)] + [(-1, top), (-1, top - 1), (-1, top - 2)],
        [(v, top - 1) for v in range(NVAR)] + [(0, top - 3), (1, top - 3), (2, top - 3)],
        [(v, top - 2) for v in range(NVAR)] + [(3, top - 3), (4, top - 3)],
    )
    for t, slots in enumerate(tiles):
        values = [visc[a] if v < 0 else state[v, a] for v, a in slots]
        for s in range(SLICES):
            packed = jnp.zeros((8, 128), jnp.float32)
            for q, value in enumerate(values):
                turn = (16 * q - (8 * s - 4)) % 128
                moved = pltpu.roll(value, turn, 1) if turn else value
                packed = jnp.where(slot8 == q, moved, packed)
            msg[s, t] = packed

    sub8 = lax.broadcasted_iota(jnp.int32, (8, 128), 0)
    table = jnp.zeros((8, 128), jnp.float32)
    for v in range(NVAR):
        for w in range(NVAR):
            here = jnp.logical_and(slot8 == v, sub8 == (w - v) % 8)
            table = jnp.where(here, coup[v, w], table)
    cst[parity, 0:8] = table
    cst[parity, 8:16] = jnp.full((8, 128), live[0].astype(jnp.float32))

    def pack_halo(j, c):
        for v in range(NVAR + 1):
            for h in range(2):
                if v < NVAR:
                    low = state[v, 2 * j + h, 0:4]
                    high = state[v, 2 * j + h, 4:8]
                else:
                    low = visc[2 * j + h, 0:4]
                    high = visc[2 * j + h, 4:8]
                hs[0, v, j, 4 * h : 4 * h + 4] = high
                hs[1, v, j, 4 * h : 4 * h + 4] = low
        return c

    lax.fori_loop(0, AXIAL // 2, pack_halo, 0)

    pl.semaphore_wait(bar, SLICES + 3 + jnp.where(is_worker, 2 * BLOCKS - 2, 0))

    mine = pl.ds(pl.multiple_of(PAD + PITCH * blk, 8), PITCH)

    def send_main(i, c):
        s = (z + SLICES // 2 + jnp.where(i % 2 == 1, (i + 1) // 2, SLICES - i // 2)) % SLICES
        wr, wb = worker_of(pair, s)
        self = jnp.logical_and(wr == row, wb == blk)

        @pl.when(jnp.logical_not(self))
        def _():
            pltpu.make_async_remote_copy(
                src_ref=msg.at[s],
                dst_ref=recv.at[parity, :, mine],
                send_sem=main_s,
                recv_sem=main_r,
                device_id=(wr, wb),
                device_id_type=MESH,
            ).start()

        return c

    lax.fori_loop(0, SLICES, send_main, 0)

    def const_copy():
        return pltpu.make_async_remote_copy(
            src_ref=cst.at[parity],
            dst_ref=cst.at[parity],
            send_sem=cst_s,
            recv_sem=cst_r,
            device_id=(row ^ 1, blk),
            device_id_type=MESH,
        )

    const_copy().start()

    def wait_bytes(ref, sem):
        pltpu.make_async_copy(ref, ref, sem).wait()

    @pl.when(is_worker)
    def _():
        wait_bytes(msg.at[pl.ds(0, SLICES - 1)], main_s)

    @pl.when(jnp.logical_not(is_worker))
    def _():
        wait_bytes(msg, main_s)

    def halo_copy(side):
        return pltpu.make_async_remote_copy(
            src_ref=hs.at[side],
            dst_ref=hr.at[side],
            send_sem=halo_s.at[side],
            recv_sem=halo_r.at[side],
            device_id=(row, after if side == 0 else before),
            device_id_type=MESH,
        )

    halo_copy(0).start()
    halo_copy(1).start()
    const_copy().wait_send()
    wait_bytes(cst.at[1 - parity], cst_r)

    @pl.when(is_worker)
    def _():
        recv[parity, :, mine] = msg[z]
        wait_bytes(st.at[pl.ds(0, 2 * BLOCKS - 1)], main_r)
        lane = lax.broadcasted_iota(jnp.int32, (CHUNK, 128), 1)
        slot = lane // 16
        cell = 8 * z - 4 + lane % 16
        first, last = cell == 0, cell == SPAN - 1
        cell_f = cell[0:1].astype(jnp.float32)

        def wrap(ref, *index):
            ref[(*index, slice(PAD - 1, PAD))] = ref[(*index, slice(PAD + NP - 1, PAD + NP))]
            ref[(*index, slice(PAD + NP, PAD + NP + 1))] = ref[(*index, slice(PAD, PAD + 1))]

        shifts = []
        for k in range(SECTIONS):
            turn = offs[k, pair]
            shifts.append((turn, (NP - turn) % NP))

        def widen(value, q):
            value = jnp.where(slot == q, value, 0.0)
            for step in (16, 32, 64):
                value = value + pltpu.roll(value, step, 1)
            return value

        for rho in range(2):
            for t in range(3):
                wrap(recv, rho, t)

            def spread(i, c):
                at = pl.multiple_of(i * CHUNK, CHUNK)
                packed = recv[rho, 0, pl.ds(PAD + at, CHUNK)]
                for q in range(3):
                    vb[rho, q, pl.ds(at, CHUNK)] = widen(packed, 5 + q)
                return c

            lax.fori_loop(0, NP // CHUNK, spread, 0)

        fields = [
            [[(recv, (rho, t)) for t in range(3)] for rho in range(2)],
            [[(xa, (rho, t)) for t in range(3)] for rho in range(2)],
            [[(xb, (rho, t)) for t in range(2)] for rho in range(2)],
            [[(xc, (rho,))] for rho in range(2)],
        ]
        for k in range(SECTIONS):
            for rho in range(2):
                ref, index = fields[k][rho][0]
                strip = ref[(*index, slice(PAD, PAD + NP))]
                coef = jnp.dot(basis[...], strip, precision=HIGHEST, preferred_element_type=jnp.float32)
                recon = jnp.dot(basis_t[...], coef, precision=HIGHEST, preferred_element_type=jnp.float32)
                half = 0.5 * (strip + recon)
                hb[k, rho, 0:NP] = half
                hb[k, rho, NP : NP + CHUNK] = half[0:CHUNK]
            if k == SECTIONS - 1:
                break
            factor = section_alphas[k] * time_step
            for rho in range(2):
                table = cst[rho]
                scale = jnp.where(cell_f < table[8:9], factor, 0.0)

                def update(i, c):
                    at = pl.multiple_of(i * CHUNK, CHUNK)

                    def take(t, move=0):
                        ref, index = fields[k][rho][t]
                        return ref[(*index, pl.ds(PAD + at + move, CHUNK))]

                    inner = [take(t) for t in range(3 - k)]
                    start = (at + shifts[k][rho]) % NP
                    ghost = hb[k, 1 - rho, pl.ds(start, CHUNK)]
                    for t in range(3 - k):
                        here = inner[t]
                        up_axial = ghost if t == 0 else inner[t - 1]
                        if t + 1 < 3 - k:
                            down_axial = inner[t + 1]
                        elif k == 0:
                            two = recv[rho, 1, pl.ds(PAD + at, CHUNK)]
                            three = recv[rho, 2, pl.ds(PAD + at, CHUNK)]
                            down_axial = jnp.where(
                                slot < 3, pltpu.roll(two, 48, 1), pltpu.roll(three, 96, 1)
                            )
                        else:
                            down_axial = take(t + 1)
                        up_pitch, down_pitch = take(t, 1), take(t, -1)
                        up_span = jnp.where(last, here, pltpu.roll(here, 127, 1))
                        down_span = jnp.where(first, here, pltpu.roll(here, 1, 1))
                        rate = (
                            speed_axial * (up_axial - here)
                            - speed_pitch * (here - down_pitch)
                            - speed_span * (here - down_span)
                        )
                        beside = up_axial + down_axial + up_pitch + down_pitch + up_span + down_span
                        rate = rate + vb[rho, t, pl.ds(at, CHUNK)] * (beside - 6.0 * here)
                        rate = rate + table[0:1] * here
                        for d in range(1, 8):
                            rate = rate + table[d : d + 1] * pltpu.roll(here, 128 - 16 * d, 1)
                        ref, index = fields[k + 1][rho][t] if t < 3 - k else None
                        ref[(*index, pl.ds(PAD + at, CHUNK))] = (
                            recv[rho, t, pl.ds(PAD + at, CHUNK)] + scale * rate
                        )
                    return c

                lax.fori_loop(0, NP // CHUNK, update, 0)
                for t in range(3 - k):
                    ref, index = fields[k + 1][rho][t]
                    wrap(ref, *index)

        lane16 = lax.broadcasted_iota(jnp.int32, (16, 128), 1)
        inside = jnp.logical_and(lane16 % 16 >= 4, lane16 % 16 < 12)

        def send_back(i, c):
            at = (blk + BLOCKS // 2 + jnp.where(i % 2 == 1, (i + 1) // 2, BLOCKS - i // 2)) % BLOCKS
            for rho in range(2):
                part = []
                for k in range(SECTIONS):
                    back = 4 if k < 3 else 0
                    start = (PITCH * at + NP - back + shifts[k][rho]) % NP
                    part.append(hb[k, 1 - rho, pl.ds(start, 16 if k < 3 else 8)])
                both = jnp.where(inside, part[0], pltpu.roll(part[1], 8, 1))
                third = jnp.where(inside, pltpu.roll(part[2], 80, 1), pltpu.roll(part[2], 40, 1))
                both = jnp.where(lane16 < 84, both, third)
                to = rho * BLOCKS + at
                st[to, 0] = both[0:8]
                st[to, 1] = both[8:16]
                st[to, 2] = part[3]
                other = rho * 1 + pair * 2
                self = jnp.logical_and(other == row, at == blk)

                @pl.when(jnp.logical_not(self))
                def _():
                    pltpu.make_async_remote_copy(
                        src_ref=st.at[to],
                        dst_ref=gbuf.at[z],
                        send_sem=ret_s,
                        recv_sem=ret_r,
                        device_id=(other, at),
                        device_id_type=MESH,
                    ).start()

            return c

        lax.fori_loop(0, BLOCKS, send_back, 0)
        gbuf[z] = st[parity * BLOCKS + blk]

    halo_copy(0).wait_recv()
    halo_copy(1).wait_recv()

    def widen_block(j, c):
        for h in range(2):
            a = 2 * j + h
            part = slice(4 * h, 4 * h + 4)
            for v in range(NVAR):
                fld[0, v, a, 0:4] = hr[0, v, j, part]
                fld[0, v, a, 4:12] = state[v, a]
                fld[0, v, a, 12:16] = hr[1, v, j, part]
            vext[a, 0:4] = hr[0, NVAR, j, part]
            vext[a, 4:12] = visc[a]
            vext[a, 12:16] = hr[1, NVAR, j, part]
        return c

    lax.fori_loop(0, AXIAL // 2, widen_block, 0)

    lane2 = lax.broadcasted_iota(jnp.int32, (16, 128), 1)
    first2, last2 = lane2 == 0, lane2 == SPAN - 1
    alive = lane2 < live[0]
    cs = [[coup[v, w] for w in range(NVAR)] for v in range(NVAR)]

    def layer(k, a, up):
        here = [fld[k, v, a] for v in range(NVAR)]
        vis = vext[a]
        below = jnp.maximum(a - 1, 0)
        scale = jnp.where(alive, section_alphas[k] * time_step, 0.0)
        for v in range(NVAR):
            u = here[v]
            up_axial, down_axial = up(v), fld[k, v, below]
            up_pitch, down_pitch = pltpu.roll(u, 15, 0), pltpu.roll(u, 1, 0)
            up_span = jnp.where(last2, u, pltpu.roll(u, 127, 1))
            down_span = jnp.where(first2, u, pltpu.roll(u, 1, 1))
            rate = (
                speed_axial * (up_axial - u)
                - speed_pitch * (u - down_pitch)
                - speed_span * (u - down_span)
            )
            beside = up_axial + down_axial + up_pitch + down_pitch + up_span + down_span
            rate = rate + vis * (beside - 6.0 * u)
            for w in range(NVAR):
                rate = rate + cs[v][w] * here[w]
            new = fld[0, v, a] + scale * rate
            if k < SECTIONS - 1:
                fld[k + 1, v, a] = new
            else:
                out[v, a] = pltpu.roll(new, 12, 0)[0:8]

    for k in range(SECTIONS):

        def inner_layer(a, c):
            layer(k, a, lambda v: fld[k, v, a + 1])
            return c

        lax.fori_loop(0, AXIAL - 1 - k, inner_layer, 0)

    @pl.when(is_worker)
    def _():
        wait_bytes(gbuf.at[pl.ds(0, SLICES - 1)], ret_r)

    @pl.when(jnp.logical_not(is_worker))
    def _():
        wait_bytes(gbuf, ret_r)

    group8 = lane8 // 8
    for v in range(NVAR):
        places = [16 * v + 4, 16 * v + 12]
        places.append(84 + 16 * v if v < 3 else 92 + 16 * (v - 3))
        for k in range(3):
            for half in range(2):
                value = jnp.zeros((8, 128), jnp.float32)
                for s in range(SLICES):
                    turn = (8 * s - places[k]) % 128
                    value = jnp.where(group8 == s, pltpu.roll(gbuf[s, half], turn, 1), value)
                gx[k, v, 8 * half : 8 * half + 8] = value
        value = jnp.zeros((8, 128), jnp.float32)
        for s in range(SLICES):
            turn = (8 * s - (16 * v + 4)) % 128
            value = jnp.where(group8 == s, pltpu.roll(gbuf[s, 2], turn, 1), value)
        gx[3, v, 0:4] = jnp.zeros((4, 128), jnp.float32)
        gx[3, v, 4:12] = value
        gx[3, v, 12:16] = jnp.zeros((4, 128), jnp.float32)

    for k in range(SECTIONS):
        for a in range(AXIAL - 1 - k, AXIAL - 1):
            layer(k, a, lambda v: fld[k, v, a + 1])
        layer(k, AXIAL - 1, lambda v: gx[k, v])

    halo_copy(0).wait_send()
    halo_copy(1).wait_send()

    @pl.when(is_worker)
    def _():
        wait_bytes(st.at[pl.ds(0, 2 * BLOCKS - 1)], ret_s)


def solution(mesh):
    weighted, plain = basis_tables()

    def body(state, visc, coup, offs, live):
        vmem = pl.BlockSpec(memory_space=pltpu.VMEM)
        smem = pl.BlockSpec(memory_space=pltpu.SMEM)
        f32 = jnp.float32
        done = pl.pallas_call(
            kernel,
            out_shape=jax.ShapeDtypeStruct((NVAR, AXIAL, PITCH, SPAN), f32),
            in_specs=[vmem, vmem, smem, smem, smem, vmem, vmem],
            out_specs=vmem,
            scratch_shapes=[
                pltpu.VMEM((SLICES, 3, 8, 128), f32),
                pltpu.VMEM((2, 3, NP + 2 * PAD, 128), f32),
                pltpu.VMEM((2, 16, 128), f32),
                pltpu.VMEM((2, NVAR + 1, AXIAL // 2, 8, 128), f32),
                pltpu.VMEM((2, NVAR + 1, AXIAL // 2, 8, 128), f32),
                pltpu.VMEM((2, 3, NP, 128), f32),
                pltpu.VMEM((2, 3, NP + 2 * PAD, 128), f32),
                pltpu.VMEM((2, 2, NP + 2 * PAD, 128), f32),
                pltpu.VMEM((2, NP + 2 * PAD, 128), f32),
                pltpu.VMEM((SECTIONS, 2, NP + CHUNK, 128), f32),
                pltpu.VMEM((2 * BLOCKS, 3, 8, 128), f32),
                pltpu.VMEM((SLICES, 3, 8, 128), f32),
                pltpu.VMEM((SECTIONS, NVAR, AXIAL, 16, 128), f32),
                pltpu.VMEM((AXIAL, 16, 128), f32),
                pltpu.VMEM((SECTIONS, NVAR, 16, 128), f32),
                pltpu.SemaphoreType.DMA,
                pltpu.SemaphoreType.DMA,
                pltpu.SemaphoreType.DMA,
                pltpu.SemaphoreType.DMA,
                pltpu.SemaphoreType.DMA((2,)),
                pltpu.SemaphoreType.DMA((2,)),
                pltpu.SemaphoreType.DMA,
                pltpu.SemaphoreType.DMA,
            ],
            compiler_params=pltpu.CompilerParams(
                collective_id=0, has_side_effects=True, vmem_limit_bytes=48 << 20
            ),
            name="sections",
        )(state[0], visc[0], coup[0], offs, live, jnp.asarray(weighted), jnp.asarray(plain))
        return done[None]

    in_specs = (
        P("row", None, None, "blk", None),
        P("row", None, "blk", None),
        P("row", None, None),
        P(),
        P("row"),
    )
    out_specs = P("row", None, None, "blk", None)
    return jax.shard_map(body, mesh=mesh, in_specs=in_specs, out_specs=out_specs, check_vma=False)
```

```python
import functools
import math

import jax
import jax.numpy as jnp
import numpy as np
from jax import lax
from jax.experimental import pallas as pl
from jax.experimental.pallas import tpu as pltpu
from jax.sharding import PartitionSpec as P

MESH = pl.DeviceIdType.MESH
MODES = 5
SECTIONS = 4
NVAR = 5
AXIAL = 16
PITCH = 8
SPAN = 128
BLOCKS = 64
NP = BLOCKS * PITCH
SLICES = 16
CHUNK = 128
WRAP = 128
PAD = 8

section_alphas = (0.25, 1.0 / 3.0, 0.5, 1.0)
time_step = 0.25
speed_axial = 1.0
speed_pitch = 0.6
speed_span = 0.3

def split(value):
    high = value.astype(jnp.bfloat16)
    return high, (value - high.astype(jnp.float32)).astype(jnp.bfloat16)


def basis_tables():
    theta = np.arange(NP) * (2.0 * math.pi / NP)
    rows = [np.ones(NP)]
    rows += [np.cos(j * theta) for j in range(1, MODES + 1)]
    rows += [np.sin(j * theta) for j in range(1, MODES + 1)]
    table = np.zeros((16, NP), np.float32)
    table[: 2 * MODES + 1] = np.stack(rows)
    weights = np.full((16, 1), 2.0 / NP, np.float32)
    weights[0] = 1.0 / NP

    def parts(value):
        high = value.astype(jnp.bfloat16)
        return high, (value - high.astype(np.float32)).astype(jnp.bfloat16)

    back = np.zeros((NP, 128), jnp.bfloat16)
    high, low = parts(np.ascontiguousarray(table.T))
    back[:, 0:16], back[:, 16:32], back[:, 32:48] = high, low, high
    return np.concatenate(parts(table * weights)), back


def worker_of(pair, s):
    return 2 * pair + (s // 2) % 2, 4 * s + 2 * (s % 2)


def kernel(
    state_hbm, visc_hbm, coup, offs, live, basis_hbm, basis_t_hbm, out,
    state, visc, basis, basis_t, mix, load_s,
    msg, recv, cst, hs, hr, vb, xa, xb, xc, hb, st, gbuf, fld, vext, gx,
    main_s, main_r, cst_s, cst_r, halo_s, halo_r, ret_s, ret_r,
):
    loads = [
        pltpu.make_async_copy(source, target, load_s.at[i])
        for i, (source, target) in enumerate(
            [(state_hbm, state), (visc_hbm, visc), (basis_hbm, basis), (basis_t_hbm, basis_t)]
        )
    ]
    for load in loads:
        load.start()
    row = lax.axis_index("row")
    blk = lax.axis_index("blk")
    pair, parity = row // 2, row % 2
    z = blk // 4
    own_row, own_blk = worker_of(pair, z)
    is_worker = jnp.logical_and(own_row == row, own_blk == blk)
    after, before = (blk + 1) % BLOCKS, (blk + BLOCKS - 1) % BLOCKS

    bar = pltpu.get_barrier_semaphore()

    def greet(r, b):
        pl.semaphore_signal(bar, inc=1, device_id=(r, b), device_id_type=MESH)

    @pl.when(is_worker)
    def _():
        def greet_source(i, c):
            at = (blk + BLOCKS // 2 + i) % BLOCKS
            greet(row ^ 1, at)

            @pl.when(at != blk)
            def _():
                greet(row, at)

            return c

        lax.fori_loop(0, BLOCKS, greet_source, 0)

    for i in range(SLICES):
        s = (z + SLICES // 2 + i) % SLICES
        wr, wb = worker_of(pair, s)

        @pl.when(jnp.logical_not(jnp.logical_and(wr == row, wb == blk)))
        def _():
            greet(wr, wb)

    greet(row, after)
    greet(row, before)
    greet(row ^ 1, blk)

    for load in loads:
        load.wait()

    lane8 = lax.broadcasted_iota(jnp.int32, (8, 128), 1)
    slot8 = lane8 // 16
    top = AXIAL - 1
    tiles = (
        [(v, top) for v in range(NVAR)] + [(-1, top), (-1, top - 1), (-1, top - 2)],
        [(v, top - 1) for v in range(NVAR)] + [(0, top - 3), (1, top - 3), (2, top - 3)],
        [(v, top - 2) for v in range(NVAR)] + [(3, top - 3), (4, top - 3)],
    )
    for t, slots in enumerate(tiles):
        values = [visc[a] if v < 0 else state[v, a] for v, a in slots]
        for s in range(SLICES):
            packed = jnp.zeros((8, 128), jnp.float32)
            for q, value in enumerate(values):
                turn = (16 * q - (8 * s - 4)) % 128
                moved = pltpu.roll(value, turn, 1) if turn else value
                packed = jnp.where(slot8 == q, moved, packed)
            msg[s, t] = packed

    sub8 = lax.broadcasted_iota(jnp.int32, (8, 128), 0)
    table = jnp.zeros((8, 128), jnp.float32)
    for v in range(NVAR):
        for w in range(NVAR):
            here = jnp.logical_and(slot8 == v, sub8 == (w - v) % 8)
            table = jnp.where(here, coup[v, 0, w], table)
    cst[parity, 0:8] = table
    cst[parity, 8:16] = jnp.full((8, 128), live[0].astype(jnp.float32))

    def pack_halo(j, c):
        for v in range(NVAR + 1):
            for h in range(2):
                if v < NVAR:
                    low = state[v, 2 * j + h, 0:4]
                    high = state[v, 2 * j + h, 4:8]
                else:
                    low = visc[2 * j + h, 0:4]
                    high = visc[2 * j + h, 4:8]
                hs[0, v, j, 4 * h : 4 * h + 4] = high
                hs[1, v, j, 4 * h : 4 * h + 4] = low
        return c

    lax.fori_loop(0, AXIAL // 2, pack_halo, 0)

    pl.semaphore_wait(bar, SLICES + 3 + jnp.where(is_worker, 2 * BLOCKS - 2, 0))

    mine = pl.ds(pl.multiple_of(PAD + PITCH * blk, 8), PITCH)

    def send_main(i, c):
        s = (z + SLICES // 2 + jnp.where(i % 2 == 1, (i + 1) // 2, SLICES - i // 2)) % SLICES
        wr, wb = worker_of(pair, s)
        self = jnp.logical_and(wr == row, wb == blk)

        @pl.when(jnp.logical_not(self))
        def _():
            pltpu.make_async_remote_copy(
                src_ref=msg.at[s],
                dst_ref=recv.at[parity, :, mine],
                send_sem=main_s,
                recv_sem=main_r,
                device_id=(wr, wb),
                device_id_type=MESH,
            ).start()

        return c

    lax.fori_loop(0, SLICES, send_main, 0)

    def const_copy():
        return pltpu.make_async_remote_copy(
            src_ref=cst.at[parity],
            dst_ref=cst.at[parity],
            send_sem=cst_s,
            recv_sem=cst_r,
            device_id=(row ^ 1, blk),
            device_id_type=MESH,
        )

    const_copy().start()

    def wait_bytes(ref, sem):
        pltpu.make_async_copy(ref, ref, sem).wait()

    @pl.when(is_worker)
    def _():
        wait_bytes(msg.at[pl.ds(0, SLICES - 1)], main_s)

    @pl.when(jnp.logical_not(is_worker))
    def _():
        wait_bytes(msg, main_s)

    def halo_copy(side):
        return pltpu.make_async_remote_copy(
            src_ref=hs.at[side],
            dst_ref=hr.at[side],
            send_sem=halo_s.at[side],
            recv_sem=halo_r.at[side],
            device_id=(row, after if side == 0 else before),
            device_id_type=MESH,
        )

    halo_copy(0).start()
    halo_copy(1).start()
    const_copy().wait_send()
    wait_bytes(cst.at[1 - parity], cst_r)

    @pl.when(is_worker)
    def _():
        recv[parity, :, mine] = msg[z]
        source = lax.broadcasted_iota(jnp.int32, (128, 128), 0)
        target = lax.broadcasted_iota(jnp.int32, (128, 128), 1)
        place = 8 * z - 4 + target % 16
        lower = jnp.where(place == 0, target, target - 1)
        upper = jnp.where(place == SPAN - 1, target, target + 1)

        def one(here):
            return jnp.where(here, 1.0, 0.0)

        around = one(source == lower) + one(source == upper) - 6.0 * one(source == target)
        still = speed_span * one(source == lower) - (
            speed_axial + speed_pitch + speed_span
        ) * one(source == target)
        for rho in range(2):
            both = still
            for d in range(8):
                both = both + jnp.where(
                    source == (target + 16 * d) % 128, cst[rho, d : d + 1], 0.0
                )
            high, low = split(both)
            for half in range(2):
                mix[rho, 128 * half : 128 * half + 128, 0:128] = high
                mix[rho, 128 * half : 128 * half + 128, 128:256] = around.astype(jnp.bfloat16)
            mix[rho, 256:384, 0:128] = low
        wait_bytes(st.at[pl.ds(0, 2 * BLOCKS - 1)], main_r)
        lane = lax.broadcasted_iota(jnp.int32, (CHUNK, 128), 1)
        slot = lane // 16
        cell = 8 * z - 4 + lane % 16
        cell_f = cell[0:1].astype(jnp.float32)

        def wrap(ref, *index):
            ref[(*index, slice(PAD - 1, PAD))] = ref[(*index, slice(PAD + NP - 1, PAD + NP))]
            ref[(*index, slice(PAD + NP, PAD + NP + 1))] = ref[(*index, slice(PAD, PAD + 1))]

        shifts = []
        for k in range(SECTIONS):
            turn = offs[k, pair]
            shifts.append((turn, (NP - turn) % NP))

        def widen(value, q):
            value = jnp.where(slot == q, value, 0.0)
            for step in (16, 32, 64):
                value = value + pltpu.roll(value, step, 1)
            return value

        for rho in range(2):
            for t in range(3):
                wrap(recv, rho, t)

            def spread(i, c):
                at = pl.multiple_of(i * CHUNK, CHUNK)
                packed = recv[rho, 0, pl.ds(PAD + at, CHUNK)]
                for q in range(3):
                    vb[rho, q, pl.ds(at, CHUNK)] = widen(packed, 5 + q)
                return c

            lax.fori_loop(0, NP // CHUNK, spread, 0)

        fields = [
            [[(recv, (rho, t)) for t in range(3)] for rho in range(2)],
            [[(xa, (rho, t)) for t in range(3)] for rho in range(2)],
            [[(xb, (rho, t)) for t in range(2)] for rho in range(2)],
            [[(xc, (rho,))] for rho in range(2)],
        ]
        for k in range(SECTIONS):
            strips = []
            for rho in range(2):
                ref, index = fields[k][rho][0]
                strips.append(ref[(*index, slice(PAD, PAD + NP))])
            strips = jnp.concatenate(strips, 1)
            high, low = split(strips)
            sums = jnp.dot(basis[...], high, preferred_element_type=jnp.float32)
            coef = sums[0:16] + sums[16:32]
            coef = coef + jnp.dot(basis[0:16], low, preferred_element_type=jnp.float32)
            high, low = split(coef)
            coefs = jnp.concatenate([high, high, low, jnp.zeros((80, 256), jnp.bfloat16)], 0)
            recon = jnp.dot(basis_t[...], coefs, preferred_element_type=jnp.float32)
            half = 0.5 * (strips + recon)
            for rho in range(2):
                hb[k, rho, 0:NP] = half[:, 128 * rho : 128 * rho + 128]
                hb[k, rho, NP : NP + WRAP] = half[0:WRAP, 128 * rho : 128 * rho + 128]
            if k == SECTIONS - 1:
                break
            factor = section_alphas[k] * time_step
            for rho in range(2):
                table = cst[rho]
                scale = jnp.where(cell_f < table[8:9], factor, 0.0)

                def update(i, c):
                    at = pl.multiple_of(i * CHUNK, CHUNK)

                    def take(t, move=0):
                        ref, index = fields[k][rho][t]
                        return ref[(*index, pl.ds(PAD + at + move, CHUNK))]

                    inner = [take(t) for t in range(3 - k)]
                    start = (at + shifts[k][rho]) % NP
                    ghost = hb[k, 1 - rho, pl.ds(start, CHUNK)]
                    for t in range(3 - k):
                        here = inner[t]
                        up_axial = ghost if t == 0 else inner[t - 1]
                        if t + 1 < 3 - k:
                            down_axial = inner[t + 1]
                        elif k == 0:
                            two = recv[rho, 1, pl.ds(PAD + at, CHUNK)]
                            three = recv[rho, 2, pl.ds(PAD + at, CHUNK)]
                            down_axial = jnp.where(
                                slot < 3, pltpu.roll(two, 48, 1), pltpu.roll(three, 96, 1)
                            )
                        else:
                            down_axial = take(t + 1)
                        up_pitch, down_pitch = take(t, 1), take(t, -1)
                        high, low = split(here)
                        linear = jnp.dot(
                            jnp.concatenate([high, low], 1),
                            mix[rho, 0:256],
                            preferred_element_type=jnp.float32,
                        )
                        low = jnp.dot(high, mix[rho, 256:384, 0:128], preferred_element_type=jnp.float32)
                        beside = up_axial + down_axial + up_pitch + down_pitch + linear[:, 128:256]
                        rate = speed_axial * up_axial + speed_pitch * down_pitch + low
                        rate = rate + linear[:, 0:128] + vb[rho, t, pl.ds(at, CHUNK)] * beside
                        ref, index = fields[k + 1][rho][t]
                        ref[(*index, pl.ds(PAD + at, CHUNK))] = (
                            recv[rho, t, pl.ds(PAD + at, CHUNK)] + scale * rate
                        )
                    return c

                lax.fori_loop(0, NP // CHUNK, update, 0)
                for t in range(3 - k):
                    ref, index = fields[k + 1][rho][t]
                    wrap(ref, *index)

        lane16 = lax.broadcasted_iota(jnp.int32, (16, 128), 1)
        inside = jnp.logical_and(lane16 % 16 >= 4, lane16 % 16 < 12)

        def send_back(i, c):
            at = (blk + BLOCKS // 2 + jnp.where(i % 2 == 1, (i + 1) // 2, BLOCKS - i // 2)) % BLOCKS
            for rho in range(2):
                part = []
                for k in range(SECTIONS):
                    back = 4 if k < 3 else 0
                    start = (PITCH * at + NP - back + shifts[k][rho]) % NP
                    part.append(hb[k, 1 - rho, pl.ds(start, 16 if k < 3 else 8)])
                both = jnp.where(inside, part[0], pltpu.roll(part[1], 8, 1))
                third = jnp.where(inside, pltpu.roll(part[2], 80, 1), pltpu.roll(part[2], 40, 1))
                both = jnp.where(lane16 < 84, both, third)
                to = rho * BLOCKS + at
                st[to, 0] = both[0:8]
                st[to, 1] = both[8:16]
                st[to, 2] = part[3]
                other = rho * 1 + pair * 2
                self = jnp.logical_and(other == row, at == blk)

                @pl.when(jnp.logical_not(self))
                def _():
                    pltpu.make_async_remote_copy(
                        src_ref=st.at[to],
                        dst_ref=gbuf.at[z],
                        send_sem=ret_s,
                        recv_sem=ret_r,
                        device_id=(other, at),
                        device_id_type=MESH,
                    ).start()

            return c

        lax.fori_loop(0, BLOCKS, send_back, 0)
        gbuf[z] = st[parity * BLOCKS + blk]

    halo_copy(0).wait_recv()
    halo_copy(1).wait_recv()

    def widen_block(j, c):
        for h in range(2):
            a = 2 * j + h
            part = slice(4 * h, 4 * h + 4)
            for v in range(NVAR):
                fld[0, v, a, 0:4] = hr[0, v, j, part]
                fld[0, v, a, 4:12] = state[v, a]
                fld[0, v, a, 12:16] = hr[1, v, j, part]
            vext[a, 0:4] = hr[0, NVAR, j, part]
            vext[a, 4:12] = visc[a]
            vext[a, 12:16] = hr[1, NVAR, j, part]
        return c

    lax.fori_loop(0, AXIAL // 2, widen_block, 0)

    lane2 = lax.broadcasted_iota(jnp.int32, (16, 128), 1)
    first2, last2 = lane2 == 0, lane2 == SPAN - 1
    alive = lane2 < live[0]
    cs = [[coup[v, 0, w] for w in range(NVAR)] for v in range(NVAR)]

    def layer(k, a, up):
        here = [fld[k, v, a] for v in range(NVAR)]
        vis = vext[a]
        below = jnp.maximum(a - 1, 0)
        scale = jnp.where(alive, section_alphas[k] * time_step, 0.0)
        for v in range(NVAR):
            u = here[v]
            up_axial, down_axial = up(v), fld[k, v, below]
            up_pitch, down_pitch = pltpu.roll(u, 15, 0), pltpu.roll(u, 1, 0)
            up_span = jnp.where(last2, u, pltpu.roll(u, 127, 1))
            down_span = jnp.where(first2, u, pltpu.roll(u, 1, 1))
            rate = (
                speed_axial * (up_axial - u)
                - speed_pitch * (u - down_pitch)
                - speed_span * (u - down_span)
            )
            beside = up_axial + down_axial + up_pitch + down_pitch + up_span + down_span
            rate = rate + vis * (beside - 6.0 * u)
            for w in range(NVAR):
                rate = rate + cs[v][w] * here[w]
            new = fld[0, v, a] + scale * rate
            if k < SECTIONS - 1:
                fld[k + 1, v, a] = new
            else:
                out[v, a] = pltpu.roll(new, 12, 0)[0:8]

    for k in range(SECTIONS):

        def inner_layer(a, c):
            layer(k, a, lambda v: fld[k, v, a + 1])
            return c

        lax.fori_loop(0, AXIAL - 1 - k, inner_layer, 0)

    @pl.when(is_worker)
    def _():
        wait_bytes(gbuf.at[pl.ds(0, SLICES - 1)], ret_r)

    @pl.when(jnp.logical_not(is_worker))
    def _():
        wait_bytes(gbuf, ret_r)

    group8 = lane8 // 8
    for v in range(NVAR):
        places = [16 * v + 4, 16 * v + 12]
        places.append(84 + 16 * v if v < 3 else 92 + 16 * (v - 3))
        for k in range(3):
            for half in range(2):
                value = jnp.zeros((8, 128), jnp.float32)
                for s in range(SLICES):
                    turn = (8 * s - places[k]) % 128
                    value = jnp.where(group8 == s, pltpu.roll(gbuf[s, half], turn, 1), value)
                gx[k, v, 8 * half : 8 * half + 8] = value
        value = jnp.zeros((8, 128), jnp.float32)
        for s in range(SLICES):
            turn = (8 * s - (16 * v + 4)) % 128
            value = jnp.where(group8 == s, pltpu.roll(gbuf[s, 2], turn, 1), value)
        gx[3, v, 0:4] = jnp.zeros((4, 128), jnp.float32)
        gx[3, v, 4:12] = value
        gx[3, v, 12:16] = jnp.zeros((4, 128), jnp.float32)

    for k in range(SECTIONS):
        for a in range(AXIAL - 1 - k, AXIAL - 1):
            layer(k, a, lambda v: fld[k, v, a + 1])
        layer(k, AXIAL - 1, lambda v: gx[k, v])

    halo_copy(0).wait_send()
    halo_copy(1).wait_send()

    @pl.when(is_worker)
    def _():
        wait_bytes(st.at[pl.ds(0, 2 * BLOCKS - 1)], ret_s)


def solution(mesh):
    weighted, plain = basis_tables()

    def body(state, visc, coup, offs, live):
        vmem = pl.BlockSpec(memory_space=pltpu.VMEM)
        hbm = pl.BlockSpec(memory_space=pltpu.HBM)
        smem = pl.BlockSpec(memory_space=pltpu.SMEM)
        f32 = jnp.float32
        done = pl.pallas_call(
            kernel,
            out_shape=jax.ShapeDtypeStruct((NVAR, AXIAL, PITCH, SPAN), f32),
            in_specs=[hbm, hbm, smem, smem, smem, hbm, hbm],
            out_specs=vmem,
            scratch_shapes=[
                pltpu.VMEM((NVAR, AXIAL, PITCH, SPAN), f32),
                pltpu.VMEM((AXIAL, PITCH, SPAN), f32),
                pltpu.VMEM((32, NP), jnp.bfloat16),
                pltpu.VMEM((NP, 128), jnp.bfloat16),
                pltpu.VMEM((2, 384, 256), jnp.bfloat16),
                pltpu.SemaphoreType.DMA((4,)),
                pltpu.VMEM((SLICES, 3, 8, 128), f32),
                pltpu.VMEM((2, 3, NP + 2 * PAD, 128), f32),
                pltpu.VMEM((2, 16, 128), f32),
                pltpu.VMEM((2, NVAR + 1, AXIAL // 2, 8, 128), f32),
                pltpu.VMEM((2, NVAR + 1, AXIAL // 2, 8, 128), f32),
                pltpu.VMEM((2, 3, NP, 128), f32),
                pltpu.VMEM((2, 3, NP + 2 * PAD, 128), f32),
                pltpu.VMEM((2, 2, NP + 2 * PAD, 128), f32),
                pltpu.VMEM((2, NP + 2 * PAD, 128), f32),
                pltpu.VMEM((SECTIONS, 2, NP + WRAP, 128), f32),
                pltpu.VMEM((2 * BLOCKS, 3, 8, 128), f32),
                pltpu.VMEM((SLICES, 3, 8, 128), f32),
                pltpu.VMEM((SECTIONS, NVAR, AXIAL, 16, 128), f32),
                pltpu.VMEM((AXIAL, 16, 128), f32),
                pltpu.VMEM((SECTIONS, NVAR, 16, 128), f32),
                pltpu.SemaphoreType.DMA,
                pltpu.SemaphoreType.DMA,
                pltpu.SemaphoreType.DMA,
                pltpu.SemaphoreType.DMA,
                pltpu.SemaphoreType.DMA((2,)),
                pltpu.SemaphoreType.DMA((2,)),
                pltpu.SemaphoreType.DMA,
                pltpu.SemaphoreType.DMA,
            ],
            compiler_params=pltpu.CompilerParams(
                collective_id=0, has_side_effects=True, vmem_limit_bytes=63 << 20
            ),
            name="sections",
        )(state[0], visc[0], jnp.transpose(coup, (1, 0, 2)), offs, live, jnp.asarray(weighted), jnp.asarray(plain))
        return done[None]

    in_specs = (
        P("row", None, None, "blk", None),
        P("row", None, "blk", None),
        P("row", None, None),
        P(),
        P("row"),
    )
    out_specs = P("row", None, None, "blk", None)
    return jax.shard_map(body, mesh=mesh, in_specs=in_specs, out_specs=out_specs, check_vma=False)
```

```python
import functools
import math

import jax
import jax.numpy as jnp
import numpy as np
from jax import lax
from jax.experimental import pallas as pl
from jax.experimental.pallas import tpu as pltpu
from jax.sharding import PartitionSpec as P

MESH = pl.DeviceIdType.MESH
MODES = 5
SECTIONS = 4
NVAR = 5
AXIAL = 16
PITCH = 8
SPAN = 128
BLOCKS = 64
NP = BLOCKS * PITCH
SLICES = 16
CHUNK = 512
WRAP = 512
PAD = 8

section_alphas = (0.25, 1.0 / 3.0, 0.5, 1.0)
time_step = 0.25
speed_axial = 1.0
speed_pitch = 0.6
speed_span = 0.3

def split(value):
    high = value.astype(jnp.bfloat16)
    return high, (value - high.astype(jnp.float32)).astype(jnp.bfloat16)


def basis_tables():
    theta = np.arange(NP) * (2.0 * math.pi / NP)
    rows = [np.ones(NP)]
    rows += [np.cos(j * theta) for j in range(1, MODES + 1)]
    rows += [np.sin(j * theta) for j in range(1, MODES + 1)]
    table = np.zeros((16, NP), np.float32)
    table[: 2 * MODES + 1] = np.stack(rows)
    weights = np.full((16, 1), 2.0 / NP, np.float32)
    weights[0] = 1.0 / NP

    def parts(value):
        high = value.astype(jnp.bfloat16)
        return high, (value - high.astype(np.float32)).astype(jnp.bfloat16)

    back = np.zeros((NP, 128), jnp.bfloat16)
    high, low = parts(np.ascontiguousarray(table.T))
    back[:, 0:16], back[:, 16:32], back[:, 32:48] = high, low, high
    return np.concatenate(parts(table * weights)), back


def worker_of(pair, s):
    return 2 * pair + (s // 2) % 2, 4 * s + 2 * (s % 2)


def kernel(
    state_hbm, visc_hbm, coup, offs, live, basis_hbm, basis_t_hbm, out,
    state, visc, basis, basis_t, mix, size, load_s,
    msg, recv, cst, hs, hr, vb, xa, xb, xc, hb, st, gbuf, fld, vext, gx,
    main_s, main_r, cst_s, cst_r, halo_s, halo_r, ret_s, ret_r,
):
    loads = [
        pltpu.make_async_copy(source, target, load_s.at[i])
        for i, (source, target) in enumerate(
            [(state_hbm, state), (visc_hbm, visc), (basis_hbm, basis), (basis_t_hbm, basis_t)]
        )
    ]
    for load in loads:
        load.start()
    row = lax.axis_index("row")
    blk = lax.axis_index("blk")
    pair, parity = row // 2, row % 2
    z = blk // 4
    own_row, own_blk = worker_of(pair, z)
    is_worker = jnp.logical_and(own_row == row, own_blk == blk)
    after, before = (blk + 1) % BLOCKS, (blk + BLOCKS - 1) % BLOCKS

    many = size.at[pl.ds(0, 2 * BLOCKS - 1)]

    bar = pltpu.get_barrier_semaphore()

    def greet(r, b):
        pl.semaphore_signal(bar, inc=1, device_id=(r, b), device_id_type=MESH)

    @pl.when(is_worker)
    def _():
        def greet_source(i, c):
            at = (blk + BLOCKS // 2 + jnp.where(i % 2 == 1, (i + 1) // 2, BLOCKS - i // 2)) % BLOCKS
            greet(row ^ 1, at)

            @pl.when(at != blk)
            def _():
                greet(row, at)

            return c

        lax.fori_loop(0, BLOCKS, greet_source, 0)

    for i in range(SLICES):
        s = (z + SLICES // 2 + i) % SLICES
        wr, wb = worker_of(pair, s)

        @pl.when(jnp.logical_not(jnp.logical_and(wr == row, wb == blk)))
        def _():
            greet(wr, wb)

    greet(row, after)
    greet(row, before)
    greet(row ^ 1, blk)

    for load in loads:
        load.wait()

    lane8 = lax.broadcasted_iota(jnp.int32, (8, 128), 1)
    slot8 = lane8 // 16
    top = AXIAL - 1
    tiles = (
        [(v, top) for v in range(NVAR)] + [(-1, top), (-1, top - 1), (-1, top - 2)],
        [(v, top - 1) for v in range(NVAR)] + [(0, top - 3), (1, top - 3), (2, top - 3)],
        [(v, top - 2) for v in range(NVAR)] + [(3, top - 3), (4, top - 3)],
    )
    for t, slots in enumerate(tiles):
        values = [visc[a] if v < 0 else state[v, a] for v, a in slots]
        for s in range(SLICES):
            packed = jnp.zeros((8, 128), jnp.float32)
            for q, value in enumerate(values):
                turn = (16 * q - (8 * s - 4)) % 128
                moved = pltpu.roll(value, turn, 1) if turn else value
                packed = jnp.where(slot8 == q, moved, packed)
            msg[s, t] = packed

    sub8 = lax.broadcasted_iota(jnp.int32, (8, 128), 0)
    table = jnp.zeros((8, 128), jnp.float32)
    for v in range(NVAR):
        for w in range(NVAR):
            here = jnp.logical_and(slot8 == v, sub8 == (w - v) % 8)
            table = jnp.where(here, coup[v, 0, w], table)
    cst[parity, 0:8] = table
    cst[parity, 8:16] = jnp.full((8, 128), live[0].astype(jnp.float32))

    def pack_halo(j, c):
        for v in range(NVAR + 1):
            for h in range(2):
                if v < NVAR:
                    low = state[v, 2 * j + h, 0:4]
                    high = state[v, 2 * j + h, 4:8]
                else:
                    low = visc[2 * j + h, 0:4]
                    high = visc[2 * j + h, 4:8]
                hs[0, v, j, 4 * h : 4 * h + 4] = high
                hs[1, v, j, 4 * h : 4 * h + 4] = low
        return c

    lax.fori_loop(0, AXIAL // 2, pack_halo, 0)

    pl.semaphore_wait(bar, SLICES + 3 + jnp.where(is_worker, 2 * BLOCKS - 2, 0))

    mine = pl.ds(pl.multiple_of(PAD + PITCH * blk, 8), PITCH)

    def send_main(i, c):
        s = (z + SLICES // 2 + jnp.where(i % 2 == 1, (i + 1) // 2, SLICES - i // 2)) % SLICES
        wr, wb = worker_of(pair, s)
        self = jnp.logical_and(wr == row, wb == blk)

        @pl.when(jnp.logical_not(self))
        def _():
            pltpu.make_async_remote_copy(
                src_ref=msg.at[s],
                dst_ref=recv.at[parity, :, mine],
                send_sem=main_s,
                recv_sem=main_r,
                device_id=(wr, wb),
                device_id_type=MESH,
            ).start()

        return c

    lax.fori_loop(0, SLICES, send_main, 0)

    def const_copy():
        return pltpu.make_async_remote_copy(
            src_ref=cst.at[parity],
            dst_ref=cst.at[parity],
            send_sem=cst_s,
            recv_sem=cst_r,
            device_id=(row ^ 1, blk),
            device_id_type=MESH,
        )

    const_copy().start()

    def wait_bytes(ref, sem):
        pltpu.make_async_copy(ref, ref, sem).wait()

    @pl.when(is_worker)
    def _():
        wait_bytes(msg.at[pl.ds(0, SLICES - 1)], main_s)

    @pl.when(jnp.logical_not(is_worker))
    def _():
        wait_bytes(msg, main_s)

    def halo_copy(side):
        return pltpu.make_async_remote_copy(
            src_ref=hs.at[side],
            dst_ref=hr.at[side],
            send_sem=halo_s.at[side],
            recv_sem=halo_r.at[side],
            device_id=(row, after if side == 0 else before),
            device_id_type=MESH,
        )

    halo_copy(0).start()
    halo_copy(1).start()
    const_copy().wait_send()
    wait_bytes(cst.at[1 - parity], cst_r)

    @pl.when(is_worker)
    def _():
        recv[parity, :, mine] = msg[z]
        source = lax.broadcasted_iota(jnp.int32, (128, 128), 0)
        target = lax.broadcasted_iota(jnp.int32, (128, 128), 1)
        place = 8 * z - 4 + target % 16
        lower = jnp.where(place == 0, target, target - 1)
        upper = jnp.where(place == SPAN - 1, target, target + 1)

        def one(here):
            return jnp.where(here, 1.0, 0.0)

        around = one(source == lower) + one(source == upper) - 6.0 * one(source == target)
        still = speed_span * one(source == lower) - (
            speed_axial + speed_pitch + speed_span
        ) * one(source == target)
        for rho in range(2):
            both = still
            for d in range(8):
                both = both + jnp.where(
                    source == (target + 16 * d) % 128, cst[rho, d : d + 1], 0.0
                )
            high, low = split(both)
            for half in range(2):
                mix[rho, 128 * half : 128 * half + 128, 0:128] = high
                mix[rho, 128 * half : 128 * half + 128, 128:256] = around.astype(jnp.bfloat16)
                for q in range(3):
                    wide = one(source == 16 * (5 + q) + target % 16).astype(jnp.bfloat16)
                    mix[rho, 128 * half : 128 * half + 128, 256 + 128 * q : 384 + 128 * q] = wide
            mix[rho, 256:384, 0:128] = low
        wait_bytes(many, main_r)
        lane = lax.broadcasted_iota(jnp.int32, (CHUNK, 128), 1)
        slot = lane // 16
        cell = 8 * z - 4 + lane % 16
        cell_f = cell[0:1].astype(jnp.float32)

        def wrap(ref, *index):
            ref[(*index, slice(PAD - 1, PAD))] = ref[(*index, slice(PAD + NP - 1, PAD + NP))]
            ref[(*index, slice(PAD + NP, PAD + NP + 1))] = ref[(*index, slice(PAD, PAD + 1))]

        shifts = []
        for k in range(SECTIONS):
            turn = offs[k, pair]
            shifts.append((turn, (NP - turn) % NP))

        for rho in range(2):
            for t in range(3):
                wrap(recv, rho, t)

        fields = [
            [[(recv, (rho, t)) for t in range(3)] for rho in range(2)],
            [[(xa, (rho, t)) for t in range(3)] for rho in range(2)],
            [[(xb, (rho, t)) for t in range(2)] for rho in range(2)],
            [[(xc, (rho,))] for rho in range(2)],
        ]
        for k in range(SECTIONS):
            strips = []
            for rho in range(2):
                ref, index = fields[k][rho][0]
                strips.append(ref[(*index, slice(PAD, PAD + NP))])
            strips = jnp.concatenate(strips, 1)
            high, low = split(strips)
            sums = jnp.dot(basis[...], high, preferred_element_type=jnp.float32)
            coef = sums[0:16] + sums[16:32]
            coef = coef + jnp.dot(basis[0:16], low, preferred_element_type=jnp.float32)
            high, low = split(coef)
            coefs = jnp.concatenate([high, high, low, jnp.zeros((80, 256), jnp.bfloat16)], 0)
            recon = jnp.dot(basis_t[...], coefs, preferred_element_type=jnp.float32)
            half = 0.5 * (strips + recon)
            for rho in range(2):
                hb[k, rho, 0:NP] = half[:, 128 * rho : 128 * rho + 128]
                hb[k, rho, NP : NP + WRAP] = half[0:WRAP, 128 * rho : 128 * rho + 128]
            if k == SECTIONS - 1:
                break
            factor = section_alphas[k] * time_step
            for rho in range(2):
                table = cst[rho]
                scale = jnp.where(cell_f < table[8:9], factor, 0.0)

                def update(i, c):
                    at = pl.multiple_of(i * CHUNK, CHUNK)

                    def take(t, move=0):
                        ref, index = fields[k][rho][t]
                        return ref[(*index, pl.ds(PAD + at + move, CHUNK))]

                    inner = [take(t) for t in range(3 - k)]
                    vis = [vb[rho, t, pl.ds(at, CHUNK)] for t in range(3 - k)] if k else None
                    start = (at + shifts[k][rho]) % NP
                    ghost = hb[k, 1 - rho, pl.ds(start, CHUNK)]
                    for t in range(3 - k):
                        here = inner[t]
                        up_axial = ghost if t == 0 else inner[t - 1]
                        if t + 1 < 3 - k:
                            down_axial = inner[t + 1]
                        elif k == 0:
                            two = recv[rho, 1, pl.ds(PAD + at, CHUNK)]
                            three = recv[rho, 2, pl.ds(PAD + at, CHUNK)]
                            down_axial = jnp.where(
                                slot < 3, pltpu.roll(two, 48, 1), pltpu.roll(three, 96, 1)
                            )
                        else:
                            down_axial = take(t + 1)
                        up_pitch, down_pitch = take(t, 1), take(t, -1)
                        high, low = split(here)
                        first = k == 0 and t == 0
                        linear = jnp.dot(
                            jnp.concatenate([high, low], 1),
                            mix[rho, 0:256] if first else mix[rho, 0:256, 0:256],
                            preferred_element_type=jnp.float32,
                        )
                        if first:
                            vis = [linear[:, 256 + 128 * q : 384 + 128 * q] for q in range(3)]
                            for q in range(2):
                                vb[rho, q, pl.ds(at, CHUNK)] = vis[q]
                        low = jnp.dot(high, mix[rho, 256:384, 0:128], preferred_element_type=jnp.float32)
                        beside = up_axial + down_axial + up_pitch + down_pitch + linear[:, 128:256]
                        rate = speed_axial * up_axial + speed_pitch * down_pitch + low
                        rate = rate + linear[:, 0:128] + vis[t] * beside
                        ref, index = fields[k + 1][rho][t]
                        ref[(*index, pl.ds(PAD + at, CHUNK))] = (
                            recv[rho, t, pl.ds(PAD + at, CHUNK)] + scale * rate
                        )
                    return c

                lax.fori_loop(0, NP // CHUNK, update, 0)
                for t in range(3 - k):
                    ref, index = fields[k + 1][rho][t]
                    wrap(ref, *index)

        inside = jnp.logical_and(lane % 16 >= 4, lane % 16 < 12)
        for rho in range(2):

            def pack_back(i, c):
                at = pl.multiple_of(i * CHUNK, CHUNK)
                part = []
                for k in range(SECTIONS):
                    back = 4 if k < 3 else 0
                    start = (at + NP - back + shifts[k][rho]) % NP
                    part.append(hb[k, 1 - rho, pl.ds(start, CHUNK)])
                both = jnp.where(inside, part[0], pltpu.roll(part[1], 8, 1))
                third = jnp.where(inside, pltpu.roll(part[2], 80, 1), pltpu.roll(part[2], 40, 1))
                both = jnp.where(lane < 84, both, third)
                st[rho, 0, pl.ds(at, CHUNK)] = both
                st[rho, 1, pl.ds(at, CHUNK - 8)] = both[8:CHUNK]
                before_at = pl.multiple_of((at + NP - 8) % NP, 8)
                st[rho, 1, pl.ds(before_at, 8)] = both[0:8]
                st[rho, 2, pl.ds(at, CHUNK)] = part[3]
                return c

            lax.fori_loop(0, NP // CHUNK, pack_back, 0)

        def send_back(i, c):
            at = (blk + BLOCKS // 2 + jnp.where(i % 2 == 1, (i + 1) // 2, BLOCKS - i // 2)) % BLOCKS
            source_rows = pl.ds(pl.multiple_of(PITCH * at, 8), PITCH)
            for rho in range(2):
                other = 2 * pair + rho

                @pl.when(jnp.logical_not(jnp.logical_and(other == row, at == blk)))
                def _():
                    pltpu.make_async_remote_copy(
                        src_ref=st.at[rho, :, source_rows],
                        dst_ref=gbuf.at[z],
                        send_sem=ret_s,
                        recv_sem=ret_r,
                        device_id=(other, at),
                        device_id_type=MESH,
                    ).start()

            return c

        lax.fori_loop(0, BLOCKS, send_back, 0)
        gbuf[z] = st[parity, :, pl.ds(pl.multiple_of(PITCH * blk, 8), PITCH)]

    halo_copy(0).wait_recv()
    halo_copy(1).wait_recv()

    def widen_block(j, c):
        for h in range(2):
            a = 2 * j + h
            part = slice(4 * h, 4 * h + 4)
            for v in range(NVAR):
                fld[0, v, a, 0:4] = hr[0, v, j, part]
                fld[0, v, a, 4:12] = state[v, a]
                fld[0, v, a, 12:16] = hr[1, v, j, part]
            vext[a, 0:4] = hr[0, NVAR, j, part]
            vext[a, 4:12] = visc[a]
            vext[a, 12:16] = hr[1, NVAR, j, part]
        return c

    lax.fori_loop(0, AXIAL // 2, widen_block, 0)

    lane2 = lax.broadcasted_iota(jnp.int32, (16, 128), 1)
    first2, last2 = lane2 == 0, lane2 == SPAN - 1
    alive = lane2 < live[0]
    cs = [[coup[v, 0, w] for w in range(NVAR)] for v in range(NVAR)]

    def layer(k, a, up):
        here = [fld[k, v, a] for v in range(NVAR)]
        vis = vext[a]
        below = jnp.maximum(a - 1, 0)
        scale = jnp.where(alive, section_alphas[k] * time_step, 0.0)
        for v in range(NVAR):
            u = here[v]
            up_axial, down_axial = up(v), fld[k, v, below]
            up_pitch, down_pitch = pltpu.roll(u, 15, 0), pltpu.roll(u, 1, 0)
            up_span = jnp.where(last2, u, pltpu.roll(u, 127, 1))
            down_span = jnp.where(first2, u, pltpu.roll(u, 1, 1))
            rate = (
                speed_axial * (up_axial - u)
                - speed_pitch * (u - down_pitch)
                - speed_span * (u - down_span)
            )
            beside = up_axial + down_axial + up_pitch + down_pitch + up_span + down_span
            rate = rate + vis * (beside - 6.0 * u)
            for w in range(NVAR):
                rate = rate + cs[v][w] * here[w]
            new = fld[0, v, a] + scale * rate
            if k < SECTIONS - 1:
                fld[k + 1, v, a] = new
            else:
                out[v, a] = pltpu.roll(new, 12, 0)[0:8]

    for k in range(SECTIONS):

        def inner_layer(a, c):
            layer(k, a, lambda v: fld[k, v, a + 1])
            return c

        lax.fori_loop(0, AXIAL - 1 - k, inner_layer, 0)

    @pl.when(is_worker)
    def _():
        wait_bytes(gbuf.at[pl.ds(0, SLICES - 1)], ret_r)

    @pl.when(jnp.logical_not(is_worker))
    def _():
        wait_bytes(gbuf, ret_r)

    group8 = lane8 // 8
    for v in range(NVAR):
        places = [16 * v + 4, 16 * v + 12]
        places.append(84 + 16 * v if v < 3 else 92 + 16 * (v - 3))
        for k in range(3):
            for half in range(2):
                value = jnp.zeros((8, 128), jnp.float32)
                for s in range(SLICES):
                    turn = (8 * s - places[k]) % 128
                    value = jnp.where(group8 == s, pltpu.roll(gbuf[s, half], turn, 1), value)
                gx[k, v, 8 * half : 8 * half + 8] = value
        value = jnp.zeros((8, 128), jnp.float32)
        for s in range(SLICES):
            turn = (8 * s - (16 * v + 4)) % 128
            value = jnp.where(group8 == s, pltpu.roll(gbuf[s, 2], turn, 1), value)
        gx[3, v, 0:4] = jnp.zeros((4, 128), jnp.float32)
        gx[3, v, 4:12] = value
        gx[3, v, 12:16] = jnp.zeros((4, 128), jnp.float32)

    for k in range(SECTIONS):
        for a in range(AXIAL - 1 - k, AXIAL - 1):
            layer(k, a, lambda v: fld[k, v, a + 1])
        layer(k, AXIAL - 1, lambda v: gx[k, v])

    halo_copy(0).wait_send()
    halo_copy(1).wait_send()

    @pl.when(is_worker)
    def _():
        wait_bytes(many, ret_s)


def solution(mesh):
    weighted, plain = basis_tables()

    def body(state, visc, coup, offs, live):
        vmem = pl.BlockSpec(memory_space=pltpu.VMEM)
        hbm = pl.BlockSpec(memory_space=pltpu.HBM)
        smem = pl.BlockSpec(memory_space=pltpu.SMEM)
        f32 = jnp.float32
        done = pl.pallas_call(
            kernel,
            out_shape=jax.ShapeDtypeStruct((NVAR, AXIAL, PITCH, SPAN), f32),
            in_specs=[hbm, hbm, smem, smem, smem, hbm, hbm],
            out_specs=vmem,
            scratch_shapes=[
                pltpu.VMEM((NVAR, AXIAL, PITCH, SPAN), f32),
                pltpu.VMEM((AXIAL, PITCH, SPAN), f32),
                pltpu.VMEM((32, NP), jnp.bfloat16),
                pltpu.VMEM((NP, 128), jnp.bfloat16),
                pltpu.VMEM((2, 384, 640), jnp.bfloat16),
                pltpu.VMEM((2 * BLOCKS, 3, 8, 128), f32),
                pltpu.SemaphoreType.DMA((4,)),
                pltpu.VMEM((SLICES, 3, 8, 128), f32),
                pltpu.VMEM((2, 3, NP + 2 * PAD, 128), f32),
                pltpu.VMEM((2, 16, 128), f32),
                pltpu.VMEM((2, NVAR + 1, AXIAL // 2, 8, 128), f32),
                pltpu.VMEM((2, NVAR + 1, AXIAL // 2, 8, 128), f32),
                pltpu.VMEM((2, 2, NP, 128), f32),
                pltpu.VMEM((2, 3, NP + 2 * PAD, 128), f32),
                pltpu.VMEM((2, 2, NP + 2 * PAD, 128), f32),
                pltpu.VMEM((2, NP + 2 * PAD, 128), f32),
                pltpu.VMEM((SECTIONS, 2, NP + WRAP, 128), f32),
                pltpu.VMEM((2, 3, NP, 128), f32),
                pltpu.VMEM((SLICES, 3, 8, 128), f32),
                pltpu.VMEM((SECTIONS, NVAR, AXIAL, 16, 128), f32),
                pltpu.VMEM((AXIAL, 16, 128), f32),
                pltpu.VMEM((SECTIONS, NVAR, 16, 128), f32),
                pltpu.SemaphoreType.DMA,
                pltpu.SemaphoreType.DMA,
                pltpu.SemaphoreType.DMA,
                pltpu.SemaphoreType.DMA,
                pltpu.SemaphoreType.DMA((2,)),
                pltpu.SemaphoreType.DMA((2,)),
                pltpu.SemaphoreType.DMA,
                pltpu.SemaphoreType.DMA,
            ],
            compiler_params=pltpu.CompilerParams(
                collective_id=0, has_side_effects=True, vmem_limit_bytes=63 << 20
            ),
            name="sections",
        )(state[0], visc[0], jnp.transpose(coup, (1, 0, 2)), offs, live, jnp.asarray(weighted), jnp.asarray(plain))
        return done[None]

    in_specs = (
        P("row", None, None, "blk", None),
        P("row", None, "blk", None),
        P("row", None, None),
        P(),
        P("row"),
    )
    out_specs = P("row", None, None, "blk", None)
    return jax.shard_map(body, mesh=mesh, in_specs=in_specs, out_specs=out_specs, check_vma=False)
```

```python
import functools
import math

import jax
import jax.numpy as jnp
import numpy as np
from jax import lax
from jax.experimental import pallas as pl
from jax.experimental.pallas import tpu as pltpu
from jax.sharding import PartitionSpec as P

MESH = pl.DeviceIdType.MESH
MODES = 5
SECTIONS = 4
NVAR = 5
AXIAL = 16
PITCH = 8
SPAN = 128
BLOCKS = 64
NP = BLOCKS * PITCH
SLICES = 16
CHUNK = 512
WRAP = 512
PAD = 8

section_alphas = (0.25, 1.0 / 3.0, 0.5, 1.0)
time_step = 0.25
speed_axial = 1.0
speed_pitch = 0.6
speed_span = 0.3

def split(value):
    high = value.astype(jnp.bfloat16)
    return high, (value - high.astype(jnp.float32)).astype(jnp.bfloat16)


def basis_tables():
    theta = np.arange(NP) * (2.0 * math.pi / NP)
    rows = [np.ones(NP)]
    rows += [np.cos(j * theta) for j in range(1, MODES + 1)]
    rows += [np.sin(j * theta) for j in range(1, MODES + 1)]
    table = np.zeros((16, NP), np.float32)
    table[: 2 * MODES + 1] = np.stack(rows)
    weights = np.full((16, 1), 2.0 / NP, np.float32)
    weights[0] = 1.0 / NP

    def parts(value):
        high = value.astype(jnp.bfloat16)
        return high, (value - high.astype(np.float32)).astype(jnp.bfloat16)

    back = np.zeros((NP, 128), jnp.bfloat16)
    high, low = parts(np.ascontiguousarray(table.T))
    back[:, 0:16], back[:, 16:32], back[:, 32:48] = high, low, high
    return np.concatenate(parts(table * weights)), back


def worker_of(pair, s):
    return 2 * pair + (s // 2) % 2, 4 * s + 2 * (s % 2) + 1


def kernel(
    state_hbm, visc_hbm, coup, offs, live, basis_hbm, basis_t_hbm, out,
    state, visc, basis, basis_t, mix, size, load_s,
    msg, recv, hs, hr, vb, xa, xb, xc, hb, st, gbuf, fld, vext, gx,
    main_s, main_r, ready, halo_s, halo_r, ret_s, ret_r,
):
    loads = [
        pltpu.make_async_copy(source, target, load_s.at[i])
        for i, (source, target) in enumerate(
            [(state_hbm, state), (visc_hbm, visc), (basis_hbm, basis), (basis_t_hbm, basis_t)]
        )
    ]
    for load in loads:
        load.start()
    row = lax.axis_index("row")
    blk = lax.axis_index("blk")
    pair, parity = row // 2, row % 2
    z = blk // 4
    own_row, own_blk = worker_of(pair, z)
    is_worker = jnp.logical_and(own_row == row, own_blk == blk)
    after, before = (blk + 1) % BLOCKS, (blk + BLOCKS - 1) % BLOCKS

    many = size.at[pl.ds(0, 2 * BLOCKS - 1)]

    bar = pltpu.get_barrier_semaphore()

    def greet(r, b):
        pl.semaphore_signal(bar, inc=1, device_id=(r, b), device_id_type=MESH)

    @pl.when(is_worker)
    def _():
        def greet_source(i, c):
            at = (blk + BLOCKS // 2 + jnp.where(i % 2 == 1, (i + 1) // 2, BLOCKS - i // 2)) % BLOCKS
            greet(row ^ 1, at)

            @pl.when(at != blk)
            def _():
                greet(row, at)

            return c

        lax.fori_loop(0, BLOCKS, greet_source, 0)

    greet(row, after)

    for load in loads:
        load.wait()

    lane8 = lax.broadcasted_iota(jnp.int32, (8, 128), 1)
    slot8 = lane8 // 16
    top = AXIAL - 1
    tiles = (
        [(v, top) for v in range(NVAR)] + [(-1, top), (-1, top - 1), (-1, top - 2)],
        [(v, top - 1) for v in range(NVAR)] + [(0, top - 3), (1, top - 3), (2, top - 3)],
        [(v, top - 2) for v in range(NVAR)] + [(3, top - 3), (4, top - 3)],
    )
    sub8 = lax.broadcasted_iota(jnp.int32, (8, 128), 0)
    consts = jnp.where(lane8 == 112 + NVAR, live[0].astype(jnp.float32), 0.0)
    for v in range(NVAR):
        for w in range(NVAR):
            here = jnp.logical_and(lane8 == 112 + v, sub8 == (w - v) % 8)
            consts = jnp.where(here, coup[v, 0, w], consts)
    for t, slots in enumerate(tiles):
        values = [visc[a] if v < 0 else state[v, a] for v, a in slots]
        for s in range(SLICES):
            packed = consts if t == 2 else jnp.zeros((8, 128), jnp.float32)
            for q, value in enumerate(values):
                turn = (16 * q - (8 * s - 4)) % 128
                moved = pltpu.roll(value, turn, 1) if turn else value
                packed = jnp.where(slot8 == q, moved, packed)
            msg[s, t] = packed

    def pack_halo(j, c):
        for v in range(NVAR + 1):
            for h in range(2):
                if v < NVAR:
                    low = state[v, 2 * j + h, 0:4]
                    high = state[v, 2 * j + h, 4:8]
                else:
                    low = visc[2 * j + h, 0:4]
                    high = visc[2 * j + h, 4:8]
                hs[0, v, j, 4 * h : 4 * h + 4] = high
                hs[1, v, j, 4 * h : 4 * h + 4] = low
        return c

    lax.fori_loop(0, AXIAL // 2, pack_halo, 0)

    pl.semaphore_wait(bar, SLICES + 1 - jnp.where(is_worker, 1, 0))
    pl.semaphore_signal(ready, inc=1, device_id=(row, before), device_id_type=MESH)

    mine = pl.ds(pl.multiple_of(PAD + PITCH * blk, 8), PITCH)

    def send_main(i, c):
        s = (z + SLICES // 2 + jnp.where(i % 2 == 1, (i + 1) // 2, SLICES - i // 2)) % SLICES
        wr, wb = worker_of(pair, s)
        self = jnp.logical_and(wr == row, wb == blk)

        @pl.when(jnp.logical_not(self))
        def _():
            pltpu.make_async_remote_copy(
                src_ref=msg.at[s],
                dst_ref=recv.at[parity, :, mine],
                send_sem=main_s,
                recv_sem=main_r,
                device_id=(wr, wb),
                device_id_type=MESH,
            ).start()

        return c

    lax.fori_loop(0, SLICES, send_main, 0)

    def wait_bytes(ref, sem):
        pltpu.make_async_copy(ref, ref, sem).wait()

    @pl.when(is_worker)
    def _():
        wait_bytes(msg.at[pl.ds(0, SLICES - 1)], main_s)

    @pl.when(jnp.logical_not(is_worker))
    def _():
        wait_bytes(msg, main_s)

    def halo_copy(side):
        return pltpu.make_async_remote_copy(
            src_ref=hs.at[side],
            dst_ref=hr.at[side],
            send_sem=halo_s.at[side],
            recv_sem=halo_r.at[side],
            device_id=(row, after if side == 0 else before),
            device_id_type=MESH,
        )

    halo_copy(1).start()
    pl.semaphore_wait(ready, 1)
    halo_copy(0).start()

    @pl.when(is_worker)
    def _():
        recv[parity, :, mine] = msg[z]
        source = lax.broadcasted_iota(jnp.int32, (128, 128), 0)
        target = lax.broadcasted_iota(jnp.int32, (128, 128), 1)
        place = 8 * z - 4 + target % 16
        lower = jnp.where(place == 0, target, target - 1)
        upper = jnp.where(place == SPAN - 1, target, target + 1)

        def one(here):
            return jnp.where(here, 1.0, 0.0)

        around = one(source == lower) + one(source == upper) - 6.0 * one(source == target)
        still = speed_span * one(source == lower) - (
            speed_axial + speed_pitch + speed_span
        ) * one(source == target)
        for rho in range(2):
            for half in range(2):
                mix[rho, 128 * half : 128 * half + 128, 128:256] = around.astype(jnp.bfloat16)
                for q in range(3):
                    wide = one(source == 16 * (5 + q) + target % 16).astype(jnp.bfloat16)
                    mix[rho, 128 * half : 128 * half + 128, 256 + 128 * q : 384 + 128 * q] = wide
        wait_bytes(many, main_r)
        alive_to = []
        for rho in range(2):
            given = recv[rho, 2, PAD : PAD + 8]
            table = jnp.zeros((8, 128), jnp.float32)
            for v in range(NVAR):
                column = jnp.broadcast_to(given[:, 112 + v : 113 + v], (8, 128))
                table = jnp.where(slot8 == v, column, table)
            alive_to.append(given[0:1, 112 + NVAR : 113 + NVAR])
            both = still
            for d in range(8):
                both = both + jnp.where(source == (target + 16 * d) % 128, table[d : d + 1], 0.0)
            high, low = split(both)
            for half in range(2):
                mix[rho, 128 * half : 128 * half + 128, 0:128] = high
            mix[rho, 256:384, 0:128] = low
        lane = lax.broadcasted_iota(jnp.int32, (CHUNK, 128), 1)
        slot = lane // 16
        cell = 8 * z - 4 + lane % 16
        cell_f = cell[0:1].astype(jnp.float32)

        def wrap(ref, *index):
            ref[(*index, slice(PAD - 1, PAD))] = ref[(*index, slice(PAD + NP - 1, PAD + NP))]
            ref[(*index, slice(PAD + NP, PAD + NP + 1))] = ref[(*index, slice(PAD, PAD + 1))]

        shifts = []
        for k in range(SECTIONS):
            turn = offs[k, pair]
            shifts.append((turn, (NP - turn) % NP))

        for rho in range(2):
            for t in range(3):
                wrap(recv, rho, t)

        fields = [
            [[(recv, (rho, t)) for t in range(3)] for rho in range(2)],
            [[(xa, (rho, t)) for t in range(3)] for rho in range(2)],
            [[(xb, (rho, t)) for t in range(2)] for rho in range(2)],
            [[(xc, (rho,))] for rho in range(2)],
        ]
        for k in range(SECTIONS):
            strips = []
            for rho in range(2):
                ref, index = fields[k][rho][0]
                strips.append(ref[(*index, slice(PAD, PAD + NP))])
            strips = jnp.concatenate(strips, 1)
            high, low = split(strips)
            sums = jnp.dot(basis[...], high, preferred_element_type=jnp.float32)
            coef = sums[0:16] + sums[16:32]
            coef = coef + jnp.dot(basis[0:16], low, preferred_element_type=jnp.float32)
            high, low = split(coef)
            coefs = jnp.concatenate([high, high, low, jnp.zeros((80, 256), jnp.bfloat16)], 0)
            recon = jnp.dot(basis_t[...], coefs, preferred_element_type=jnp.float32)
            half = 0.5 * (strips + recon)
            for rho in range(2):
                hb[k, rho, 0:NP] = half[:, 128 * rho : 128 * rho + 128]
                hb[k, rho, NP : NP + WRAP] = half[0:WRAP, 128 * rho : 128 * rho + 128]
            if k == SECTIONS - 1:
                break
            factor = section_alphas[k] * time_step
            for rho in range(2):
                scale = jnp.where(cell_f < alive_to[rho], factor, 0.0)

                def update(i, c):
                    at = pl.multiple_of(i * CHUNK, CHUNK)

                    def take(t, move=0):
                        ref, index = fields[k][rho][t]
                        return ref[(*index, pl.ds(PAD + at + move, CHUNK))]

                    inner = [take(t) for t in range(3 - k)]
                    vis = [vb[rho, t, pl.ds(at, CHUNK)] for t in range(3 - k)] if k else None
                    start = (at + shifts[k][rho]) % NP
                    ghost = hb[k, 1 - rho, pl.ds(start, CHUNK)]
                    for t in range(3 - k):
                        here = inner[t]
                        up_axial = ghost if t == 0 else inner[t - 1]
                        if t + 1 < 3 - k:
                            down_axial = inner[t + 1]
                        elif k == 0:
                            two = recv[rho, 1, pl.ds(PAD + at, CHUNK)]
                            three = recv[rho, 2, pl.ds(PAD + at, CHUNK)]
                            down_axial = jnp.where(
                                slot < 3, pltpu.roll(two, 48, 1), pltpu.roll(three, 96, 1)
                            )
                        else:
                            down_axial = take(t + 1)
                        up_pitch, down_pitch = take(t, 1), take(t, -1)
                        high, low = split(here)
                        first = k == 0 and t == 0
                        linear = jnp.dot(
                            jnp.concatenate([high, low], 1),
                            mix[rho, 0:256] if first else mix[rho, 0:256, 0:256],
                            preferred_element_type=jnp.float32,
                        )
                        if first:
                            vis = [linear[:, 256 + 128 * q : 384 + 128 * q] for q in range(3)]
                            for q in range(2):
                                vb[rho, q, pl.ds(at, CHUNK)] = vis[q]
                        low = jnp.dot(high, mix[rho, 256:384, 0:128], preferred_element_type=jnp.float32)
                        beside = up_axial + down_axial + up_pitch + down_pitch + linear[:, 128:256]
                        rate = speed_axial * up_axial + speed_pitch * down_pitch + low
                        rate = rate + linear[:, 0:128] + vis[t] * beside
                        ref, index = fields[k + 1][rho][t]
                        ref[(*index, pl.ds(PAD + at, CHUNK))] = (
                            recv[rho, t, pl.ds(PAD + at, CHUNK)] + scale * rate
                        )
                    return c

                lax.fori_loop(0, NP // CHUNK, update, 0)
                for t in range(3 - k):
                    ref, index = fields[k + 1][rho][t]
                    wrap(ref, *index)

        inside = jnp.logical_and(lane % 16 >= 4, lane % 16 < 12)
        for rho in range(2):

            def pack_back(i, c):
                at = pl.multiple_of(i * CHUNK, CHUNK)
                part = []
                for k in range(SECTIONS):
                    back = 4 if k < 3 else 0
                    start = (at + NP - back + shifts[k][rho]) % NP
                    part.append(hb[k, 1 - rho, pl.ds(start, CHUNK)])
                both = jnp.where(inside, part[0], pltpu.roll(part[1], 8, 1))
                third = jnp.where(inside, pltpu.roll(part[2], 80, 1), pltpu.roll(part[2], 40, 1))
                both = jnp.where(lane < 84, both, third)
                st[rho, 0, pl.ds(at, CHUNK)] = both
                st[rho, 1, pl.ds(at, CHUNK - 8)] = both[8:CHUNK]
                before_at = pl.multiple_of((at + NP - 8) % NP, 8)
                st[rho, 1, pl.ds(before_at, 8)] = both[0:8]
                st[rho, 2, pl.ds(at, CHUNK)] = part[3]
                return c

            lax.fori_loop(0, NP // CHUNK, pack_back, 0)

        def send_back(i, c):
            at = (blk + BLOCKS // 2 + jnp.where(i % 2 == 1, (i + 1) // 2, BLOCKS - i // 2)) % BLOCKS
            source_rows = pl.ds(pl.multiple_of(PITCH * at, 8), PITCH)
            for rho in range(2):
                other = 2 * pair + rho

                @pl.when(jnp.logical_not(jnp.logical_and(other == row, at == blk)))
                def _():
                    pltpu.make_async_remote_copy(
                        src_ref=st.at[rho, :, source_rows],
                        dst_ref=gbuf.at[z],
                        send_sem=ret_s,
                        recv_sem=ret_r,
                        device_id=(other, at),
                        device_id_type=MESH,
                    ).start()

            return c

        lax.fori_loop(0, BLOCKS, send_back, 0)
        gbuf[z] = st[parity, :, pl.ds(pl.multiple_of(PITCH * blk, 8), PITCH)]

    halo_copy(0).wait_recv()
    halo_copy(1).wait_recv()

    def widen_block(j, c):
        for h in range(2):
            a = 2 * j + h
            part = slice(4 * h, 4 * h + 4)
            for v in range(NVAR):
                fld[0, v, a, 0:4] = hr[0, v, j, part]
                fld[0, v, a, 4:12] = state[v, a]
                fld[0, v, a, 12:16] = hr[1, v, j, part]
            vext[a, 0:4] = hr[0, NVAR, j, part]
            vext[a, 4:12] = visc[a]
            vext[a, 12:16] = hr[1, NVAR, j, part]
        return c

    lax.fori_loop(0, AXIAL // 2, widen_block, 0)

    lane2 = lax.broadcasted_iota(jnp.int32, (16, 128), 1)
    first2, last2 = lane2 == 0, lane2 == SPAN - 1
    alive = lane2 < live[0]
    cs = [[coup[v, 0, w] for w in range(NVAR)] for v in range(NVAR)]

    def layer(k, a, up):
        here = [fld[k, v, a] for v in range(NVAR)]
        vis = vext[a]
        below = jnp.maximum(a - 1, 0)
        scale = jnp.where(alive, section_alphas[k] * time_step, 0.0)
        for v in range(NVAR):
            u = here[v]
            up_axial, down_axial = up(v), fld[k, v, below]
            up_pitch, down_pitch = pltpu.roll(u, 15, 0), pltpu.roll(u, 1, 0)
            up_span = jnp.where(last2, u, pltpu.roll(u, 127, 1))
            down_span = jnp.where(first2, u, pltpu.roll(u, 1, 1))
            rate = (
                speed_axial * (up_axial - u)
                - speed_pitch * (u - down_pitch)
                - speed_span * (u - down_span)
            )
            beside = up_axial + down_axial + up_pitch + down_pitch + up_span + down_span
            rate = rate + vis * (beside - 6.0 * u)
            for w in range(NVAR):
                rate = rate + cs[v][w] * here[w]
            new = fld[0, v, a] + scale * rate
            if k < SECTIONS - 1:
                fld[k + 1, v, a] = new
            else:
                out[v, a] = pltpu.roll(new, 12, 0)[0:8]

    for k in range(SECTIONS):

        def inner_layer(a, c):
            layer(k, a, lambda v: fld[k, v, a + 1])
            return c

        lax.fori_loop(0, AXIAL - 1 - k, inner_layer, 0)

    @pl.when(is_worker)
    def _():
        wait_bytes(gbuf.at[pl.ds(0, SLICES - 1)], ret_r)

    @pl.when(jnp.logical_not(is_worker))
    def _():
        wait_bytes(gbuf, ret_r)

    group8 = lane8 // 8
    for v in range(NVAR):
        places = [16 * v + 4, 16 * v + 12]
        places.append(84 + 16 * v if v < 3 else 92 + 16 * (v - 3))
        for k in range(3):
            for half in range(2):
                value = jnp.zeros((8, 128), jnp.float32)
                for s in range(SLICES):
                    turn = (8 * s - places[k]) % 128
                    value = jnp.where(group8 == s, pltpu.roll(gbuf[s, half], turn, 1), value)
                gx[k, v, 8 * half : 8 * half + 8] = value
        value = jnp.zeros((8, 128), jnp.float32)
        for s in range(SLICES):
            turn = (8 * s - (16 * v + 4)) % 128
            value = jnp.where(group8 == s, pltpu.roll(gbuf[s, 2], turn, 1), value)
        gx[3, v, 0:4] = jnp.zeros((4, 128), jnp.float32)
        gx[3, v, 4:12] = value
        gx[3, v, 12:16] = jnp.zeros((4, 128), jnp.float32)

    for k in range(SECTIONS):
        for a in range(AXIAL - 1 - k, AXIAL - 1):
            layer(k, a, lambda v: fld[k, v, a + 1])
        layer(k, AXIAL - 1, lambda v: gx[k, v])

    halo_copy(0).wait_send()
    halo_copy(1).wait_send()

    @pl.when(is_worker)
    def _():
        wait_bytes(many, ret_s)


def solution(mesh):
    weighted, plain = basis_tables()

    def body(state, visc, coup, offs, live):
        vmem = pl.BlockSpec(memory_space=pltpu.VMEM)
        hbm = pl.BlockSpec(memory_space=pltpu.HBM)
        smem = pl.BlockSpec(memory_space=pltpu.SMEM)
        f32 = jnp.float32
        done = pl.pallas_call(
            kernel,
            out_shape=jax.ShapeDtypeStruct((NVAR, AXIAL, PITCH, SPAN), f32),
            in_specs=[hbm, hbm, smem, smem, smem, hbm, hbm],
            out_specs=vmem,
            scratch_shapes=[
                pltpu.VMEM((NVAR, AXIAL, PITCH, SPAN), f32),
                pltpu.VMEM((AXIAL, PITCH, SPAN), f32),
                pltpu.VMEM((32, NP), jnp.bfloat16),
                pltpu.VMEM((NP, 128), jnp.bfloat16),
                pltpu.VMEM((2, 384, 640), jnp.bfloat16),
                pltpu.VMEM((2 * BLOCKS, 3, 8, 128), f32),
                pltpu.SemaphoreType.DMA((4,)),
                pltpu.VMEM((SLICES, 3, 8, 128), f32),
                pltpu.VMEM((2, 3, NP + 2 * PAD, 128), f32),
                pltpu.VMEM((2, NVAR + 1, AXIAL // 2, 8, 128), f32),
                pltpu.VMEM((2, NVAR + 1, AXIAL // 2, 8, 128), f32),
                pltpu.VMEM((2, 2, NP, 128), f32),
                pltpu.VMEM((2, 3, NP + 2 * PAD, 128), f32),
                pltpu.VMEM((2, 2, NP + 2 * PAD, 128), f32),
                pltpu.VMEM((2, NP + 2 * PAD, 128), f32),
                pltpu.VMEM((SECTIONS, 2, NP + WRAP, 128), f32),
                pltpu.VMEM((2, 3, NP, 128), f32),
                pltpu.VMEM((SLICES, 3, 8, 128), f32),
                pltpu.VMEM((SECTIONS, NVAR, AXIAL, 16, 128), f32),
                pltpu.VMEM((AXIAL, 16, 128), f32),
                pltpu.VMEM((SECTIONS, NVAR, 16, 128), f32),
                pltpu.SemaphoreType.DMA,
                pltpu.SemaphoreType.DMA,
                pltpu.SemaphoreType.REGULAR,
                pltpu.SemaphoreType.DMA((2,)),
                pltpu.SemaphoreType.DMA((2,)),
                pltpu.SemaphoreType.DMA,
                pltpu.SemaphoreType.DMA,
            ],
            compiler_params=pltpu.CompilerParams(
                collective_id=0, has_side_effects=True, vmem_limit_bytes=63 << 20
            ),
            name="sections",
        )(state[0], visc[0], jnp.transpose(coup, (1, 0, 2)), offs, live, jnp.asarray(weighted), jnp.asarray(plain))
        return done[None]

    in_specs = (
        P("row", None, None, "blk", None),
        P("row", None, "blk", None),
        P("row", None, None),
        P(),
        P("row"),
    )
    out_specs = P("row", None, None, "blk", None)
    return jax.shard_map(body, mesh=mesh, in_specs=in_specs, out_specs=out_specs, check_vma=False)
```

```python
import functools
import math

import jax
import jax.numpy as jnp
import numpy as np
from jax import lax
from jax.experimental import pallas as pl
from jax.experimental.pallas import tpu as pltpu
from jax.sharding import PartitionSpec as P

MESH = pl.DeviceIdType.MESH
MODES = 5
SECTIONS = 4
NVAR = 5
AXIAL = 16
PITCH = 8
SPAN = 128
BLOCKS = 64
NP = BLOCKS * PITCH
SLICES = 16
CHUNK = 512
WRAP = 512
PAD = 8

section_alphas = (0.25, 1.0 / 3.0, 0.5, 1.0)
time_step = 0.25
speed_axial = 1.0
speed_pitch = 0.6
speed_span = 0.3

def split(value):
    high = value.astype(jnp.bfloat16)
    return high, (value - high.astype(jnp.float32)).astype(jnp.bfloat16)


def basis_tables():
    theta = np.arange(NP) * (2.0 * math.pi / NP)
    rows = [np.ones(NP)]
    rows += [np.cos(j * theta) for j in range(1, MODES + 1)]
    rows += [np.sin(j * theta) for j in range(1, MODES + 1)]
    table = np.zeros((16, NP), np.float32)
    table[: 2 * MODES + 1] = np.stack(rows)
    weights = np.full((16, 1), 2.0 / NP, np.float32)
    weights[0] = 1.0 / NP

    def parts(value):
        high = value.astype(jnp.bfloat16)
        return high, (value - high.astype(np.float32)).astype(jnp.bfloat16)

    back = np.zeros((NP, 128), jnp.bfloat16)
    high, low = parts(np.ascontiguousarray(table.T))
    back[:, 0:16], back[:, 16:32], back[:, 32:48] = high, low, high
    return np.concatenate(parts(table * weights)), back


def worker_of(pair, s):
    plane = 2 * (s // 2) + pair % 2
    return 2 * pair + (s // 2) % 2, 4 * plane + 2 * (s % 2) + 1


def kernel(
    state_hbm, visc_hbm, coup, offs, live, basis_hbm, basis_t_hbm, out,
    state, visc, basis, basis_t, mix, size, load_s,
    msg, recv, hs, hr, vb, xa, xb, xc, hb, st, gbuf, fld, vext, gx,
    main_s, main_r, ready, halo_s, halo_r, ret_s, ret_r,
):
    loads = [
        pltpu.make_async_copy(source, target, load_s.at[i])
        for i, (source, target) in enumerate(
            [(state_hbm, state), (visc_hbm, visc), (basis_hbm, basis), (basis_t_hbm, basis_t)]
        )
    ]
    for load in loads:
        load.start()
    row = lax.axis_index("row")
    blk = lax.axis_index("blk")
    pair, parity = row // 2, row % 2
    z = blk // 4
    own = 2 * (z // 2) + (blk // 2) % 2
    own_row, own_blk = worker_of(pair, own)
    is_worker = jnp.logical_and(own_row == row, own_blk == blk)
    after, before = (blk + 1) % BLOCKS, (blk + BLOCKS - 1) % BLOCKS

    many = size.at[pl.ds(0, 2 * BLOCKS - 1)]

    bar = pltpu.get_barrier_semaphore()

    def greet(r, b):
        pl.semaphore_signal(bar, inc=1, device_id=(r, b), device_id_type=MESH)

    @pl.when(is_worker)
    def _():
        def greet_source(i, c):
            at = (blk + BLOCKS // 2 + jnp.where(i % 2 == 1, (i + 1) // 2, BLOCKS - i // 2)) % BLOCKS
            greet(row ^ 1, at)

            @pl.when(at != blk)
            def _():
                greet(row, at)

            return c

        lax.fori_loop(0, BLOCKS, greet_source, 0)

    greet(row, after)

    for load in loads:
        load.wait()

    lane8 = lax.broadcasted_iota(jnp.int32, (8, 128), 1)
    slot8 = lane8 // 16
    top = AXIAL - 1
    tiles = (
        [(v, top) for v in range(NVAR)] + [(-1, top), (-1, top - 1), (-1, top - 2)],
        [(v, top - 1) for v in range(NVAR)] + [(0, top - 3), (1, top - 3), (2, top - 3)],
        [(v, top - 2) for v in range(NVAR)] + [(3, top - 3), (4, top - 3)],
    )
    sub8 = lax.broadcasted_iota(jnp.int32, (8, 128), 0)
    consts = jnp.where(lane8 == 112 + NVAR, live[0].astype(jnp.float32), 0.0)
    for v in range(NVAR):
        for w in range(NVAR):
            here = jnp.logical_and(lane8 == 112 + v, sub8 == (w - v) % 8)
            consts = jnp.where(here, coup[v, 0, w], consts)
    for t, slots in enumerate(tiles):
        values = [visc[a] if v < 0 else state[v, a] for v, a in slots]
        for s in range(SLICES):
            packed = consts if t == 2 else jnp.zeros((8, 128), jnp.float32)
            for q, value in enumerate(values):
                turn = (16 * q - (8 * s - 4)) % 128
                moved = pltpu.roll(value, turn, 1) if turn else value
                packed = jnp.where(slot8 == q, moved, packed)
            msg[s, t] = packed

    def pack_halo(j, c):
        for v in range(NVAR + 1):
            for h in range(2):
                if v < NVAR:
                    low = state[v, 2 * j + h, 0:4]
                    high = state[v, 2 * j + h, 4:8]
                else:
                    low = visc[2 * j + h, 0:4]
                    high = visc[2 * j + h, 4:8]
                hs[0, v, j, 4 * h : 4 * h + 4] = high
                hs[1, v, j, 4 * h : 4 * h + 4] = low
        return c

    lax.fori_loop(0, AXIAL // 2, pack_halo, 0)

    pl.semaphore_wait(bar, SLICES + 1 - jnp.where(is_worker, 1, 0))
    pl.semaphore_signal(ready, inc=1, device_id=(row, before), device_id_type=MESH)

    mine = pl.ds(pl.multiple_of(PAD + PITCH * blk, 8), PITCH)

    def send_main(i, c):
        s = (z + SLICES // 2 + jnp.where(i % 2 == 1, (i + 1) // 2, SLICES - i // 2)) % SLICES
        wr, wb = worker_of(pair, s)
        self = jnp.logical_and(wr == row, wb == blk)

        @pl.when(jnp.logical_not(self))
        def _():
            pltpu.make_async_remote_copy(
                src_ref=msg.at[s],
                dst_ref=recv.at[parity, :, mine],
                send_sem=main_s,
                recv_sem=main_r,
                device_id=(wr, wb),
                device_id_type=MESH,
            ).start()

        return c

    lax.fori_loop(0, SLICES, send_main, 0)

    def wait_bytes(ref, sem):
        pltpu.make_async_copy(ref, ref, sem).wait()

    @pl.when(is_worker)
    def _():
        wait_bytes(msg.at[pl.ds(0, SLICES - 1)], main_s)

    @pl.when(jnp.logical_not(is_worker))
    def _():
        wait_bytes(msg, main_s)

    def halo_copy(side):
        return pltpu.make_async_remote_copy(
            src_ref=hs.at[side],
            dst_ref=hr.at[side],
            send_sem=halo_s.at[side],
            recv_sem=halo_r.at[side],
            device_id=(row, after if side == 0 else before),
            device_id_type=MESH,
        )

    halo_copy(1).start()
    pl.semaphore_wait(ready, 1)
    halo_copy(0).start()

    @pl.when(is_worker)
    def _():
        recv[parity, :, mine] = msg[own]
        source = lax.broadcasted_iota(jnp.int32, (128, 128), 0)
        target = lax.broadcasted_iota(jnp.int32, (128, 128), 1)
        place = 8 * own - 4 + target % 16
        lower = jnp.where(place == 0, target, target - 1)
        upper = jnp.where(place == SPAN - 1, target, target + 1)

        def one(here):
            return jnp.where(here, 1.0, 0.0)

        around = one(source == lower) + one(source == upper) - 6.0 * one(source == target)
        still = speed_span * one(source == lower) - (
            speed_axial + speed_pitch + speed_span
        ) * one(source == target)
        for rho in range(2):
            for half in range(2):
                mix[rho, 128 * half : 128 * half + 128, 128:256] = around.astype(jnp.bfloat16)
                for q in range(3):
                    wide = one(source == 16 * (5 + q) + target % 16).astype(jnp.bfloat16)
                    mix[rho, 128 * half : 128 * half + 128, 256 + 128 * q : 384 + 128 * q] = wide
        wait_bytes(many, main_r)
        alive_to = []
        for rho in range(2):
            given = recv[rho, 2, PAD : PAD + 8]
            table = jnp.zeros((8, 128), jnp.float32)
            for v in range(NVAR):
                column = jnp.broadcast_to(given[:, 112 + v : 113 + v], (8, 128))
                table = jnp.where(slot8 == v, column, table)
            alive_to.append(given[0:1, 112 + NVAR : 113 + NVAR])
            both = still
            for d in range(8):
                both = both + jnp.where(source == (target + 16 * d) % 128, table[d : d + 1], 0.0)
            high, low = split(both)
            for half in range(2):
                mix[rho, 128 * half : 128 * half + 128, 0:128] = high
            mix[rho, 256:384, 0:128] = low
        lane = lax.broadcasted_iota(jnp.int32, (CHUNK, 128), 1)
        slot = lane // 16
        cell = 8 * own - 4 + lane % 16
        cell_f = cell[0:1].astype(jnp.float32)

        def wrap(ref, *index):
            ref[(*index, slice(PAD - 1, PAD))] = ref[(*index, slice(PAD + NP - 1, PAD + NP))]
            ref[(*index, slice(PAD + NP, PAD + NP + 1))] = ref[(*index, slice(PAD, PAD + 1))]

        shifts = []
        for k in range(SECTIONS):
            turn = offs[k, pair]
            shifts.append((turn, (NP - turn) % NP))

        for rho in range(2):
            for t in range(3):
                wrap(recv, rho, t)

        fields = [
            [[(recv, (rho, t)) for t in range(3)] for rho in range(2)],
            [[(xa, (rho, t)) for t in range(3)] for rho in range(2)],
            [[(xb, (rho, t)) for t in range(2)] for rho in range(2)],
            [[(xc, (rho,))] for rho in range(2)],
        ]
        for k in range(SECTIONS):
            strips = []
            for rho in range(2):
                ref, index = fields[k][rho][0]
                strips.append(ref[(*index, slice(PAD, PAD + NP))])
            strips = jnp.concatenate(strips, 1)
            high, low = split(strips)
            sums = jnp.dot(basis[...], high, preferred_element_type=jnp.float32)
            coef = sums[0:16] + sums[16:32]
            coef = coef + jnp.dot(basis[0:16], low, preferred_element_type=jnp.float32)
            high, low = split(coef)
            coefs = jnp.concatenate([high, high, low, jnp.zeros((80, 256), jnp.bfloat16)], 0)
            recon = jnp.dot(basis_t[...], coefs, preferred_element_type=jnp.float32)
            half = 0.5 * (strips + recon)
            for rho in range(2):
                hb[k, rho, 0:NP] = half[:, 128 * rho : 128 * rho + 128]
                hb[k, rho, NP : NP + WRAP] = half[0:WRAP, 128 * rho : 128 * rho + 128]
            if k == SECTIONS - 1:
                break
            factor = section_alphas[k] * time_step
            for rho in range(2):
                scale = jnp.where(cell_f < alive_to[rho], factor, 0.0)

                def update(i, c):
                    at = pl.multiple_of(i * CHUNK, CHUNK)

                    def take(t, move=0):
                        ref, index = fields[k][rho][t]
                        return ref[(*index, pl.ds(PAD + at + move, CHUNK))]

                    inner = [take(t) for t in range(3 - k)]
                    vis = [vb[rho, t, pl.ds(at, CHUNK)] for t in range(3 - k)] if k else None
                    start = (at + shifts[k][rho]) % NP
                    ghost = hb[k, 1 - rho, pl.ds(start, CHUNK)]
                    for t in range(3 - k):
                        here = inner[t]
                        up_axial = ghost if t == 0 else inner[t - 1]
                        if t + 1 < 3 - k:
                            down_axial = inner[t + 1]
                        elif k == 0:
                            two = recv[rho, 1, pl.ds(PAD + at, CHUNK)]
                            three = recv[rho, 2, pl.ds(PAD + at, CHUNK)]
                            down_axial = jnp.where(
                                slot < 3, pltpu.roll(two, 48, 1), pltpu.roll(three, 96, 1)
                            )
                        else:
                            down_axial = take(t + 1)
                        up_pitch, down_pitch = take(t, 1), take(t, -1)
                        high, low = split(here)
                        first = k == 0 and t == 0
                        linear = jnp.dot(
                            jnp.concatenate([high, low], 1),
                            mix[rho, 0:256] if first else mix[rho, 0:256, 0:256],
                            preferred_element_type=jnp.float32,
                        )
                        if first:
                            vis = [linear[:, 256 + 128 * q : 384 + 128 * q] for q in range(3)]
                            for q in range(2):
                                vb[rho, q, pl.ds(at, CHUNK)] = vis[q]
                        low = jnp.dot(high, mix[rho, 256:384, 0:128], preferred_element_type=jnp.float32)
                        beside = up_axial + down_axial + up_pitch + down_pitch + linear[:, 128:256]
                        rate = speed_axial * up_axial + speed_pitch * down_pitch + low
                        rate = rate + linear[:, 0:128] + vis[t] * beside
                        ref, index = fields[k + 1][rho][t]
                        ref[(*index, pl.ds(PAD + at, CHUNK))] = (
                            recv[rho, t, pl.ds(PAD + at, CHUNK)] + scale * rate
                        )
                    return c

                lax.fori_loop(0, NP // CHUNK, update, 0)
                for t in range(3 - k):
                    ref, index = fields[k + 1][rho][t]
                    wrap(ref, *index)

        inside = jnp.logical_and(lane % 16 >= 4, lane % 16 < 12)
        for rho in range(2):

            def pack_back(i, c):
                at = pl.multiple_of(i * CHUNK, CHUNK)
                part = []
                for k in range(SECTIONS):
                    back = 4 if k < 3 else 0
                    start = (at + NP - back + shifts[k][rho]) % NP
                    part.append(hb[k, 1 - rho, pl.ds(start, CHUNK)])
                both = jnp.where(inside, part[0], pltpu.roll(part[1], 8, 1))
                third = jnp.where(inside, pltpu.roll(part[2], 80, 1), pltpu.roll(part[2], 40, 1))
                both = jnp.where(lane < 84, both, third)
                st[rho, 0, pl.ds(at, CHUNK)] = both
                st[rho, 1, pl.ds(at, CHUNK - 8)] = both[8:CHUNK]
                before_at = pl.multiple_of((at + NP - 8) % NP, 8)
                st[rho, 1, pl.ds(before_at, 8)] = both[0:8]
                st[rho, 2, pl.ds(at, CHUNK)] = part[3]
                return c

            lax.fori_loop(0, NP // CHUNK, pack_back, 0)

        def send_back(i, c):
            at = (blk + BLOCKS // 2 + jnp.where(i % 2 == 1, (i + 1) // 2, BLOCKS - i // 2)) % BLOCKS
            source_rows = pl.ds(pl.multiple_of(PITCH * at, 8), PITCH)
            for rho in range(2):
                other = 2 * pair + rho

                @pl.when(jnp.logical_not(jnp.logical_and(other == row, at == blk)))
                def _():
                    pltpu.make_async_remote_copy(
                        src_ref=st.at[rho, :, source_rows],
                        dst_ref=gbuf.at[own],
                        send_sem=ret_s,
                        recv_sem=ret_r,
                        device_id=(other, at),
                        device_id_type=MESH,
                    ).start()

            return c

        lax.fori_loop(0, BLOCKS, send_back, 0)
        gbuf[own] = st[parity, :, pl.ds(pl.multiple_of(PITCH * blk, 8), PITCH)]

    halo_copy(0).wait_recv()
    halo_copy(1).wait_recv()

    def widen_block(j, c):
        for h in range(2):
            a = 2 * j + h
            part = slice(4 * h, 4 * h + 4)
            for v in range(NVAR):
                fld[0, v, a, 0:4] = hr[0, v, j, part]
                fld[0, v, a, 4:12] = state[v, a]
                fld[0, v, a, 12:16] = hr[1, v, j, part]
            vext[a, 0:4] = hr[0, NVAR, j, part]
            vext[a, 4:12] = visc[a]
            vext[a, 12:16] = hr[1, NVAR, j, part]
        return c

    lax.fori_loop(0, AXIAL // 2, widen_block, 0)

    lane2 = lax.broadcasted_iota(jnp.int32, (16, 128), 1)
    first2, last2 = lane2 == 0, lane2 == SPAN - 1
    alive = lane2 < live[0]
    cs = [[coup[v, 0, w] for w in range(NVAR)] for v in range(NVAR)]

    def layer(k, a, up):
        here = [fld[k, v, a] for v in range(NVAR)]
        vis = vext[a]
        below = jnp.maximum(a - 1, 0)
        scale = jnp.where(alive, section_alphas[k] * time_step, 0.0)
        for v in range(NVAR):
            u = here[v]
            up_axial, down_axial = up(v), fld[k, v, below]
            up_pitch, down_pitch = pltpu.roll(u, 15, 0), pltpu.roll(u, 1, 0)
            up_span = jnp.where(last2, u, pltpu.roll(u, 127, 1))
            down_span = jnp.where(first2, u, pltpu.roll(u, 1, 1))
            rate = (
                speed_axial * (up_axial - u)
                - speed_pitch * (u - down_pitch)
                - speed_span * (u - down_span)
            )
            beside = up_axial + down_axial + up_pitch + down_pitch + up_span + down_span
            rate = rate + vis * (beside - 6.0 * u)
            for w in range(NVAR):
                rate = rate + cs[v][w] * here[w]
            new = fld[0, v, a] + scale * rate
            if k < SECTIONS - 1:
                fld[k + 1, v, a] = new
            else:
                out[v, a] = pltpu.roll(new, 12, 0)[0:8]

    for k in range(SECTIONS):

        def inner_layer(a, c):
            layer(k, a, lambda v: fld[k, v, a + 1])
            return c

        lax.fori_loop(0, AXIAL - 1 - k, inner_layer, 0)

    @pl.when(is_worker)
    def _():
        wait_bytes(gbuf.at[pl.ds(0, SLICES - 1)], ret_r)

    @pl.when(jnp.logical_not(is_worker))
    def _():
        wait_bytes(gbuf, ret_r)

    group8 = lane8 // 8
    for v in range(NVAR):
        places = [16 * v + 4, 16 * v + 12]
        places.append(84 + 16 * v if v < 3 else 92 + 16 * (v - 3))
        for k in range(3):
            for half in range(2):
                value = jnp.zeros((8, 128), jnp.float32)
                for s in range(SLICES):
                    turn = (8 * s - places[k]) % 128
                    value = jnp.where(group8 == s, pltpu.roll(gbuf[s, half], turn, 1), value)
                gx[k, v, 8 * half : 8 * half + 8] = value
        value = jnp.zeros((8, 128), jnp.float32)
        for s in range(SLICES):
            turn = (8 * s - (16 * v + 4)) % 128
            value = jnp.where(group8 == s, pltpu.roll(gbuf[s, 2], turn, 1), value)
        gx[3, v, 0:4] = jnp.zeros((4, 128), jnp.float32)
        gx[3, v, 4:12] = value
        gx[3, v, 12:16] = jnp.zeros((4, 128), jnp.float32)

    for k in range(SECTIONS):
        for a in range(AXIAL - 1 - k, AXIAL - 1):
            layer(k, a, lambda v: fld[k, v, a + 1])
        layer(k, AXIAL - 1, lambda v: gx[k, v])

    halo_copy(0).wait_send()
    halo_copy(1).wait_send()

    @pl.when(is_worker)
    def _():
        wait_bytes(many, ret_s)


def solution(mesh):
    weighted, plain = basis_tables()

    def body(state, visc, coup, offs, live):
        vmem = pl.BlockSpec(memory_space=pltpu.VMEM)
        hbm = pl.BlockSpec(memory_space=pltpu.HBM)
        smem = pl.BlockSpec(memory_space=pltpu.SMEM)
        f32 = jnp.float32
        done = pl.pallas_call(
            kernel,
            out_shape=jax.ShapeDtypeStruct((NVAR, AXIAL, PITCH, SPAN), f32),
            in_specs=[hbm, hbm, smem, smem, smem, hbm, hbm],
            out_specs=vmem,
            scratch_shapes=[
                pltpu.VMEM((NVAR, AXIAL, PITCH, SPAN), f32),
                pltpu.VMEM((AXIAL, PITCH, SPAN), f32),
                pltpu.VMEM((32, NP), jnp.bfloat16),
                pltpu.VMEM((NP, 128), jnp.bfloat16),
                pltpu.VMEM((2, 384, 640), jnp.bfloat16),
                pltpu.VMEM((2 * BLOCKS, 3, 8, 128), f32),
                pltpu.SemaphoreType.DMA((4,)),
                pltpu.VMEM((SLICES, 3, 8, 128), f32),
                pltpu.VMEM((2, 3, NP + 2 * PAD, 128), f32),
                pltpu.VMEM((2, NVAR + 1, AXIAL // 2, 8, 128), f32),
                pltpu.VMEM((2, NVAR + 1, AXIAL // 2, 8, 128), f32),
                pltpu.VMEM((2, 2, NP, 128), f32),
                pltpu.VMEM((2, 3, NP + 2 * PAD, 128), f32),
                pltpu.VMEM((2, 2, NP + 2 * PAD, 128), f32),
                pltpu.VMEM((2, NP + 2 * PAD, 128), f32),
                pltpu.VMEM((SECTIONS, 2, NP + WRAP, 128), f32),
                pltpu.VMEM((2, 3, NP, 128), f32),
                pltpu.VMEM((SLICES, 3, 8, 128), f32),
                pltpu.VMEM((SECTIONS, NVAR, AXIAL, 16, 128), f32),
                pltpu.VMEM((AXIAL, 16, 128), f32),
                pltpu.VMEM((SECTIONS, NVAR, 16, 128), f32),
                pltpu.SemaphoreType.DMA,
                pltpu.SemaphoreType.DMA,
                pltpu.SemaphoreType.REGULAR,
                pltpu.SemaphoreType.DMA((2,)),
                pltpu.SemaphoreType.DMA((2,)),
                pltpu.SemaphoreType.DMA,
                pltpu.SemaphoreType.DMA,
            ],
            compiler_params=pltpu.CompilerParams(
                collective_id=0, has_side_effects=True, vmem_limit_bytes=63 << 20
            ),
            name="sections",
        )(state[0], visc[0], jnp.transpose(coup, (1, 0, 2)), offs, live, jnp.asarray(weighted), jnp.asarray(plain))
        return done[None]

    in_specs = (
        P("row", None, None, "blk", None),
        P("row", None, "blk", None),
        P("row", None, None),
        P(),
        P("row"),
    )
    out_specs = P("row", None, None, "blk", None)
    return jax.shard_map(body, mesh=mesh, in_specs=in_specs, out_specs=out_specs, check_vma=False)
```

```python
import functools
import math

import jax
import jax.numpy as jnp
import numpy as np
from jax import lax
from jax.experimental import pallas as pl
from jax.experimental.pallas import tpu as pltpu
from jax.sharding import PartitionSpec as P

MESH = pl.DeviceIdType.MESH
MODES = 5
SECTIONS = 4
NVAR = 5
AXIAL = 16
PITCH = 8
SPAN = 128
BLOCKS = 64
NP = BLOCKS * PITCH
SLICES = 16
CHUNK = 512
WRAP = 512
PAD = 8

section_alphas = (0.25, 1.0 / 3.0, 0.5, 1.0)
time_step = 0.25
speed_axial = 1.0
speed_pitch = 0.6
speed_span = 0.3

def split(value):
    high = value.astype(jnp.bfloat16)
    return high, (value - high.astype(jnp.float32)).astype(jnp.bfloat16)


def basis_tables():
    theta = np.arange(NP) * (2.0 * math.pi / NP)
    rows = [np.ones(NP)]
    rows += [np.cos(j * theta) for j in range(1, MODES + 1)]
    rows += [np.sin(j * theta) for j in range(1, MODES + 1)]
    table = np.zeros((16, NP), np.float32)
    table[: 2 * MODES + 1] = np.stack(rows)
    weights = np.full((16, 1), 2.0 / NP, np.float32)
    weights[0] = 1.0 / NP

    def parts(value):
        high = value.astype(jnp.bfloat16)
        return high, (value - high.astype(np.float32)).astype(jnp.bfloat16)

    back = np.zeros((NP, 128), jnp.bfloat16)
    high, low = parts(np.ascontiguousarray(table.T))
    back[:, 0:16], back[:, 16:32], back[:, 32:48] = high, low, high
    return np.concatenate(parts(table * weights)), back


def worker_of(pair, s):
    plane = 2 * (s // 2) + pair % 2
    return 2 * pair + (s // 2) % 2, 4 * plane + 2 * (s % 2) + 1


def kernel(
    state_hbm, visc_hbm, coup_hbm, offs_hbm, live_hbm, basis_hbm, basis_t_hbm, out,
    state, visc, basis, basis_t, mix, size, coup, offs, live, load_s,
    msg, recv, hs, hr, vb, xa, xb, xc, hb, st, gbuf, fld, vext, gx,
    main_s, main_r, ready, halo_s, halo_r, ret_s, ret_r,
):
    row = lax.axis_index("row")
    blk = lax.axis_index("blk")
    pair, parity = row // 2, row % 2
    z = blk // 4
    own = 2 * (z // 2) + (blk // 2) % 2
    own_row, own_blk = worker_of(pair, own)
    is_worker = jnp.logical_and(own_row == row, own_blk == blk)
    after, before = (blk + 1) % BLOCKS, (blk + BLOCKS - 1) % BLOCKS

    many = size.at[pl.ds(0, 2 * BLOCKS - 1)]

    bar = pltpu.get_barrier_semaphore()

    def greet(r, b):
        pl.semaphore_signal(bar, inc=1, device_id=(r, b), device_id_type=MESH)

    @pl.when(is_worker)
    def _():
        def greet_source(i, c):
            at = (blk + BLOCKS // 2 + jnp.where(i % 2 == 1, (i + 1) // 2, BLOCKS - i // 2)) % BLOCKS
            greet(row ^ 1, at)

            @pl.when(at != blk)
            def _():
                greet(row, at)

            return c

        lax.fori_loop(0, BLOCKS, greet_source, 0)

    greet(row, after)

    loads = [
        pltpu.make_async_copy(source, target, load_s.at[i])
        for i, (source, target) in enumerate(
            [
                (state_hbm, state), (visc_hbm, visc), (basis_hbm, basis), (basis_t_hbm, basis_t),
                (coup_hbm, coup), (offs_hbm, offs), (live_hbm, live),
            ]
        )
    ]
    for load in loads:
        load.start()

    for load in loads:
        load.wait()

    lane8 = lax.broadcasted_iota(jnp.int32, (8, 128), 1)
    slot8 = lane8 // 16
    top = AXIAL - 1
    tiles = (
        [(v, top) for v in range(NVAR)] + [(-1, top), (-1, top - 1), (-1, top - 2)],
        [(v, top - 1) for v in range(NVAR)] + [(0, top - 3), (1, top - 3), (2, top - 3)],
        [(v, top - 2) for v in range(NVAR)] + [(3, top - 3), (4, top - 3)],
    )
    sub8 = lax.broadcasted_iota(jnp.int32, (8, 128), 0)
    consts = jnp.where(lane8 == 112 + NVAR, live[0].astype(jnp.float32), 0.0)
    for v in range(NVAR):
        for w in range(NVAR):
            here = jnp.logical_and(lane8 == 112 + v, sub8 == (w - v) % 8)
            consts = jnp.where(here, coup[v, 0, w], consts)
    for t, slots in enumerate(tiles):
        values = [visc[a] if v < 0 else state[v, a] for v, a in slots]
        for s in range(SLICES):
            packed = consts if t == 2 else jnp.zeros((8, 128), jnp.float32)
            for q, value in enumerate(values):
                turn = (16 * q - (8 * s - 4)) % 128
                moved = pltpu.roll(value, turn, 1) if turn else value
                packed = jnp.where(slot8 == q, moved, packed)
            msg[s, t] = packed

    def pack_halo(j, c):
        for v in range(NVAR + 1):
            for h in range(2):
                if v < NVAR:
                    low = state[v, 2 * j + h, 0:4]
                    high = state[v, 2 * j + h, 4:8]
                else:
                    low = visc[2 * j + h, 0:4]
                    high = visc[2 * j + h, 4:8]
                hs[0, v, j, 4 * h : 4 * h + 4] = high
                hs[1, v, j, 4 * h : 4 * h + 4] = low
        return c

    lax.fori_loop(0, AXIAL // 2, pack_halo, 0)

    pl.semaphore_wait(bar, SLICES + 1 - jnp.where(is_worker, 1, 0))
    pl.semaphore_signal(ready, inc=1, device_id=(row, before), device_id_type=MESH)

    mine = pl.ds(pl.multiple_of(PAD + PITCH * blk, 8), PITCH)

    def send_main(i, c):
        s = (z + SLICES // 2 + jnp.where(i % 2 == 1, (i + 1) // 2, SLICES - i // 2)) % SLICES
        wr, wb = worker_of(pair, s)
        self = jnp.logical_and(wr == row, wb == blk)

        @pl.when(jnp.logical_not(self))
        def _():
            pltpu.make_async_remote_copy(
                src_ref=msg.at[s],
                dst_ref=recv.at[parity, :, mine],
                send_sem=main_s,
                recv_sem=main_r,
                device_id=(wr, wb),
                device_id_type=MESH,
            ).start()

        return c

    lax.fori_loop(0, SLICES, send_main, 0)

    def wait_bytes(ref, sem):
        pltpu.make_async_copy(ref, ref, sem).wait()

    @pl.when(is_worker)
    def _():
        wait_bytes(msg.at[pl.ds(0, SLICES - 1)], main_s)

    @pl.when(jnp.logical_not(is_worker))
    def _():
        wait_bytes(msg, main_s)

    def halo_copy(side):
        return pltpu.make_async_remote_copy(
            src_ref=hs.at[side],
            dst_ref=hr.at[side],
            send_sem=halo_s.at[side],
            recv_sem=halo_r.at[side],
            device_id=(row, after if side == 0 else before),
            device_id_type=MESH,
        )

    halo_copy(1).start()
    pl.semaphore_wait(ready, 1)
    halo_copy(0).start()

    @pl.when(is_worker)
    def _():
        recv[parity, :, mine] = msg[own]
        source = lax.broadcasted_iota(jnp.int32, (128, 128), 0)
        target = lax.broadcasted_iota(jnp.int32, (128, 128), 1)
        place = 8 * own - 4 + target % 16
        lower = jnp.where(place == 0, target, target - 1)
        upper = jnp.where(place == SPAN - 1, target, target + 1)

        def one(here):
            return jnp.where(here, 1.0, 0.0)

        around = one(source == lower) + one(source == upper) - 6.0 * one(source == target)
        still = speed_span * one(source == lower) - (
            speed_axial + speed_pitch + speed_span
        ) * one(source == target)
        for rho in range(2):
            for half in range(2):
                mix[rho, 128 * half : 128 * half + 128, 128:256] = around.astype(jnp.bfloat16)
                for q in range(3):
                    wide = one(source == 16 * (5 + q) + target % 16).astype(jnp.bfloat16)
                    mix[rho, 128 * half : 128 * half + 128, 256 + 128 * q : 384 + 128 * q] = wide
        wait_bytes(many, main_r)
        alive_to = []
        for rho in range(2):
            given = recv[rho, 2, PAD : PAD + 8]
            table = jnp.zeros((8, 128), jnp.float32)
            for v in range(NVAR):
                column = jnp.broadcast_to(given[:, 112 + v : 113 + v], (8, 128))
                table = jnp.where(slot8 == v, column, table)
            alive_to.append(given[0:1, 112 + NVAR : 113 + NVAR])
            both = still
            for d in range(8):
                both = both + jnp.where(source == (target + 16 * d) % 128, table[d : d + 1], 0.0)
            high, low = split(both)
            for half in range(2):
                mix[rho, 128 * half : 128 * half + 128, 0:128] = high
            mix[rho, 256:384, 0:128] = low
        lane = lax.broadcasted_iota(jnp.int32, (CHUNK, 128), 1)
        slot = lane // 16
        cell = 8 * own - 4 + lane % 16
        cell_f = cell[0:1].astype(jnp.float32)

        def wrap(ref, *index):
            ref[(*index, slice(PAD - 1, PAD))] = ref[(*index, slice(PAD + NP - 1, PAD + NP))]
            ref[(*index, slice(PAD + NP, PAD + NP + 1))] = ref[(*index, slice(PAD, PAD + 1))]

        shifts = []
        for k in range(SECTIONS):
            turn = offs[k, pair]
            shifts.append((turn, (NP - turn) % NP))

        for rho in range(2):
            for t in range(3):
                wrap(recv, rho, t)

        fields = [
            [[(recv, (rho, t)) for t in range(3)] for rho in range(2)],
            [[(xa, (rho, t)) for t in range(3)] for rho in range(2)],
            [[(xb, (rho, t)) for t in range(2)] for rho in range(2)],
            [[(xc, (rho,))] for rho in range(2)],
        ]
        for k in range(SECTIONS):
            strips = []
            for rho in range(2):
                ref, index = fields[k][rho][0]
                strips.append(ref[(*index, slice(PAD, PAD + NP))])
            strips = jnp.concatenate(strips, 1)
            high, low = split(strips)
            sums = jnp.dot(basis[...], high, preferred_element_type=jnp.float32)
            coef = sums[0:16] + sums[16:32]
            coef = coef + jnp.dot(basis[0:16], low, preferred_element_type=jnp.float32)
            high, low = split(coef)
            coefs = jnp.concatenate([high, high, low, jnp.zeros((80, 256), jnp.bfloat16)], 0)
            recon = jnp.dot(basis_t[...], coefs, preferred_element_type=jnp.float32)
            half = 0.5 * (strips + recon)
            for rho in range(2):
                hb[k, rho, 0:NP] = half[:, 128 * rho : 128 * rho + 128]
                hb[k, rho, NP : NP + WRAP] = half[0:WRAP, 128 * rho : 128 * rho + 128]
            if k == SECTIONS - 1:
                break
            factor = section_alphas[k] * time_step
            for rho in range(2):
                scale = jnp.where(cell_f < alive_to[rho], factor, 0.0)

                def update(i, c):
                    at = pl.multiple_of(i * CHUNK, CHUNK)

                    def take(t, move=0):
                        ref, index = fields[k][rho][t]
                        return ref[(*index, pl.ds(PAD + at + move, CHUNK))]

                    inner = [take(t) for t in range(3 - k)]
                    vis = [vb[rho, t, pl.ds(at, CHUNK)] for t in range(3 - k)] if k else None
                    start = (at + shifts[k][rho]) % NP
                    ghost = hb[k, 1 - rho, pl.ds(start, CHUNK)]
                    for t in range(3 - k):
                        here = inner[t]
                        up_axial = ghost if t == 0 else inner[t - 1]
                        if t + 1 < 3 - k:
                            down_axial = inner[t + 1]
                        elif k == 0:
                            two = recv[rho, 1, pl.ds(PAD + at, CHUNK)]
                            three = recv[rho, 2, pl.ds(PAD + at, CHUNK)]
                            down_axial = jnp.where(
                                slot < 3, pltpu.roll(two, 48, 1), pltpu.roll(three, 96, 1)
                            )
                        else:
                            down_axial = take(t + 1)
                        up_pitch, down_pitch = take(t, 1), take(t, -1)
                        high, low = split(here)
                        first = k == 0 and t == 0
                        linear = jnp.dot(
                            jnp.concatenate([high, low], 1),
                            mix[rho, 0:256] if first else mix[rho, 0:256, 0:256],
                            preferred_element_type=jnp.float32,
                        )
                        if first:
                            vis = [linear[:, 256 + 128 * q : 384 + 128 * q] for q in range(3)]
                            for q in range(2):
                                vb[rho, q, pl.ds(at, CHUNK)] = vis[q]
                        low = jnp.dot(high, mix[rho, 256:384, 0:128], preferred_element_type=jnp.float32)
                        beside = up_axial + down_axial + up_pitch + down_pitch + linear[:, 128:256]
                        rate = speed_axial * up_axial + speed_pitch * down_pitch + low
                        rate = rate + linear[:, 0:128] + vis[t] * beside
                        ref, index = fields[k + 1][rho][t]
                        ref[(*index, pl.ds(PAD + at, CHUNK))] = (
                            recv[rho, t, pl.ds(PAD + at, CHUNK)] + scale * rate
                        )
                    return c

                lax.fori_loop(0, NP // CHUNK, update, 0)
                for t in range(3 - k):
                    ref, index = fields[k + 1][rho][t]
                    wrap(ref, *index)

        inside = jnp.logical_and(lane % 16 >= 4, lane % 16 < 12)
        for rho in range(2):

            def pack_back(i, c):
                at = pl.multiple_of(i * CHUNK, CHUNK)
                part = []
                for k in range(SECTIONS):
                    back = 4 if k < 3 else 0
                    start = (at + NP - back + shifts[k][rho]) % NP
                    part.append(hb[k, 1 - rho, pl.ds(start, CHUNK)])
                both = jnp.where(inside, part[0], pltpu.roll(part[1], 8, 1))
                third = jnp.where(inside, pltpu.roll(part[2], 80, 1), pltpu.roll(part[2], 40, 1))
                both = jnp.where(lane < 84, both, third)
                blocks = both.reshape(BLOCKS, PITCH, 128)
                st[rho, :, 0] = blocks
                st[rho, 0 : BLOCKS - 1, 1] = blocks[1:]
                st[rho, BLOCKS - 1, 1] = blocks[0]
                st[rho, :, 2] = part[3].reshape(BLOCKS, PITCH, 128)
                return c

            lax.fori_loop(0, NP // CHUNK, pack_back, 0)

        def send_back(other, at):
            pltpu.make_async_remote_copy(
                src_ref=st.at[other % 2, at],
                dst_ref=gbuf.at[own],
                send_sem=ret_s,
                recv_sem=ret_r,
                device_id=(other, at),
                device_id_type=MESH,
            ).start()

        def send_both(i, c):
            at = (blk + BLOCKS // 2 + jnp.where(i % 2 == 1, (i + 1) // 2, BLOCKS - i // 2)) % BLOCKS
            send_back(row ^ 1, at)
            send_back(row, at)
            return c

        lax.fori_loop(0, BLOCKS - 1, send_both, 0, unroll=3)
        send_back(row ^ 1, blk)
        gbuf[own] = st[parity, blk]

    halo_copy(0).wait_recv()
    halo_copy(1).wait_recv()

    def widen_block(j, c):
        for h in range(2):
            a = 2 * j + h
            part = slice(4 * h, 4 * h + 4)
            for v in range(NVAR):
                fld[0, v, a, 0:4] = hr[0, v, j, part]
                fld[0, v, a, 4:12] = state[v, a]
                fld[0, v, a, 12:16] = hr[1, v, j, part]
            vext[a, 0:4] = hr[0, NVAR, j, part]
            vext[a, 4:12] = visc[a]
            vext[a, 12:16] = hr[1, NVAR, j, part]
        return c

    lax.fori_loop(0, AXIAL // 2, widen_block, 0)

    lane2 = lax.broadcasted_iota(jnp.int32, (16, 128), 1)
    first2, last2 = lane2 == 0, lane2 == SPAN - 1
    alive = lane2 < live[0]
    cs = [[coup[v, 0, w] for w in range(NVAR)] for v in range(NVAR)]

    def layer(k, a, up):
        here = [fld[k, v, a] for v in range(NVAR)]
        vis = vext[a]
        below = jnp.maximum(a - 1, 0)
        scale = jnp.where(alive, section_alphas[k] * time_step, 0.0)
        for v in range(NVAR):
            u = here[v]
            up_axial, down_axial = up(v), fld[k, v, below]
            up_pitch, down_pitch = pltpu.roll(u, 15, 0), pltpu.roll(u, 1, 0)
            up_span = jnp.where(last2, u, pltpu.roll(u, 127, 1))
            down_span = jnp.where(first2, u, pltpu.roll(u, 1, 1))
            rate = (
                speed_axial * (up_axial - u)
                - speed_pitch * (u - down_pitch)
                - speed_span * (u - down_span)
            )
            beside = up_axial + down_axial + up_pitch + down_pitch + up_span + down_span
            rate = rate + vis * (beside - 6.0 * u)
            for w in range(NVAR):
                rate = rate + cs[v][w] * here[w]
            new = fld[0, v, a] + scale * rate
            if k < SECTIONS - 1:
                fld[k + 1, v, a] = new
            else:
                out[v, a] = pltpu.roll(new, 12, 0)[0:8]

    for k in range(SECTIONS):

        def inner_layer(a, c):
            layer(k, a, lambda v: fld[k, v, a + 1])
            return c

        lax.fori_loop(0, AXIAL - 1 - k, inner_layer, 0)

    @pl.when(is_worker)
    def _():
        wait_bytes(gbuf.at[pl.ds(0, SLICES - 1)], ret_r)

    @pl.when(jnp.logical_not(is_worker))
    def _():
        wait_bytes(gbuf, ret_r)

    group8 = lane8 // 8
    for v in range(NVAR):
        places = [16 * v + 4, 16 * v + 12]
        places.append(84 + 16 * v if v < 3 else 92 + 16 * (v - 3))
        for k in range(3):
            for half in range(2):
                value = jnp.zeros((8, 128), jnp.float32)
                for s in range(SLICES):
                    turn = (8 * s - places[k]) % 128
                    value = jnp.where(group8 == s, pltpu.roll(gbuf[s, half], turn, 1), value)
                gx[k, v, 8 * half : 8 * half + 8] = value
        value = jnp.zeros((8, 128), jnp.float32)
        for s in range(SLICES):
            turn = (8 * s - (16 * v + 4)) % 128
            value = jnp.where(group8 == s, pltpu.roll(gbuf[s, 2], turn, 1), value)
        gx[3, v, 0:4] = jnp.zeros((4, 128), jnp.float32)
        gx[3, v, 4:12] = value
        gx[3, v, 12:16] = jnp.zeros((4, 128), jnp.float32)

    for k in range(SECTIONS):
        for a in range(AXIAL - 1 - k, AXIAL - 1):
            layer(k, a, lambda v: fld[k, v, a + 1])
        layer(k, AXIAL - 1, lambda v: gx[k, v])

    halo_copy(0).wait_send()
    halo_copy(1).wait_send()

    @pl.when(is_worker)
    def _():
        wait_bytes(many, ret_s)


def solution(mesh):
    weighted, plain = basis_tables()

    def body(state, visc, coup, offs, live):
        vmem = pl.BlockSpec(memory_space=pltpu.VMEM)
        hbm = pl.BlockSpec(memory_space=pltpu.HBM)
        f32 = jnp.float32
        done = pl.pallas_call(
            kernel,
            out_shape=jax.ShapeDtypeStruct((NVAR, AXIAL, PITCH, SPAN), f32),
            in_specs=[hbm] * 7,
            out_specs=vmem,
            scratch_shapes=[
                pltpu.VMEM((NVAR, AXIAL, PITCH, SPAN), f32),
                pltpu.VMEM((AXIAL, PITCH, SPAN), f32),
                pltpu.VMEM((32, NP), jnp.bfloat16),
                pltpu.VMEM((NP, 128), jnp.bfloat16),
                pltpu.VMEM((2, 384, 640), jnp.bfloat16),
                pltpu.VMEM((2 * BLOCKS, 3, 8, 128), f32),
                pltpu.SMEM((NVAR, 1, NVAR), f32),
                pltpu.SMEM((4, 8), jnp.int32),
                pltpu.SMEM((1,), jnp.int32),
                pltpu.SemaphoreType.DMA((7,)),
                pltpu.VMEM((SLICES, 3, 8, 128), f32),
                pltpu.VMEM((2, 3, NP + 2 * PAD, 128), f32),
                pltpu.VMEM((2, NVAR + 1, AXIAL // 2, 8, 128), f32),
                pltpu.VMEM((2, NVAR + 1, AXIAL // 2, 8, 128), f32),
                pltpu.VMEM((2, 2, NP, 128), f32),
                pltpu.VMEM((2, 3, NP + 2 * PAD, 128), f32),
                pltpu.VMEM((2, 2, NP + 2 * PAD, 128), f32),
                pltpu.VMEM((2, NP + 2 * PAD, 128), f32),
                pltpu.VMEM((SECTIONS, 2, NP + WRAP, 128), f32),
                pltpu.VMEM((2, BLOCKS, 3, 8, 128), f32),
                pltpu.VMEM((SLICES, 3, 8, 128), f32),
                pltpu.VMEM((SECTIONS, NVAR, AXIAL, 16, 128), f32),
                pltpu.VMEM((AXIAL, 16, 128), f32),
                pltpu.VMEM((SECTIONS, NVAR, 16, 128), f32),
                pltpu.SemaphoreType.DMA,
                pltpu.SemaphoreType.DMA,
                pltpu.SemaphoreType.REGULAR,
                pltpu.SemaphoreType.DMA((2,)),
                pltpu.SemaphoreType.DMA((2,)),
                pltpu.SemaphoreType.DMA,
                pltpu.SemaphoreType.DMA,
            ],
            compiler_params=pltpu.CompilerParams(
                collective_id=0, has_side_effects=True, vmem_limit_bytes=63 << 20
            ),
            name="sections",
        )(state[0], visc[0], jnp.transpose(coup, (1, 0, 2)), offs, live, jnp.asarray(weighted), jnp.asarray(plain))
        return done[None]

    in_specs = (
        P("row", None, None, "blk", None),
        P("row", None, "blk", None),
        P("row", None, None),
        P(),
        P("row"),
    )
    out_specs = P("row", None, None, "blk", None)
    return jax.shard_map(body, mesh=mesh, in_specs=in_specs, out_specs=out_specs, check_vma=False)
```

```python
import functools
import math

import jax
import jax.numpy as jnp
import numpy as np
from jax import lax
from jax.experimental import pallas as pl
from jax.experimental.pallas import tpu as pltpu
from jax.sharding import PartitionSpec as P

MESH = pl.DeviceIdType.MESH
MODES = 5
SECTIONS = 4
NVAR = 5
AXIAL = 16
PITCH = 8
SPAN = 128
BLOCKS = 64
NP = BLOCKS * PITCH
SLICES = 16
CHUNK = 512
WRAP = 512
PAD = 8

section_alphas = (0.25, 1.0 / 3.0, 0.5, 1.0)
time_step = 0.25
speed_axial = 1.0
speed_pitch = 0.6
speed_span = 0.3

def split(value):
    high = value.astype(jnp.bfloat16)
    return high, (value - high.astype(jnp.float32)).astype(jnp.bfloat16)


def basis_tables():
    theta = np.arange(NP) * (2.0 * math.pi / NP)
    rows = [np.ones(NP)]
    rows += [np.cos(j * theta) for j in range(1, MODES + 1)]
    rows += [np.sin(j * theta) for j in range(1, MODES + 1)]
    table = np.zeros((16, NP), np.float32)
    table[: 2 * MODES + 1] = np.stack(rows)
    weights = np.full((16, 1), 2.0 / NP, np.float32)
    weights[0] = 1.0 / NP

    def parts(value):
        high = value.astype(jnp.bfloat16)
        return high, (value - high.astype(np.float32)).astype(jnp.bfloat16)

    back = np.zeros((NP, 128), jnp.bfloat16)
    high, low = parts(np.ascontiguousarray(table.T))
    back[:, 0:16], back[:, 16:32], back[:, 32:48] = high, low, high
    return np.concatenate(parts(table * weights)), back


def worker_of(pair, s):
    plane = 2 * (s // 2) + pair % 2
    return 2 * pair + (s // 2) % 2, 4 * plane + 2 * (s % 2) + 1


def kernel(
    state_hbm, visc_hbm, coup_hbm, offs_hbm, live_hbm, basis_hbm, basis_t_hbm, out,
    state, visc, basis, basis_t, mix, size, coup, offs, live, load_s,
    msg, recv, hs, hr, vb, xa, xb, xc, hb, st, gbuf, fld, vext, gx,
    main_s, main_r, ready, halo_s, halo_r, ret_s, ret_r,
):
    row = lax.axis_index("row")
    blk = lax.axis_index("blk")
    pair, parity = row // 2, row % 2
    z = blk // 4
    own = 2 * (z // 2) + (blk // 2) % 2
    own_row, own_blk = worker_of(pair, own)
    is_worker = jnp.logical_and(own_row == row, own_blk == blk)
    after, before = (blk + 1) % BLOCKS, (blk + BLOCKS - 1) % BLOCKS

    many = size.at[pl.ds(0, 2 * BLOCKS - 1)]

    bar = pltpu.get_barrier_semaphore()

    def greet(r, b):
        pl.semaphore_signal(bar, inc=1, device_id=(r, b), device_id_type=MESH)

    @pl.when(is_worker)
    def _():
        def greet_source(i, c):
            at = (blk + BLOCKS // 2 + jnp.where(i % 2 == 1, (i + 1) // 2, BLOCKS - i // 2)) % BLOCKS
            greet(row ^ 1, at)

            @pl.when(at != blk)
            def _():
                greet(row, at)

            return c

        lax.fori_loop(0, BLOCKS, greet_source, 0)

    greet(row, after)

    loads = [
        pltpu.make_async_copy(source, target, load_s.at[i])
        for i, (source, target) in enumerate(
            [
                (state_hbm, state), (visc_hbm, visc), (basis_hbm, basis), (basis_t_hbm, basis_t),
                (coup_hbm, coup), (offs_hbm, offs), (live_hbm, live),
            ]
        )
    ]
    for load in loads:
        load.start()

    for load in loads:
        load.wait()

    lane8 = lax.broadcasted_iota(jnp.int32, (8, 128), 1)
    slot8 = lane8 // 16
    top = AXIAL - 1
    tiles = (
        [(v, top) for v in range(NVAR)] + [(-1, top), (-1, top - 1), (-1, top - 2)],
        [(v, top - 1) for v in range(NVAR)] + [(0, top - 3), (1, top - 3), (2, top - 3)],
        [(v, top - 2) for v in range(NVAR)] + [(3, top - 3), (4, top - 3)],
    )
    sub8 = lax.broadcasted_iota(jnp.int32, (8, 128), 0)
    consts = jnp.where(lane8 == 112 + NVAR, live[0].astype(jnp.float32), 0.0)
    for v in range(NVAR):
        for w in range(NVAR):
            here = jnp.logical_and(lane8 == 112 + v, sub8 == (w - v) % 8)
            consts = jnp.where(here, coup[v, 0, w], consts)
    for t, slots in enumerate(tiles):
        values = [visc[a] if v < 0 else state[v, a] for v, a in slots]
        for s in range(SLICES):
            packed = consts if t == 2 else jnp.zeros((8, 128), jnp.float32)
            for q, value in enumerate(values):
                turn = (16 * q - (8 * s - 4)) % 128
                moved = pltpu.roll(value, turn, 1) if turn else value
                packed = jnp.where(slot8 == q, moved, packed)
            msg[s, t] = packed

    def pack_halo(j, c):
        for v in range(NVAR + 1):
            for h in range(2):
                if v < NVAR:
                    low = state[v, 2 * j + h, 0:4]
                    high = state[v, 2 * j + h, 4:8]
                else:
                    low = visc[2 * j + h, 0:4]
                    high = visc[2 * j + h, 4:8]
                hs[0, v, j, 4 * h : 4 * h + 4] = high
                hs[1, v, j, 4 * h : 4 * h + 4] = low
        return c

    lax.fori_loop(0, AXIAL // 2, pack_halo, 0)

    pl.semaphore_wait(bar, SLICES + 1 - jnp.where(is_worker, 1, 0))
    pl.semaphore_signal(ready, inc=1, device_id=(row, before), device_id_type=MESH)

    mine = pl.ds(pl.multiple_of(PAD + PITCH * blk, 8), PITCH)

    def send_main(i, c):
        s = (z + SLICES // 2 + jnp.where(i % 2 == 1, (i + 1) // 2, SLICES - i // 2)) % SLICES
        wr, wb = worker_of(pair, s)
        self = jnp.logical_and(wr == row, wb == blk)

        @pl.when(jnp.logical_not(self))
        def _():
            pltpu.make_async_remote_copy(
                src_ref=msg.at[s],
                dst_ref=recv.at[parity, :, mine],
                send_sem=main_s,
                recv_sem=main_r,
                device_id=(wr, wb),
                device_id_type=MESH,
            ).start()

        return c

    lax.fori_loop(0, SLICES, send_main, 0)

    def wait_bytes(ref, sem):
        pltpu.make_async_copy(ref, ref, sem).wait()

    @pl.when(is_worker)
    def _():
        wait_bytes(msg.at[pl.ds(0, SLICES - 1)], main_s)

    @pl.when(jnp.logical_not(is_worker))
    def _():
        wait_bytes(msg, main_s)

    def halo_copy(side):
        return pltpu.make_async_remote_copy(
            src_ref=hs.at[side],
            dst_ref=hr.at[side],
            send_sem=halo_s.at[side],
            recv_sem=halo_r.at[side],
            device_id=(row, after if side == 0 else before),
            device_id_type=MESH,
        )

    halo_copy(1).start()
    pl.semaphore_wait(ready, 1)
    halo_copy(0).start()

    @pl.when(is_worker)
    def _():
        recv[parity, :, mine] = msg[own]
        source = lax.broadcasted_iota(jnp.int32, (128, 128), 0)
        target = lax.broadcasted_iota(jnp.int32, (128, 128), 1)
        place = 8 * own - 4 + target % 16
        lower = jnp.where(place == 0, target, target - 1)
        upper = jnp.where(place == SPAN - 1, target, target + 1)

        def one(here):
            return jnp.where(here, 1.0, 0.0)

        around = one(source == lower) + one(source == upper) - 6.0 * one(source == target)
        still = speed_span * one(source == lower) - (
            speed_axial + speed_pitch + speed_span
        ) * one(source == target)
        for rho in range(2):
            for half in range(2):
                mix[rho, 128 * half : 128 * half + 128, 128:256] = around.astype(jnp.bfloat16)
                for q in range(3):
                    wide = one(source == 16 * (5 + q) + target % 16).astype(jnp.bfloat16)
                    mix[rho, 128 * half : 128 * half + 128, 256 + 128 * q : 384 + 128 * q] = wide
        wait_bytes(many, main_r)
        alive_to = []
        for rho in range(2):
            given = recv[rho, 2, PAD : PAD + 8]
            table = jnp.zeros((8, 128), jnp.float32)
            for v in range(NVAR):
                column = jnp.broadcast_to(given[:, 112 + v : 113 + v], (8, 128))
                table = jnp.where(slot8 == v, column, table)
            alive_to.append(given[0:1, 112 + NVAR : 113 + NVAR])
            both = still
            for d in range(8):
                both = both + jnp.where(source == (target + 16 * d) % 128, table[d : d + 1], 0.0)
            high, low = split(both)
            for half in range(2):
                mix[rho, 128 * half : 128 * half + 128, 0:128] = high
            mix[rho, 256:384, 0:128] = low
        lane = lax.broadcasted_iota(jnp.int32, (CHUNK, 128), 1)
        slot = lane // 16
        cell = 8 * own - 4 + lane % 16
        cell_f = cell[0:1].astype(jnp.float32)

        def wrap(ref, *index):
            ref[(*index, slice(PAD - 1, PAD))] = ref[(*index, slice(PAD + NP - 1, PAD + NP))]
            ref[(*index, slice(PAD + NP, PAD + NP + 1))] = ref[(*index, slice(PAD, PAD + 1))]

        shifts = []
        for k in range(SECTIONS):
            turn = offs[k, pair]
            shifts.append((turn, (NP - turn) % NP))

        for rho in range(2):
            for t in range(3):
                wrap(recv, rho, t)

        fields = [
            [[(recv, (rho, t)) for t in range(3)] for rho in range(2)],
            [[(xa, (rho, t)) for t in range(3)] for rho in range(2)],
            [[(xb, (rho, t)) for t in range(2)] for rho in range(2)],
            [[(xc, (rho,))] for rho in range(2)],
        ]
        for k in range(SECTIONS):
            strips = []
            for rho in range(2):
                ref, index = fields[k][rho][0]
                strips.append(ref[(*index, slice(PAD, PAD + NP))])
            strips = jnp.concatenate(strips, 1)
            high, low = split(strips)
            sums = jnp.dot(basis[...], high, preferred_element_type=jnp.float32)
            coef = sums[0:16] + sums[16:32]
            coef = coef + jnp.dot(basis[0:16], low, preferred_element_type=jnp.float32)
            high, low = split(coef)
            coefs = jnp.concatenate([high, high, low, jnp.zeros((80, 256), jnp.bfloat16)], 0)
            recon = jnp.dot(basis_t[...], coefs, preferred_element_type=jnp.float32)
            half = 0.5 * (strips + recon)
            for rho in range(2):
                hb[k, rho, 0:NP] = half[:, 128 * rho : 128 * rho + 128]
                hb[k, rho, NP : NP + WRAP] = half[0:WRAP, 128 * rho : 128 * rho + 128]
            if k == SECTIONS - 1:
                break
            factor = section_alphas[k] * time_step
            for rho in range(2):
                scale = jnp.where(cell_f < alive_to[rho], factor, 0.0)

                def update(i, c):
                    at = pl.multiple_of(i * CHUNK, CHUNK)

                    def take(t, move=0):
                        ref, index = fields[k][rho][t]
                        return ref[(*index, pl.ds(PAD + at + move, CHUNK))]

                    inner = [take(t) for t in range(3 - k)]
                    vis = [vb[rho, t, pl.ds(at, CHUNK)] for t in range(3 - k)] if k else None
                    start = (at + shifts[k][rho]) % NP
                    ghost = hb[k, 1 - rho, pl.ds(start, CHUNK)]
                    for t in range(3 - k):
                        here = inner[t]
                        up_axial = ghost if t == 0 else inner[t - 1]
                        if t + 1 < 3 - k:
                            down_axial = inner[t + 1]
                        elif k == 0:
                            two = recv[rho, 1, pl.ds(PAD + at, CHUNK)]
                            three = recv[rho, 2, pl.ds(PAD + at, CHUNK)]
                            down_axial = jnp.where(
                                slot < 3, pltpu.roll(two, 48, 1), pltpu.roll(three, 96, 1)
                            )
                        else:
                            down_axial = take(t + 1)
                        up_pitch, down_pitch = take(t, 1), take(t, -1)
                        high, low = split(here)
                        first = k == 0 and t == 0
                        linear = jnp.dot(
                            jnp.concatenate([high, low], 1),
                            mix[rho, 0:256] if first else mix[rho, 0:256, 0:256],
                            preferred_element_type=jnp.float32,
                        )
                        if first:
                            vis = [linear[:, 256 + 128 * q : 384 + 128 * q] for q in range(3)]
                            for q in range(2):
                                vb[rho, q, pl.ds(at, CHUNK)] = vis[q]
                        low = jnp.dot(high, mix[rho, 256:384, 0:128], preferred_element_type=jnp.float32)
                        beside = up_axial + down_axial + up_pitch + down_pitch + linear[:, 128:256]
                        rate = speed_axial * up_axial + speed_pitch * down_pitch + low
                        rate = rate + linear[:, 0:128] + vis[t] * beside
                        ref, index = fields[k + 1][rho][t]
                        ref[(*index, pl.ds(PAD + at, CHUNK))] = (
                            recv[rho, t, pl.ds(PAD + at, CHUNK)] + scale * rate
                        )
                    return c

                lax.fori_loop(0, NP // CHUNK, update, 0)
                for t in range(3 - k):
                    ref, index = fields[k + 1][rho][t]
                    wrap(ref, *index)

        inside = jnp.logical_and(lane % 16 >= 4, lane % 16 < 12)
        for rho in range(2):

            def pack_back(i, c):
                at = pl.multiple_of(i * CHUNK, CHUNK)
                part = []
                for k in range(SECTIONS):
                    back = 4 if k < 3 else 0
                    start = (at + NP - back + shifts[k][rho]) % NP
                    part.append(hb[k, 1 - rho, pl.ds(start, CHUNK)])
                both = jnp.where(inside, part[0], pltpu.roll(part[1], 8, 1))
                third = jnp.where(inside, pltpu.roll(part[2], 80, 1), pltpu.roll(part[2], 40, 1))
                both = jnp.where(lane < 84, both, third)
                blocks = both.reshape(BLOCKS, PITCH, 128)
                st[rho, :, 0] = blocks
                st[rho, 0 : BLOCKS - 1, 1] = blocks[1:]
                st[rho, BLOCKS - 1, 1] = blocks[0]
                st[rho, :, 2] = part[3].reshape(BLOCKS, PITCH, 128)
                return c

            lax.fori_loop(0, NP // CHUNK, pack_back, 0)

        def send_back(other, at):
            pltpu.make_async_remote_copy(
                src_ref=st.at[other % 2, at],
                dst_ref=gbuf.at[own],
                send_sem=ret_s,
                recv_sem=ret_r,
                device_id=(other, at),
                device_id_type=MESH,
            ).start()

        def send_both(i, c):
            send_back(row ^ 1, i)
            send_back(row, i + jnp.where(i >= blk, 1, 0))
            return c

        lax.fori_loop(0, BLOCKS - 1, send_both, 0, unroll=3)
        send_back(row ^ 1, BLOCKS - 1)
        gbuf[own] = st[parity, blk]

    halo_copy(0).wait_recv()
    halo_copy(1).wait_recv()

    def widen_block(j, c):
        for h in range(2):
            a = 2 * j + h
            part = slice(4 * h, 4 * h + 4)
            for v in range(NVAR):
                fld[0, v, a, 0:4] = hr[0, v, j, part]
                fld[0, v, a, 4:12] = state[v, a]
                fld[0, v, a, 12:16] = hr[1, v, j, part]
            vext[a, 0:4] = hr[0, NVAR, j, part]
            vext[a, 4:12] = visc[a]
            vext[a, 12:16] = hr[1, NVAR, j, part]
        return c

    lax.fori_loop(0, AXIAL // 2, widen_block, 0)

    lane2 = lax.broadcasted_iota(jnp.int32, (16, 128), 1)
    first2, last2 = lane2 == 0, lane2 == SPAN - 1
    alive = lane2 < live[0]
    cs = [[coup[v, 0, w] for w in range(NVAR)] for v in range(NVAR)]

    def layer(k, a, up):
        here = [fld[k, v, a] for v in range(NVAR)]
        vis = vext[a]
        below = jnp.maximum(a - 1, 0)
        scale = jnp.where(alive, section_alphas[k] * time_step, 0.0)
        for v in range(NVAR):
            u = here[v]
            up_axial, down_axial = up(v), fld[k, v, below]
            up_pitch, down_pitch = pltpu.roll(u, 15, 0), pltpu.roll(u, 1, 0)
            up_span = jnp.where(last2, u, pltpu.roll(u, 127, 1))
            down_span = jnp.where(first2, u, pltpu.roll(u, 1, 1))
            rate = (
                speed_axial * (up_axial - u)
                - speed_pitch * (u - down_pitch)
                - speed_span * (u - down_span)
            )
            beside = up_axial + down_axial + up_pitch + down_pitch + up_span + down_span
            rate = rate + vis * (beside - 6.0 * u)
            for w in range(NVAR):
                rate = rate + cs[v][w] * here[w]
            new = fld[0, v, a] + scale * rate
            if k < SECTIONS - 1:
                fld[k + 1, v, a] = new
            else:
                out[v, a] = pltpu.roll(new, 12, 0)[0:8]

    for k in range(SECTIONS):

        def inner_layer(a, c):
            layer(k, a, lambda v: fld[k, v, a + 1])
            return c

        lax.fori_loop(0, AXIAL - 1 - k, inner_layer, 0)

    @pl.when(is_worker)
    def _():
        wait_bytes(gbuf.at[pl.ds(0, SLICES - 1)], ret_r)

    @pl.when(jnp.logical_not(is_worker))
    def _():
        wait_bytes(gbuf, ret_r)

    group8 = lane8 // 8
    for v in range(NVAR):
        places = [16 * v + 4, 16 * v + 12]
        places.append(84 + 16 * v if v < 3 else 92 + 16 * (v - 3))
        for k in range(3):
            for half in range(2):
                value = jnp.zeros((8, 128), jnp.float32)
                for s in range(SLICES):
                    turn = (8 * s - places[k]) % 128
                    value = jnp.where(group8 == s, pltpu.roll(gbuf[s, half], turn, 1), value)
                gx[k, v, 8 * half : 8 * half + 8] = value
        value = jnp.zeros((8, 128), jnp.float32)
        for s in range(SLICES):
            turn = (8 * s - (16 * v + 4)) % 128
            value = jnp.where(group8 == s, pltpu.roll(gbuf[s, 2], turn, 1), value)
        gx[3, v, 0:4] = jnp.zeros((4, 128), jnp.float32)
        gx[3, v, 4:12] = value
        gx[3, v, 12:16] = jnp.zeros((4, 128), jnp.float32)

    for k in range(SECTIONS):
        for a in range(AXIAL - 1 - k, AXIAL - 1):
            layer(k, a, lambda v: fld[k, v, a + 1])
        layer(k, AXIAL - 1, lambda v: gx[k, v])

    halo_copy(0).wait_send()
    halo_copy(1).wait_send()

    @pl.when(is_worker)
    def _():
        wait_bytes(many, ret_s)


def solution(mesh):
    weighted, plain = basis_tables()

    def body(state, visc, coup, offs, live):
        vmem = pl.BlockSpec(memory_space=pltpu.VMEM)
        hbm = pl.BlockSpec(memory_space=pltpu.HBM)
        f32 = jnp.float32
        done = pl.pallas_call(
            kernel,
            out_shape=jax.ShapeDtypeStruct((NVAR, AXIAL, PITCH, SPAN), f32),
            in_specs=[hbm] * 7,
            out_specs=vmem,
            scratch_shapes=[
                pltpu.VMEM((NVAR, AXIAL, PITCH, SPAN), f32),
                pltpu.VMEM((AXIAL, PITCH, SPAN), f32),
                pltpu.VMEM((32, NP), jnp.bfloat16),
                pltpu.VMEM((NP, 128), jnp.bfloat16),
                pltpu.VMEM((2, 384, 640), jnp.bfloat16),
                pltpu.VMEM((2 * BLOCKS, 3, 8, 128), f32),
                pltpu.SMEM((NVAR, 1, NVAR), f32),
                pltpu.SMEM((4, 8), jnp.int32),
                pltpu.SMEM((1,), jnp.int32),
                pltpu.SemaphoreType.DMA((7,)),
                pltpu.VMEM((SLICES, 3, 8, 128), f32),
                pltpu.VMEM((2, 3, NP + 2 * PAD, 128), f32),
                pltpu.VMEM((2, NVAR + 1, AXIAL // 2, 8, 128), f32),
                pltpu.VMEM((2, NVAR + 1, AXIAL // 2, 8, 128), f32),
                pltpu.VMEM((2, 2, NP, 128), f32),
                pltpu.VMEM((2, 3, NP + 2 * PAD, 128), f32),
                pltpu.VMEM((2, 2, NP + 2 * PAD, 128), f32),
                pltpu.VMEM((2, NP + 2 * PAD, 128), f32),
                pltpu.VMEM((SECTIONS, 2, NP + WRAP, 128), f32),
                pltpu.VMEM((2, BLOCKS, 3, 8, 128), f32),
                pltpu.VMEM((SLICES, 3, 8, 128), f32),
                pltpu.VMEM((SECTIONS, NVAR, AXIAL, 16, 128), f32),
                pltpu.VMEM((AXIAL, 16, 128), f32),
                pltpu.VMEM((SECTIONS, NVAR, 16, 128), f32),
                pltpu.SemaphoreType.DMA,
                pltpu.SemaphoreType.DMA,
                pltpu.SemaphoreType.REGULAR,
                pltpu.SemaphoreType.DMA((2,)),
                pltpu.SemaphoreType.DMA((2,)),
                pltpu.SemaphoreType.DMA,
                pltpu.SemaphoreType.DMA,
            ],
            compiler_params=pltpu.CompilerParams(
                collective_id=0, has_side_effects=True, vmem_limit_bytes=63 << 20
            ),
            name="sections",
        )(state[0], visc[0], jnp.transpose(coup, (1, 0, 2)), offs, live, jnp.asarray(weighted), jnp.asarray(plain))
        return done[None]

    in_specs = (
        P("row", None, None, "blk", None),
        P("row", None, "blk", None),
        P("row", None, None),
        P(),
        P("row"),
    )
    out_specs = P("row", None, None, "blk", None)
    return jax.shard_map(body, mesh=mesh, in_specs=in_specs, out_specs=out_specs, check_vma=False)
```

```python
import functools
import math

import jax
import jax.numpy as jnp
import numpy as np
from jax import lax
from jax.experimental import pallas as pl
from jax.experimental.pallas import tpu as pltpu
from jax.sharding import PartitionSpec as P

MESH = pl.DeviceIdType.MESH
MODES = 5
SECTIONS = 4
NVAR = 5
AXIAL = 16
PITCH = 8
SPAN = 128
BLOCKS = 64
NP = BLOCKS * PITCH
SLICES = 16
CHUNK = 512
WRAP = 512
PAD = 8

section_alphas = (0.25, 1.0 / 3.0, 0.5, 1.0)
time_step = 0.25
speed_axial = 1.0
speed_pitch = 0.6
speed_span = 0.3

def split(value):
    high = value.astype(jnp.bfloat16)
    return high, (value - high.astype(jnp.float32)).astype(jnp.bfloat16)


def basis_tables():
    theta = np.arange(NP) * (2.0 * math.pi / NP)
    rows = [np.ones(NP)]
    rows += [np.cos(j * theta) for j in range(1, MODES + 1)]
    rows += [np.sin(j * theta) for j in range(1, MODES + 1)]
    table = np.zeros((16, NP), np.float32)
    table[: 2 * MODES + 1] = np.stack(rows)
    weights = np.full((16, 1), 2.0 / NP, np.float32)
    weights[0] = 1.0 / NP

    def parts(value):
        high = value.astype(jnp.bfloat16)
        return high, (value - high.astype(np.float32)).astype(jnp.bfloat16)

    back = np.zeros((NP, 128), jnp.bfloat16)
    high, low = parts(np.ascontiguousarray(table.T))
    back[:, 0:16], back[:, 16:32], back[:, 32:48] = high, low, high
    return np.concatenate(parts(table * weights)), back


def worker_of(pair, s):
    plane = s // 2
    return 2 * pair + (plane + pair) % 2, 4 * plane + 2 * (s % 2) + 1


def kernel(
    state_hbm, visc_hbm, coup_hbm, offs_hbm, live_hbm, basis_hbm, basis_t_hbm, out,
    state, visc, basis, basis_t, mix, size, coup, offs, live, load_s,
    msg, recv, hs, hr, vb, xa, xb, xc, hb, st, gbuf, fld, vext, gx,
    main_s, main_r, ready, halo_s, halo_r, ret_s, ret_r,
):
    row = lax.axis_index("row")
    blk = lax.axis_index("blk")
    pair, parity = row // 2, row % 2
    z = blk // 4
    own = 2 * (z % (SLICES // 2)) + (blk // 2) % 2
    own_row, own_blk = worker_of(pair, own)
    is_worker = jnp.logical_and(own_row == row, own_blk == blk)
    after, before = (blk + 1) % BLOCKS, (blk + BLOCKS - 1) % BLOCKS

    many = size.at[pl.ds(0, 2 * BLOCKS - 1)]

    bar = pltpu.get_barrier_semaphore()

    def greet(r, b):
        pl.semaphore_signal(bar, inc=1, device_id=(r, b), device_id_type=MESH)

    @pl.when(is_worker)
    def _():
        def greet_source(i, c):
            at = (blk + BLOCKS // 2 + jnp.where(i % 2 == 1, (i + 1) // 2, BLOCKS - i // 2)) % BLOCKS
            greet(row ^ 1, at)

            @pl.when(at != blk)
            def _():
                greet(row, at)

            return c

        lax.fori_loop(0, BLOCKS, greet_source, 0)

    greet(row, after)

    loads = [
        pltpu.make_async_copy(source, target, load_s.at[i])
        for i, (source, target) in enumerate(
            [
                (state_hbm, state), (visc_hbm, visc), (basis_hbm, basis), (basis_t_hbm, basis_t),
                (coup_hbm, coup), (offs_hbm, offs), (live_hbm, live),
            ]
        )
    ]
    for load in loads:
        load.start()

    for load in loads:
        load.wait()

    lane8 = lax.broadcasted_iota(jnp.int32, (8, 128), 1)
    slot8 = lane8 // 16
    top = AXIAL - 1
    tiles = (
        [(v, top) for v in range(NVAR)] + [(-1, top), (-1, top - 1), (-1, top - 2)],
        [(v, top - 1) for v in range(NVAR)] + [(0, top - 3), (1, top - 3), (2, top - 3)],
        [(v, top - 2) for v in range(NVAR)] + [(3, top - 3), (4, top - 3)],
    )
    sub8 = lax.broadcasted_iota(jnp.int32, (8, 128), 0)
    consts = jnp.where(lane8 == 112 + NVAR, live[0].astype(jnp.float32), 0.0)
    for v in range(NVAR):
        for w in range(NVAR):
            here = jnp.logical_and(lane8 == 112 + v, sub8 == (w - v) % 8)
            consts = jnp.where(here, coup[v, 0, w], consts)
    for t, slots in enumerate(tiles):
        values = [visc[a] if v < 0 else state[v, a] for v, a in slots]
        for s in range(SLICES):
            packed = consts if t == 2 else jnp.zeros((8, 128), jnp.float32)
            for q, value in enumerate(values):
                turn = (16 * q - (8 * s - 4)) % 128
                moved = pltpu.roll(value, turn, 1) if turn else value
                packed = jnp.where(slot8 == q, moved, packed)
            msg[s, t] = packed

    def pack_halo(j, c):
        for v in range(NVAR + 1):
            for h in range(2):
                if v < NVAR:
                    low = state[v, 2 * j + h, 0:4]
                    high = state[v, 2 * j + h, 4:8]
                else:
                    low = visc[2 * j + h, 0:4]
                    high = visc[2 * j + h, 4:8]
                hs[0, v, j, 4 * h : 4 * h + 4] = high
                hs[1, v, j, 4 * h : 4 * h + 4] = low
        return c

    lax.fori_loop(0, AXIAL // 2, pack_halo, 0)

    pl.semaphore_wait(bar, SLICES + 1 - jnp.where(is_worker, 1, 0))
    pl.semaphore_signal(ready, inc=1, device_id=(row, before), device_id_type=MESH)

    mine = pl.ds(pl.multiple_of(PAD + PITCH * blk, 8), PITCH)

    def send_main(i, c):
        s = (2 * z + SLICES // 2 + jnp.where(i % 2 == 1, (i + 1) // 2, SLICES - i // 2)) % SLICES
        wr, wb = worker_of(pair, s)
        self = jnp.logical_and(wr == row, wb == blk)

        @pl.when(jnp.logical_not(self))
        def _():
            pltpu.make_async_remote_copy(
                src_ref=msg.at[s],
                dst_ref=recv.at[parity, :, mine],
                send_sem=main_s,
                recv_sem=main_r,
                device_id=(wr, wb),
                device_id_type=MESH,
            ).start()

        return c

    lax.fori_loop(0, SLICES, send_main, 0)

    def wait_bytes(ref, sem):
        pltpu.make_async_copy(ref, ref, sem).wait()

    @pl.when(is_worker)
    def _():
        wait_bytes(msg.at[pl.ds(0, SLICES - 1)], main_s)

    @pl.when(jnp.logical_not(is_worker))
    def _():
        wait_bytes(msg, main_s)

    def halo_copy(side):
        return pltpu.make_async_remote_copy(
            src_ref=hs.at[side],
            dst_ref=hr.at[side],
            send_sem=halo_s.at[side],
            recv_sem=halo_r.at[side],
            device_id=(row, after if side == 0 else before),
            device_id_type=MESH,
        )

    halo_copy(1).start()
    pl.semaphore_wait(ready, 1)
    halo_copy(0).start()

    @pl.when(is_worker)
    def _():
        recv[parity, :, mine] = msg[own]
        source = lax.broadcasted_iota(jnp.int32, (128, 128), 0)
        target = lax.broadcasted_iota(jnp.int32, (128, 128), 1)
        place = 8 * own - 4 + target % 16
        lower = jnp.where(place == 0, target, target - 1)
        upper = jnp.where(place == SPAN - 1, target, target + 1)

        def one(here):
            return jnp.where(here, 1.0, 0.0)

        around = one(source == lower) + one(source == upper) - 6.0 * one(source == target)
        still = speed_span * one(source == lower) - (
            speed_axial + speed_pitch + speed_span
        ) * one(source == target)
        for rho in range(2):
            for half in range(2):
                mix[rho, 128 * half : 128 * half + 128, 128:256] = around.astype(jnp.bfloat16)
                for q in range(3):
                    wide = one(source == 16 * (5 + q) + target % 16).astype(jnp.bfloat16)
                    mix[rho, 128 * half : 128 * half + 128, 256 + 128 * q : 384 + 128 * q] = wide
        wait_bytes(many, main_r)
        alive_to = []
        for rho in range(2):
            given = recv[rho, 2, PAD : PAD + 8]
            table = jnp.zeros((8, 128), jnp.float32)
            for v in range(NVAR):
                column = jnp.broadcast_to(given[:, 112 + v : 113 + v], (8, 128))
                table = jnp.where(slot8 == v, column, table)
            alive_to.append(given[0:1, 112 + NVAR : 113 + NVAR])
            both = still
            for d in range(8):
                both = both + jnp.where(source == (target + 16 * d) % 128, table[d : d + 1], 0.0)
            high, low = split(both)
            for half in range(2):
                mix[rho, 128 * half : 128 * half + 128, 0:128] = high
            mix[rho, 256:384, 0:128] = low
        lane = lax.broadcasted_iota(jnp.int32, (CHUNK, 128), 1)
        slot = lane // 16
        cell = 8 * own - 4 + lane % 16
        cell_f = cell[0:1].astype(jnp.float32)

        def wrap(ref, *index):
            ref[(*index, slice(PAD - 1, PAD))] = ref[(*index, slice(PAD + NP - 1, PAD + NP))]
            ref[(*index, slice(PAD + NP, PAD + NP + 1))] = ref[(*index, slice(PAD, PAD + 1))]

        shifts = []
        for k in range(SECTIONS):
            turn = offs[k, pair]
            shifts.append((turn, (NP - turn) % NP))

        for rho in range(2):
            for t in range(3):
                wrap(recv, rho, t)

        fields = [
            [[(recv, (rho, t)) for t in range(3)] for rho in range(2)],
            [[(xa, (rho, t)) for t in range(3)] for rho in range(2)],
            [[(xb, (rho, t)) for t in range(2)] for rho in range(2)],
            [[(xc, (rho,))] for rho in range(2)],
        ]
        for k in range(SECTIONS):
            strips = []
            for rho in range(2):
                ref, index = fields[k][rho][0]
                strips.append(ref[(*index, slice(PAD, PAD + NP))])
            strips = jnp.concatenate(strips, 1)
            high, low = split(strips)
            sums = jnp.dot(basis[...], high, preferred_element_type=jnp.float32)
            coef = sums[0:16] + sums[16:32]
            coef = coef + jnp.dot(basis[0:16], low, preferred_element_type=jnp.float32)
            high, low = split(coef)
            coefs = jnp.concatenate([high, high, low, jnp.zeros((80, 256), jnp.bfloat16)], 0)
            recon = jnp.dot(basis_t[...], coefs, preferred_element_type=jnp.float32)
            half = 0.5 * (strips + recon)
            for rho in range(2):
                hb[k, rho, 0:NP] = half[:, 128 * rho : 128 * rho + 128]
                hb[k, rho, NP : NP + WRAP] = half[0:WRAP, 128 * rho : 128 * rho + 128]
            if k == SECTIONS - 1:
                break
            factor = section_alphas[k] * time_step
            for rho in range(2):
                scale = jnp.where(cell_f < alive_to[rho], factor, 0.0)

                def update(i, c):
                    at = pl.multiple_of(i * CHUNK, CHUNK)

                    def take(t, move=0):
                        ref, index = fields[k][rho][t]
                        return ref[(*index, pl.ds(PAD + at + move, CHUNK))]

                    inner = [take(t) for t in range(3 - k)]
                    vis = [vb[rho, t, pl.ds(at, CHUNK)] for t in range(3 - k)] if k else None
                    start = (at + shifts[k][rho]) % NP
                    ghost = hb[k, 1 - rho, pl.ds(start, CHUNK)]
                    for t in range(3 - k):
                        here = inner[t]
                        up_axial = ghost if t == 0 else inner[t - 1]
                        if t + 1 < 3 - k:
                            down_axial = inner[t + 1]
                        elif k == 0:
                            two = recv[rho, 1, pl.ds(PAD + at, CHUNK)]
                            three = recv[rho, 2, pl.ds(PAD + at, CHUNK)]
                            down_axial = jnp.where(
                                slot < 3, pltpu.roll(two, 48, 1), pltpu.roll(three, 96, 1)
                            )
                        else:
                            down_axial = take(t + 1)
                        up_pitch, down_pitch = take(t, 1), take(t, -1)
                        high, low = split(here)
                        first = k == 0 and t == 0
                        linear = jnp.dot(
                            jnp.concatenate([high, low], 1),
                            mix[rho, 0:256] if first else mix[rho, 0:256, 0:256],
                            preferred_element_type=jnp.float32,
                        )
                        if first:
                            vis = [linear[:, 256 + 128 * q : 384 + 128 * q] for q in range(3)]
                            for q in range(2):
                                vb[rho, q, pl.ds(at, CHUNK)] = vis[q]
                        low = jnp.dot(high, mix[rho, 256:384, 0:128], preferred_element_type=jnp.float32)
                        beside = up_axial + down_axial + up_pitch + down_pitch + linear[:, 128:256]
                        rate = speed_axial * up_axial + speed_pitch * down_pitch + low
                        rate = rate + linear[:, 0:128] + vis[t] * beside
                        ref, index = fields[k + 1][rho][t]
                        ref[(*index, pl.ds(PAD + at, CHUNK))] = (
                            recv[rho, t, pl.ds(PAD + at, CHUNK)] + scale * rate
                        )
                    return c

                lax.fori_loop(0, NP // CHUNK, update, 0)
                for t in range(3 - k):
                    ref, index = fields[k + 1][rho][t]
                    wrap(ref, *index)

        inside = jnp.logical_and(lane % 16 >= 4, lane % 16 < 12)
        for rho in range(2):

            def pack_back(i, c):
                at = pl.multiple_of(i * CHUNK, CHUNK)
                part = []
                for k in range(SECTIONS):
                    back = 4 if k < 3 else 0
                    start = (at + NP - back + shifts[k][rho]) % NP
                    part.append(hb[k, 1 - rho, pl.ds(start, CHUNK)])
                both = jnp.where(inside, part[0], pltpu.roll(part[1], 8, 1))
                third = jnp.where(inside, pltpu.roll(part[2], 80, 1), pltpu.roll(part[2], 40, 1))
                both = jnp.where(lane < 84, both, third)
                blocks = both.reshape(BLOCKS, PITCH, 128)
                st[rho, :, 0] = blocks
                st[rho, 0 : BLOCKS - 1, 1] = blocks[1:]
                st[rho, BLOCKS - 1, 1] = blocks[0]
                st[rho, :, 2] = part[3].reshape(BLOCKS, PITCH, 128)
                return c

            lax.fori_loop(0, NP // CHUNK, pack_back, 0)

        def send_back(other, at):
            pltpu.make_async_remote_copy(
                src_ref=st.at[other % 2, at],
                dst_ref=gbuf.at[own],
                send_sem=ret_s,
                recv_sem=ret_r,
                device_id=(other, at),
                device_id_type=MESH,
            ).start()

        def send_both(i, c):
            send_back(row ^ 1, i)
            send_back(row, i + jnp.where(i >= blk, 1, 0))
            return c

        lax.fori_loop(0, BLOCKS - 1, send_both, 0, unroll=3)
        send_back(row ^ 1, BLOCKS - 1)
        gbuf[own] = st[parity, blk]

    halo_copy(0).wait_recv()
    halo_copy(1).wait_recv()

    def widen_block(j, c):
        for h in range(2):
            a = 2 * j + h
            part = slice(4 * h, 4 * h + 4)
            for v in range(NVAR):
                fld[0, v, a, 0:4] = hr[0, v, j, part]
                fld[0, v, a, 4:12] = state[v, a]
                fld[0, v, a, 12:16] = hr[1, v, j, part]
            vext[a, 0:4] = hr[0, NVAR, j, part]
            vext[a, 4:12] = visc[a]
            vext[a, 12:16] = hr[1, NVAR, j, part]
        return c

    lax.fori_loop(0, AXIAL // 2, widen_block, 0)

    lane2 = lax.broadcasted_iota(jnp.int32, (16, 128), 1)
    first2, last2 = lane2 == 0, lane2 == SPAN - 1
    alive = lane2 < live[0]
    cs = [[coup[v, 0, w] for w in range(NVAR)] for v in range(NVAR)]

    def layer(k, a, up):
        here = [fld[k, v, a] for v in range(NVAR)]
        vis = vext[a]
        below = jnp.maximum(a - 1, 0)
        scale = jnp.where(alive, section_alphas[k] * time_step, 0.0)
        for v in range(NVAR):
            u = here[v]
            up_axial, down_axial = up(v), fld[k, v, below]
            up_pitch, down_pitch = pltpu.roll(u, 15, 0), pltpu.roll(u, 1, 0)
            up_span = jnp.where(last2, u, pltpu.roll(u, 127, 1))
            down_span = jnp.where(first2, u, pltpu.roll(u, 1, 1))
            rate = (
                speed_axial * (up_axial - u)
                - speed_pitch * (u - down_pitch)
                - speed_span * (u - down_span)
            )
            beside = up_axial + down_axial + up_pitch + down_pitch + up_span + down_span
            rate = rate + vis * (beside - 6.0 * u)
            for w in range(NVAR):
                rate = rate + cs[v][w] * here[w]
            new = fld[0, v, a] + scale * rate
            if k < SECTIONS - 1:
                fld[k + 1, v, a] = new
            else:
                out[v, a] = pltpu.roll(new, 12, 0)[0:8]

    for k in range(SECTIONS):

        def inner_layer(a, c):
            layer(k, a, lambda v: fld[k, v, a + 1])
            return c

        lax.fori_loop(0, AXIAL - 1 - k, inner_layer, 0)

    @pl.when(is_worker)
    def _():
        wait_bytes(gbuf.at[pl.ds(0, SLICES - 1)], ret_r)

    @pl.when(jnp.logical_not(is_worker))
    def _():
        wait_bytes(gbuf, ret_r)

    group8 = lane8 // 8
    for v in range(NVAR):
        places = [16 * v + 4, 16 * v + 12]
        places.append(84 + 16 * v if v < 3 else 92 + 16 * (v - 3))
        for k in range(3):
            for half in range(2):
                value = jnp.zeros((8, 128), jnp.float32)
                for s in range(SLICES):
                    turn = (8 * s - places[k]) % 128
                    value = jnp.where(group8 == s, pltpu.roll(gbuf[s, half], turn, 1), value)
                gx[k, v, 8 * half : 8 * half + 8] = value
        value = jnp.zeros((8, 128), jnp.float32)
        for s in range(SLICES):
            turn = (8 * s - (16 * v + 4)) % 128
            value = jnp.where(group8 == s, pltpu.roll(gbuf[s, 2], turn, 1), value)
        gx[3, v, 0:4] = jnp.zeros((4, 128), jnp.float32)
        gx[3, v, 4:12] = value
        gx[3, v, 12:16] = jnp.zeros((4, 128), jnp.float32)

    for k in range(SECTIONS):
        for a in range(AXIAL - 1 - k, AXIAL - 1):
            layer(k, a, lambda v: fld[k, v, a + 1])
        layer(k, AXIAL - 1, lambda v: gx[k, v])

    halo_copy(0).wait_send()
    halo_copy(1).wait_send()

    @pl.when(is_worker)
    def _():
        wait_bytes(many, ret_s)


def solution(mesh):
    weighted, plain = basis_tables()

    def body(state, visc, coup, offs, live):
        vmem = pl.BlockSpec(memory_space=pltpu.VMEM)
        hbm = pl.BlockSpec(memory_space=pltpu.HBM)
        f32 = jnp.float32
        done = pl.pallas_call(
            kernel,
            out_shape=jax.ShapeDtypeStruct((NVAR, AXIAL, PITCH, SPAN), f32),
            in_specs=[hbm] * 7,
            out_specs=vmem,
            scratch_shapes=[
                pltpu.VMEM((NVAR, AXIAL, PITCH, SPAN), f32),
                pltpu.VMEM((AXIAL, PITCH, SPAN), f32),
                pltpu.VMEM((32, NP), jnp.bfloat16),
                pltpu.VMEM((NP, 128), jnp.bfloat16),
                pltpu.VMEM((2, 384, 640), jnp.bfloat16),
                pltpu.VMEM((2 * BLOCKS, 3, 8, 128), f32),
                pltpu.SMEM((NVAR, 1, NVAR), f32),
                pltpu.SMEM((4, 8), jnp.int32),
                pltpu.SMEM((1,), jnp.int32),
                pltpu.SemaphoreType.DMA((7,)),
                pltpu.VMEM((SLICES, 3, 8, 128), f32),
                pltpu.VMEM((2, 3, NP + 2 * PAD, 128), f32),
                pltpu.VMEM((2, NVAR + 1, AXIAL // 2, 8, 128), f32),
                pltpu.VMEM((2, NVAR + 1, AXIAL // 2, 8, 128), f32),
                pltpu.VMEM((2, 2, NP, 128), f32),
                pltpu.VMEM((2, 3, NP + 2 * PAD, 128), f32),
                pltpu.VMEM((2, 2, NP + 2 * PAD, 128), f32),
                pltpu.VMEM((2, NP + 2 * PAD, 128), f32),
                pltpu.VMEM((SECTIONS, 2, NP + WRAP, 128), f32),
                pltpu.VMEM((2, BLOCKS, 3, 8, 128), f32),
                pltpu.VMEM((SLICES, 3, 8, 128), f32),
                pltpu.VMEM((SECTIONS, NVAR, AXIAL, 16, 128), f32),
                pltpu.VMEM((AXIAL, 16, 128), f32),
                pltpu.VMEM((SECTIONS, NVAR, 16, 128), f32),
                pltpu.SemaphoreType.DMA,
                pltpu.SemaphoreType.DMA,
                pltpu.SemaphoreType.REGULAR,
                pltpu.SemaphoreType.DMA((2,)),
                pltpu.SemaphoreType.DMA((2,)),
                pltpu.SemaphoreType.DMA,
                pltpu.SemaphoreType.DMA,
            ],
            compiler_params=pltpu.CompilerParams(
                collective_id=0, has_side_effects=True, vmem_limit_bytes=63 << 20
            ),
            name="sections",
        )(state[0], visc[0], jnp.transpose(coup, (1, 0, 2)), offs, live, jnp.asarray(weighted), jnp.asarray(plain))
        return done[None]

    in_specs = (
        P("row", None, None, "blk", None),
        P("row", None, "blk", None),
        P("row", None, None),
        P(),
        P("row"),
    )
    out_specs = P("row", None, None, "blk", None)
    return jax.shard_map(body, mesh=mesh, in_specs=in_specs, out_specs=out_specs, check_vma=False)
```

```python
import functools
import math

import jax
import jax.numpy as jnp
import numpy as np
from jax import lax
from jax.experimental import pallas as pl
from jax.experimental.pallas import tpu as pltpu
from jax.sharding import PartitionSpec as P

MESH = pl.DeviceIdType.MESH
MODES = 5
SECTIONS = 4
NVAR = 5
AXIAL = 16
PITCH = 8
SPAN = 128
BLOCKS = 64
NP = BLOCKS * PITCH
SLICES = 16
CHUNK = 512
WRAP = 512
PAD = 8

section_alphas = (0.25, 1.0 / 3.0, 0.5, 1.0)
time_step = 0.25
speed_axial = 1.0
speed_pitch = 0.6
speed_span = 0.3

def split(value):
    high = value.astype(jnp.bfloat16)
    return high, (value - high.astype(jnp.float32)).astype(jnp.bfloat16)


def basis_tables():
    theta = np.arange(NP) * (2.0 * math.pi / NP)
    rows = [np.ones(NP)]
    rows += [np.cos(j * theta) for j in range(1, MODES + 1)]
    rows += [np.sin(j * theta) for j in range(1, MODES + 1)]
    table = np.zeros((16, NP), np.float32)
    table[: 2 * MODES + 1] = np.stack(rows)
    weights = np.full((16, 1), 2.0 / NP, np.float32)
    weights[0] = 1.0 / NP

    def parts(value):
        high = value.astype(jnp.bfloat16)
        return high, (value - high.astype(np.float32)).astype(jnp.bfloat16)

    back = np.zeros((NP, 128), jnp.bfloat16)
    high, low = parts(np.ascontiguousarray(table.T))
    back[:, 0:16], back[:, 16:32], back[:, 32:48] = high, low, high
    return np.concatenate(parts(table * weights)), back


def worker_of(pair, s):
    plane = 2 * (s // 2) + pair % 2
    return 2 * pair + (s // 2) % 2, 4 * plane + 2 * (s % 2) + 1


def kernel(
    state_hbm, visc_hbm, coup_hbm, offs_hbm, live_hbm, basis_hbm, basis_t_hbm, out,
    state, visc, basis, basis_t, mix, size, coup, offs, live, load_s,
    msg, recv, hs, hr, vb, xa, xb, xc, hb, st, gbuf, fld, vext, gx,
    main_s, main_r, ready, halo_s, halo_r, ret_s, ret_r,
):
    row = lax.axis_index("row")
    blk = lax.axis_index("blk")
    pair, parity = row // 2, row % 2
    z = blk // 4
    own = 2 * (z // 2) + (blk // 2) % 2
    own_row, own_blk = worker_of(pair, own)
    is_worker = jnp.logical_and(own_row == row, own_blk == blk)
    after, before = (blk + 1) % BLOCKS, (blk + BLOCKS - 1) % BLOCKS

    many = size.at[pl.ds(0, 2 * BLOCKS - 1)]

    bar = pltpu.get_barrier_semaphore()

    def greet(r, b):
        pl.semaphore_signal(bar, inc=1, device_id=(r, b), device_id_type=MESH)

    @pl.when(is_worker)
    def _():
        def greet_source(i, c):
            at = (blk + BLOCKS // 2 + jnp.where(i % 2 == 1, (i + 1) // 2, BLOCKS - i // 2)) % BLOCKS
            greet(row ^ 1, at)

            @pl.when(at != blk)
            def _():
                greet(row, at)

            return c

        lax.fori_loop(0, BLOCKS, greet_source, 0)

    greet(row, after)

    loads = [
        pltpu.make_async_copy(source, target, load_s.at[i])
        for i, (source, target) in enumerate(
            [
                (state_hbm, state), (visc_hbm, visc), (basis_hbm, basis), (basis_t_hbm, basis_t),
                (coup_hbm, coup), (offs_hbm, offs), (live_hbm, live),
            ]
        )
    ]
    for load in loads:
        load.start()

    for load in loads:
        load.wait()

    lane8 = lax.broadcasted_iota(jnp.int32, (8, 128), 1)
    slot8 = lane8 // 16
    top = AXIAL - 1
    tiles = (
        [(v, top) for v in range(NVAR)] + [(-1, top), (-1, top - 1), (-1, top - 2)],
        [(v, top - 1) for v in range(NVAR)] + [(0, top - 3), (1, top - 3), (2, top - 3)],
        [(v, top - 2) for v in range(NVAR)] + [(3, top - 3), (4, top - 3)],
    )
    sub8 = lax.broadcasted_iota(jnp.int32, (8, 128), 0)
    consts = jnp.where(lane8 == 112 + NVAR, live[0].astype(jnp.float32), 0.0)
    for v in range(NVAR):
        for w in range(NVAR):
            here = jnp.logical_and(lane8 == 112 + v, sub8 == (w - v) % 8)
            consts = jnp.where(here, coup[v, 0, w], consts)
    for t, slots in enumerate(tiles):
        values = [visc[a] if v < 0 else state[v, a] for v, a in slots]
        for s in range(SLICES):
            packed = consts if t == 2 else jnp.zeros((8, 128), jnp.float32)
            for q, value in enumerate(values):
                turn = (16 * q - (8 * s - 4)) % 128
                moved = pltpu.roll(value, turn, 1) if turn else value
                packed = jnp.where(slot8 == q, moved, packed)
            msg[s, t] = packed

    def pack_halo(j, c):
        for v in range(NVAR + 1):
            for h in range(2):
                if v < NVAR:
                    low = state[v, 2 * j + h, 0:4]
                    high = state[v, 2 * j + h, 4:8]
                else:
                    low = visc[2 * j + h, 0:4]
                    high = visc[2 * j + h, 4:8]
                hs[0, v, j, 4 * h : 4 * h + 4] = high
                hs[1, v, j, 4 * h : 4 * h + 4] = low
        return c

    lax.fori_loop(0, AXIAL // 2, pack_halo, 0)

    pl.semaphore_wait(bar, SLICES + 1 - jnp.where(is_worker, 1, 0))
    pl.semaphore_signal(ready, inc=1, device_id=(row, before), device_id_type=MESH)

    mine = pl.ds(pl.multiple_of(PAD + PITCH * blk, 8), PITCH)

    def send_main(i, c):
        s = (z + SLICES // 2 + jnp.where(i % 2 == 1, (i + 1) // 2, SLICES - i // 2)) % SLICES
        wr, wb = worker_of(pair, s)
        self = jnp.logical_and(wr == row, wb == blk)

        @pl.when(jnp.logical_not(self))
        def _():
            pltpu.make_async_remote_copy(
                src_ref=msg.at[s],
                dst_ref=recv.at[parity, :, mine],
                send_sem=main_s,
                recv_sem=main_r,
                device_id=(wr, wb),
                device_id_type=MESH,
            ).start()

        return c

    lax.fori_loop(0, SLICES, send_main, 0)

    def wait_bytes(ref, sem):
        pltpu.make_async_copy(ref, ref, sem).wait()

    @pl.when(is_worker)
    def _():
        wait_bytes(msg.at[pl.ds(0, SLICES - 1)], main_s)

    @pl.when(jnp.logical_not(is_worker))
    def _():
        wait_bytes(msg, main_s)

    def halo_copy(side):
        return pltpu.make_async_remote_copy(
            src_ref=hs.at[side],
            dst_ref=hr.at[side],
            send_sem=halo_s.at[side],
            recv_sem=halo_r.at[side],
            device_id=(row, after if side == 0 else before),
            device_id_type=MESH,
        )

    halo_copy(1).start()
    pl.semaphore_wait(ready, 1)
    halo_copy(0).start()

    @pl.when(is_worker)
    def _():
        recv[parity, :, mine] = msg[own]
        source = lax.broadcasted_iota(jnp.int32, (128, 128), 0)
        target = lax.broadcasted_iota(jnp.int32, (128, 128), 1)
        place = 8 * own - 4 + target % 16
        lower = jnp.where(place == 0, target, target - 1)
        upper = jnp.where(place == SPAN - 1, target, target + 1)

        def one(here):
            return jnp.where(here, 1.0, 0.0)

        around = one(source == lower) + one(source == upper) - 6.0 * one(source == target)
        still = speed_span * one(source == lower) - (
            speed_axial + speed_pitch + speed_span
        ) * one(source == target)
        for rho in range(2):
            for half in range(2):
                mix[rho, 128 * half : 128 * half + 128, 128:256] = around.astype(jnp.bfloat16)
                for q in range(3):
                    wide = one(source == 16 * (5 + q) + target % 16).astype(jnp.bfloat16)
                    mix[rho, 128 * half : 128 * half + 128, 256 + 128 * q : 384 + 128 * q] = wide
        wait_bytes(many, main_r)
        alive_to = []
        for rho in range(2):
            given = recv[rho, 2, PAD : PAD + 8]
            table = jnp.zeros((8, 128), jnp.float32)
            for v in range(NVAR):
                column = jnp.broadcast_to(given[:, 112 + v : 113 + v], (8, 128))
                table = jnp.where(slot8 == v, column, table)
            alive_to.append(given[0:1, 112 + NVAR : 113 + NVAR])
            both = still
            for d in range(8):
                both = both + jnp.where(source == (target + 16 * d) % 128, table[d : d + 1], 0.0)
            high, low = split(both)
            for half in range(2):
                mix[rho, 128 * half : 128 * half + 128, 0:128] = high
            mix[rho, 256:384, 0:128] = low
        lane = lax.broadcasted_iota(jnp.int32, (CHUNK, 128), 1)
        slot = lane // 16
        cell = 8 * own - 4 + lane % 16
        cell_f = cell[0:1].astype(jnp.float32)

        def wrap(ref, *index):
            ref[(*index, slice(PAD - 1, PAD))] = ref[(*index, slice(PAD + NP - 1, PAD + NP))]
            ref[(*index, slice(PAD + NP, PAD + NP + 1))] = ref[(*index, slice(PAD, PAD + 1))]

        shifts = []
        for k in range(SECTIONS):
            turn = offs[k, pair]
            shifts.append((turn, (NP - turn) % NP))

        for rho in range(2):
            for t in range(3):
                wrap(recv, rho, t)

        fields = [
            [[(recv, (rho, t)) for t in range(3)] for rho in range(2)],
            [[(xa, (rho, t)) for t in range(3)] for rho in range(2)],
            [[(xb, (rho, t)) for t in range(2)] for rho in range(2)],
            [[(xc, (rho,))] for rho in range(2)],
        ]
        for k in range(SECTIONS):
            strips = []
            for rho in range(2):
                ref, index = fields[k][rho][0]
                strips.append(ref[(*index, slice(PAD, PAD + NP))])
            strips = jnp.concatenate(strips, 1)
            high, low = split(strips)
            sums = jnp.dot(basis[...], high, preferred_element_type=jnp.float32)
            coef = sums[0:16] + sums[16:32]
            coef = coef + jnp.dot(basis[0:16], low, preferred_element_type=jnp.float32)
            high, low = split(coef)
            coefs = jnp.concatenate([high, high, low, jnp.zeros((80, 256), jnp.bfloat16)], 0)
            recon = jnp.dot(basis_t[...], coefs, preferred_element_type=jnp.float32)
            half = 0.5 * (strips + recon)
            for rho in range(2):
                hb[k, rho, 0:NP] = half[:, 128 * rho : 128 * rho + 128]
                hb[k, rho, NP : NP + WRAP] = half[0:WRAP, 128 * rho : 128 * rho + 128]
            if k == SECTIONS - 1:
                break
            factor = section_alphas[k] * time_step
            for rho in range(2):
                scale = jnp.where(cell_f < alive_to[rho], factor, 0.0)

                def update(i, c):
                    at = pl.multiple_of(i * CHUNK, CHUNK)

                    def take(t, move=0):
                        ref, index = fields[k][rho][t]
                        return ref[(*index, pl.ds(PAD + at + move, CHUNK))]

                    inner = [take(t) for t in range(3 - k)]
                    vis = [vb[rho, t, pl.ds(at, CHUNK)] for t in range(3 - k)] if k else None
                    start = (at + shifts[k][rho]) % NP
                    ghost = hb[k, 1 - rho, pl.ds(start, CHUNK)]
                    for t in range(3 - k):
                        here = inner[t]
                        up_axial = ghost if t == 0 else inner[t - 1]
                        if t + 1 < 3 - k:
                            down_axial = inner[t + 1]
                        elif k == 0:
                            two = recv[rho, 1, pl.ds(PAD + at, CHUNK)]
                            three = recv[rho, 2, pl.ds(PAD + at, CHUNK)]
                            down_axial = jnp.where(
                                slot < 3, pltpu.roll(two, 48, 1), pltpu.roll(three, 96, 1)
                            )
                        else:
                            down_axial = take(t + 1)
                        up_pitch, down_pitch = take(t, 1), take(t, -1)
                        high, low = split(here)
                        first = k == 0 and t == 0
                        linear = jnp.dot(
                            jnp.concatenate([high, low], 1),
                            mix[rho, 0:256] if first else mix[rho, 0:256, 0:256],
                            preferred_element_type=jnp.float32,
                        )
                        if first:
                            vis = [linear[:, 256 + 128 * q : 384 + 128 * q] for q in range(3)]
                            for q in range(2):
                                vb[rho, q, pl.ds(at, CHUNK)] = vis[q]
                        low = jnp.dot(high, mix[rho, 256:384, 0:128], preferred_element_type=jnp.float32)
                        beside = up_axial + down_axial + up_pitch + down_pitch + linear[:, 128:256]
                        rate = speed_axial * up_axial + speed_pitch * down_pitch + low
                        rate = rate + linear[:, 0:128] + vis[t] * beside
                        ref, index = fields[k + 1][rho][t]
                        ref[(*index, pl.ds(PAD + at, CHUNK))] = (
                            recv[rho, t, pl.ds(PAD + at, CHUNK)] + scale * rate
                        )
                    return c

                lax.fori_loop(0, NP // CHUNK, update, 0)
                for t in range(3 - k):
                    ref, index = fields[k + 1][rho][t]
                    wrap(ref, *index)

        inside = jnp.logical_and(lane % 16 >= 4, lane % 16 < 12)
        for rho in range(2):

            def pack_back(i, c):
                at = pl.multiple_of(i * CHUNK, CHUNK)
                part = []
                for k in range(SECTIONS):
                    back = 4 if k < 3 else 0
                    start = (at + NP - back + shifts[k][rho]) % NP
                    part.append(hb[k, 1 - rho, pl.ds(start, CHUNK)])
                both = jnp.where(inside, part[0], pltpu.roll(part[1], 8, 1))
                third = jnp.where(inside, pltpu.roll(part[2], 80, 1), pltpu.roll(part[2], 40, 1))
                both = jnp.where(lane < 84, both, third)
                blocks = both.reshape(BLOCKS, PITCH, 128)
                st[rho, :, 0] = blocks
                st[rho, 0 : BLOCKS - 1, 1] = blocks[1:]
                st[rho, BLOCKS - 1, 1] = blocks[0]
                st[rho, :, 2] = part[3].reshape(BLOCKS, PITCH, 128)
                return c

            lax.fori_loop(0, NP // CHUNK, pack_back, 0)

        def send_back(other, at):
            pltpu.make_async_remote_copy(
                src_ref=st.at[other % 2, at],
                dst_ref=gbuf.at[own],
                send_sem=ret_s,
                recv_sem=ret_r,
                device_id=(other, at),
                device_id_type=MESH,
            ).start()

        def send_both(i, c):
            send_back(row ^ 1, i)
            send_back(row, i + jnp.where(i >= blk, 1, 0))
            return c

        lax.fori_loop(0, BLOCKS - 1, send_both, 0, unroll=3)
        send_back(row ^ 1, BLOCKS - 1)
        gbuf[own] = st[parity, blk]

    halo_copy(0).wait_recv()
    halo_copy(1).wait_recv()

    def widen_block(j, c):
        for h in range(2):
            a = 2 * j + h
            part = slice(4 * h, 4 * h + 4)
            for v in range(NVAR):
                fld[0, v, a, 0:4] = hr[0, v, j, part]
                fld[0, v, a, 4:12] = state[v, a]
                fld[0, v, a, 12:16] = hr[1, v, j, part]
            vext[a, 0:4] = hr[0, NVAR, j, part]
            vext[a, 4:12] = visc[a]
            vext[a, 12:16] = hr[1, NVAR, j, part]
        return c

    lax.fori_loop(0, AXIAL // 2, widen_block, 0)

    lane2 = lax.broadcasted_iota(jnp.int32, (16, 128), 1)
    first2, last2 = lane2 == 0, lane2 == SPAN - 1
    alive = lane2 < live[0]
    cs = [[coup[v, 0, w] for w in range(NVAR)] for v in range(NVAR)]

    def layer(k, a, up):
        here = [fld[k, v, a] for v in range(NVAR)]
        vis = vext[a]
        below = jnp.maximum(a - 1, 0)
        scale = jnp.where(alive, section_alphas[k] * time_step, 0.0)
        for v in range(NVAR):
            u = here[v]
            up_axial, down_axial = up(v), fld[k, v, below]
            up_pitch, down_pitch = pltpu.roll(u, 15, 0), pltpu.roll(u, 1, 0)
            up_span = jnp.where(last2, u, pltpu.roll(u, 127, 1))
            down_span = jnp.where(first2, u, pltpu.roll(u, 1, 1))
            rate = (
                speed_axial * (up_axial - u)
                - speed_pitch * (u - down_pitch)
                - speed_span * (u - down_span)
            )
            beside = up_axial + down_axial + up_pitch + down_pitch + up_span + down_span
            rate = rate + vis * (beside - 6.0 * u)
            for w in range(NVAR):
                rate = rate + cs[v][w] * here[w]
            new = fld[0, v, a] + scale * rate
            if k < SECTIONS - 1:
                fld[k + 1, v, a] = new
            else:
                out[v, a] = pltpu.roll(new, 12, 0)[0:8]

    for k in range(SECTIONS):

        def inner_layer(a, c):
            layer(k, a, lambda v: fld[k, v, a + 1])
            return c

        lax.fori_loop(0, AXIAL - 1 - k, inner_layer, 0, unroll=True)

    @pl.when(is_worker)
    def _():
        wait_bytes(gbuf.at[pl.ds(0, SLICES - 1)], ret_r)

    @pl.when(jnp.logical_not(is_worker))
    def _():
        wait_bytes(gbuf, ret_r)

    group8 = lane8 // 8
    for v in range(NVAR):
        places = [16 * v + 4, 16 * v + 12]
        places.append(84 + 16 * v if v < 3 else 92 + 16 * (v - 3))
        for k in range(3):
            for half in range(2):
                value = jnp.zeros((8, 128), jnp.float32)
                for s in range(SLICES):
                    turn = (8 * s - places[k]) % 128
                    value = jnp.where(group8 == s, pltpu.roll(gbuf[s, half], turn, 1), value)
                gx[k, v, 8 * half : 8 * half + 8] = value
        value = jnp.zeros((8, 128), jnp.float32)
        for s in range(SLICES):
            turn = (8 * s - (16 * v + 4)) % 128
            value = jnp.where(group8 == s, pltpu.roll(gbuf[s, 2], turn, 1), value)
        gx[3, v, 0:4] = jnp.zeros((4, 128), jnp.float32)
        gx[3, v, 4:12] = value
        gx[3, v, 12:16] = jnp.zeros((4, 128), jnp.float32)

    for k in range(SECTIONS):
        for a in range(AXIAL - 1 - k, AXIAL - 1):
            layer(k, a, lambda v: fld[k, v, a + 1])
        layer(k, AXIAL - 1, lambda v: gx[k, v])

    halo_copy(0).wait_send()
    halo_copy(1).wait_send()

    @pl.when(is_worker)
    def _():
        wait_bytes(many, ret_s)


def solution(mesh):
    weighted, plain = basis_tables()

    def body(state, visc, coup, offs, live):
        vmem = pl.BlockSpec(memory_space=pltpu.VMEM)
        hbm = pl.BlockSpec(memory_space=pltpu.HBM)
        f32 = jnp.float32
        done = pl.pallas_call(
            kernel,
            out_shape=jax.ShapeDtypeStruct((NVAR, AXIAL, PITCH, SPAN), f32),
            in_specs=[hbm] * 7,
            out_specs=vmem,
            scratch_shapes=[
                pltpu.VMEM((NVAR, AXIAL, PITCH, SPAN), f32),
                pltpu.VMEM((AXIAL, PITCH, SPAN), f32),
                pltpu.VMEM((32, NP), jnp.bfloat16),
                pltpu.VMEM((NP, 128), jnp.bfloat16),
                pltpu.VMEM((2, 384, 640), jnp.bfloat16),
                pltpu.VMEM((2 * BLOCKS, 3, 8, 128), f32),
                pltpu.SMEM((NVAR, 1, NVAR), f32),
                pltpu.SMEM((4, 8), jnp.int32),
                pltpu.SMEM((1,), jnp.int32),
                pltpu.SemaphoreType.DMA((7,)),
                pltpu.VMEM((SLICES, 3, 8, 128), f32),
                pltpu.VMEM((2, 3, NP + 2 * PAD, 128), f32),
                pltpu.VMEM((2, NVAR + 1, AXIAL // 2, 8, 128), f32),
                pltpu.VMEM((2, NVAR + 1, AXIAL // 2, 8, 128), f32),
                pltpu.VMEM((2, 2, NP, 128), f32),
                pltpu.VMEM((2, 3, NP + 2 * PAD, 128), f32),
                pltpu.VMEM((2, 2, NP + 2 * PAD, 128), f32),
                pltpu.VMEM((2, NP + 2 * PAD, 128), f32),
                pltpu.VMEM((SECTIONS, 2, NP + WRAP, 128), f32),
                pltpu.VMEM((2, BLOCKS, 3, 8, 128), f32),
                pltpu.VMEM((SLICES, 3, 8, 128), f32),
                pltpu.VMEM((SECTIONS, NVAR, AXIAL, 16, 128), f32),
                pltpu.VMEM((AXIAL, 16, 128), f32),
                pltpu.VMEM((SECTIONS, NVAR, 16, 128), f32),
                pltpu.SemaphoreType.DMA,
                pltpu.SemaphoreType.DMA,
                pltpu.SemaphoreType.REGULAR,
                pltpu.SemaphoreType.DMA((2,)),
                pltpu.SemaphoreType.DMA((2,)),
                pltpu.SemaphoreType.DMA,
                pltpu.SemaphoreType.DMA,
            ],
            compiler_params=pltpu.CompilerParams(
                collective_id=0, has_side_effects=True, vmem_limit_bytes=63 << 20
            ),
            name="sections",
        )(state[0], visc[0], jnp.transpose(coup, (1, 0, 2)), offs, live, jnp.asarray(weighted), jnp.asarray(plain))
        return done[None]

    in_specs = (
        P("row", None, None, "blk", None),
        P("row", None, "blk", None),
        P("row", None, None),
        P(),
        P("row"),
    )
    out_specs = P("row", None, None, "blk", None)
    return jax.shard_map(body, mesh=mesh, in_specs=in_specs, out_specs=out_specs, check_vma=False)
```
